32 devices in a mesh: sensor: 8 (over z, y), step: 4 (over x, core).
Axes of the slice: x: 2, y: 2, z: 4, core: 2. Of those that a mesh axis runs over, the one named last changes fastest.
Arguments:
- inputs: bfloat16 [12, 512, 512], P('step', 'sensor'), may hold values from -6 to 6
- cotangent: bfloat16 [12, 512, 512], P('step', 'sensor'), may hold values from -6 to 6
- w_query: bfloat16 [512, 512], replicated, may hold values from -0.25 to 0.25
- w_key: bfloat16 [512, 512], replicated, may hold values from -0.25 to 0.25
- w_value: bfloat16 [512, 512], replicated, may hold values from -0.25 to 0.25
- w_up: bfloat16 [512, 256], replicated, may hold values from -0.25 to 0.25
- w_down: bfloat16 [256, 512], replicated, may hold values from -0.375 to 0.375
- feature_proj: float32 [8, 64, 64], replicated, may hold values from -5 to 5
- live_count: int32 [8], P('sensor'), may hold values from 32 to 64, as said below
Outputs:
- grad_inputs: bfloat16 [12, 512, 512], P('step', 'sensor')
- grad_query: float32 [512, 512], P('sensor', 'step')
- grad_key: float32 [512, 512], P('sensor', 'step')
- grad_value: float32 [512, 512], P('sensor', 'step')
The draws below stay inside these ranges and needn't reach their ends.
Inputs may be any that keep to these rules, and one draw needn't show every extreme that they name: `live_count`: some group has all 64 sensors live; every group has at least half of them live.
All inputs are finite; a program needn't handle non-finite values.
Results may differ from the reference program's by a relative error of at most 0.012.
Values sent between devices are 32-bit elements; how exact they have to be, the bound alone decides.
No kernel may reach another device: no remote copies, remote signals or barrier semaphores. Data moves between devices by JAX's collectives and lax.ppermute only.
A program may use at most 64 MiB of HBM per device.

```python
import math
import jax
import jax.numpy as jnp
from jax import lax

H = 8
E = 64
D = 512
R = 64
F = 256
SENS_DEV = 64
STEPS = 12
SENSORS = 512
N_SENSOR = 8


def draw_live_count(key, part):
    counts = jax.random.randint(jax.random.fold_in(key, 11), (N_SENSOR,), SENS_DEV // 2, SENS_DEV + 1)
    chosen = jax.random.randint(jax.random.fold_in(key, 12), (), 0, N_SENSOR)
    return jnp.where(jnp.arange(N_SENSOR) == chosen, SENS_DEV, counts).astype(jnp.int32)


def block_scale(key, dims, pieces, least, largest):
    def one(dim, blocks):
        draws = jax.random.uniform(jax.random.fold_in(jax.random.fold_in(key, 6), dim), (blocks,), jnp.float32, least / len(pieces), largest / len(pieces))
        return jnp.repeat(jnp.exp(draws), dims[dim] // blocks).reshape((-1,) + (1,) * (len(dims) - dim - 1))

    factor_of = one(*pieces[0])
    for cut in pieces[1:]:
        factor_of = factor_of * one(*cut)
    return factor_of


def noise(rng, shape, deviation, most, shards=(), kind=jnp.bfloat16):
    values = jax.random.normal(rng, shape, jnp.float32) * deviation
    if len(shards) > 0:
        values = block_scale(rng, shape, shards, -0.22, 0.18) * values
    return jnp.clip(values, min=-most, max=most).astype(kind)


def setup_inputs(seed: int = 0) -> dict:
    streams_of = jax.random.split(jax.random.key(seed), 10)
    inputs = noise(streams_of[0], (STEPS, SENSORS, D), 1.0, 6.0, ((0, 4), (1, 8)))
    cotangent = noise(streams_of[1], (STEPS, SENSORS, D), 1.0, 6.0, ((0, 4), (1, 8)))
    w_query = noise(streams_of[2], (D, D), D ** -0.5, 0.25)
    w_key = noise(streams_of[3], (D, D), D ** -0.5, 0.25)
    w_value = noise(streams_of[4], (D, D), D ** -0.5, 0.25)
    w_up = noise(streams_of[5], (D, F), D ** -0.5, 0.25)
    w_down = noise(streams_of[6], (F, D), F ** -0.5, 0.375)
    feature_proj = noise(streams_of[7], (H, E, R), 1.0, 5.0, (), jnp.float32)
    live_count = draw_live_count(jax.random.fold_in(streams_of[9], 71), 0)
    return dict(inputs=inputs, cotangent=cotangent, w_query=w_query, w_key=w_key, w_value=w_value, w_up=w_up, w_down=w_down, feature_proj=feature_proj, live_count=live_count)


HIGH = lax.Precision.HIGHEST

def feature_map(scaled, feature_proj):
    projected = jnp.einsum('...he,her->...hr', scaled, feature_proj, precision=HIGH)
    return jnp.exp(projected - 0.5 * lax.optimization_barrier(jnp.sum(scaled * scaled, -1, keepdims=True))) * feature_proj.shape[2] ** (-0.5)

def feature_back(incoming, feat, scaled, feature_proj):
    weighted = incoming * feat
    return jnp.einsum('...hr,her->...he', weighted, feature_proj, precision=HIGH) - scaled * lax.optimization_barrier(jnp.sum(weighted, -1, keepdims=True))

def step_grads(inputs, cotangent, valid, w_query, w_key, w_value, w_up, w_down, feature_proj):
    sensors, width = inputs.shape
    heads, head_dim, feats = feature_proj.shape
    factor = head_dim ** (-0.25)

    def project(weight):
        return jnp.dot(inputs, weight, preferred_element_type=jnp.float32).reshape(sensors, heads, head_dim)
    scaled_query = project(w_query) * factor
    scaled_key = project(w_key) * factor
    values = project(w_value)
    feat_query = feature_map(scaled_query, feature_proj)
    feat_key = feature_map(scaled_key, feature_proj)
    masked_key = feat_key * valid[:, None, None]
    summary = jnp.einsum('nhr,nhe->hre', masked_key, values, precision=HIGH)
    normal_sum = lax.optimization_barrier(jnp.sum(masked_key, 0))
    numer = jnp.einsum('nhr,hre->nhe', feat_query, summary, precision=HIGH)
    denom = jnp.einsum('nhr,hr->nh', feat_query, normal_sum, precision=HIGH)
    attended = numer / denom[..., None]
    flat_att = attended.reshape(sensors, width)
    rms_val = jnp.sqrt(lax.optimization_barrier(jnp.mean(flat_att * flat_att, -1, keepdims=True)) + 1e-06)
    normed = flat_att / rms_val
    pre_act = jnp.dot(normed.astype(jnp.bfloat16), w_up, preferred_element_type=jnp.float32)
    masked_cot = cotangent * valid.astype(jnp.bfloat16)[:, None]
    grad_hidden = jnp.dot(masked_cot, w_down.T, preferred_element_type=jnp.float32)
    _, gelu_back = jax.vjp(jax.nn.gelu, pre_act)
    grad_pre = gelu_back(grad_hidden)[0].astype(jnp.bfloat16)
    grad_normed = jnp.dot(grad_pre, w_up.T, preferred_element_type=jnp.float32)
    grad_att = (grad_normed - normed * lax.optimization_barrier(jnp.mean(grad_normed * normed, -1, keepdims=True))) / rms_val
    grad_att = grad_att.reshape(sensors, heads, head_dim)
    grad_num = grad_att / denom[..., None]
    grad_den = -lax.optimization_barrier(jnp.sum(grad_att * attended, -1)) / denom
    grad_fq = jnp.einsum('nhe,hre->nhr', grad_num, summary, precision=HIGH) + grad_den[..., None] * normal_sum[None]
    grad_summary = jnp.einsum('nhr,nhe->hre', feat_query, grad_num, precision=HIGH)
    grad_normal = jnp.einsum('nhr,nh->hr', feat_query, grad_den, precision=HIGH)
    grad_fk = (jnp.einsum('nhe,hre->nhr', values, grad_summary, precision=HIGH) + grad_normal[None]) * valid[:, None, None]
    grad_val = jnp.einsum('nhr,hre->nhe', masked_key, grad_summary, precision=HIGH)
    grad_q = feature_back(grad_fq, feat_query, scaled_query, feature_proj) * factor
    grad_k = feature_back(grad_fk, feat_key, scaled_key, feature_proj) * factor
    grad_q = grad_q.reshape(sensors, width).astype(jnp.bfloat16)
    grad_k = grad_k.reshape(sensors, width).astype(jnp.bfloat16)
    grad_val = grad_val.reshape(sensors, width).astype(jnp.bfloat16)
    grad_in = jnp.dot(grad_q, w_query.T, preferred_element_type=jnp.float32)
    grad_in = grad_in + jnp.dot(grad_k, w_key.T, preferred_element_type=jnp.float32)
    grad_in = grad_in + jnp.dot(grad_val, w_value.T, preferred_element_type=jnp.float32)
    weight_q = jnp.dot(inputs.T, grad_q, preferred_element_type=jnp.float32)
    weight_k = jnp.dot(inputs.T, grad_k, preferred_element_type=jnp.float32)
    weight_v = jnp.dot(inputs.T, grad_val, preferred_element_type=jnp.float32)
    return (grad_in.astype(jnp.bfloat16), (weight_q, weight_k, weight_v))

def reference(inputs, cotangent, w_query, w_key, w_value, w_up, w_down, feature_proj, live_count):
    sensors = inputs.shape[1]
    width = inputs.shape[2]
    position = jnp.arange(sensors, dtype=jnp.int32)
    valid = (position % SENS_DEV < live_count[position // SENS_DEV]).astype(jnp.float32)
    zeros = jnp.zeros((width, width), jnp.float32)

    def advance(carry, pair):
        grad_in, grads = step_grads(pair[0], pair[1], valid, w_query, w_key, w_value, w_up, w_down, feature_proj)
        return ((carry[0] + grads[0], carry[1] + grads[1], carry[2] + grads[2]), grad_in)
    totals, grad_inputs = lax.scan(advance, (zeros, zeros, zeros), (inputs, cotangent))
    norm_scale = 1.0 / math.sqrt(inputs.shape[0] * sensors)
    return (grad_inputs, totals[0] * norm_scale, totals[1] * norm_scale, totals[2] * norm_scale)
```

```python
import functools
import math

import jax
import jax.numpy as jnp
from jax import lax
from jax.experimental import pallas as pl
from jax.experimental.pallas import tpu as pltpu
from jax.sharding import PartitionSpec as P

F32 = jnp.float32
BF16 = jnp.bfloat16
NN = (((1,), (0,)), ((), ()))
NT = (((1,), (1,)), ((), ()))
TN = (((0,), (0,)), ((), ()))
VMEM = pl.BlockSpec(memory_space=pltpu.VMEM)
SMEM = pl.BlockSpec(memory_space=pltpu.SMEM)
LANES = 128
WIDE = 256


def dot(a, b, dims=NN):
    return lax.dot_general(a, b, dims, preferred_element_type=F32)


def split(x):
    high = x.astype(BF16)
    return high, (x - high.astype(F32)).astype(BF16)


def dot3(a, b, dims=NN):
    return dot(a[0], b[0], dims) + (dot(a[0], b[1], dims) + dot(a[1], b[0], dims))


def head_mask(size):
    rows = lax.broadcasted_iota(jnp.int32, (WIDE, WIDE), 0) // size
    cols = lax.broadcasted_iota(jnp.int32, (WIDE, WIDE), 1) // size
    return rows == cols


def spread(x, mask):
    return jnp.where(mask, jnp.concatenate([x] * (WIDE // x.shape[0]), 0), 0.0)


def gather_diagonal(x, size):
    head = lax.broadcasted_iota(jnp.int32, (size, WIDE), 1) // size
    out = x[:size]
    for g in range(1, WIDE // size):
        out = jnp.where(head == g, x[g * size : (g + 1) * size], out)
    return out


def head_sums(x, ones):
    high, low = split(x)
    return dot(high, ones) + dot(low, ones)


def halves(x):
    return [x[:, h : h + WIDE] for h in range(0, x.shape[1], WIDE)]


def projection(proj_ref):
    heads = proj_ref.shape[0]
    per = WIDE // proj_ref.shape[1]
    return [
        jnp.concatenate([proj_ref[g + h] for h in range(per)], -1) for g in range(0, heads, per)
    ]


def feature_map(scaled, proj, mask, ones, size):
    out = []
    for u, p in zip(halves(scaled), proj):
        projected = dot3(split(u), split(spread(p, mask)))
        out.append(jnp.exp(projected - 0.5 * head_sums(u * u, ones)) * size ** (-0.5))
    return jnp.concatenate(out, -1)


def feature_back(weighted, scaled, proj, mask, ones):
    out = []
    for w, u, p in zip(halves(weighted), halves(scaled), proj):
        high, low = split(w)
        back = dot3((high, low), split(spread(p, mask)), NT)
        out.append(back - u * (dot(high, ones) + dot(low, ones)))
    return jnp.concatenate(out, -1)


def store_summary(out_ref, step, matrices, sums):
    chunks = out_ref.shape[0]
    groups = sums.shape[1] // LANES
    per_half = WIDE // LANES
    for group in range(groups):
        part = matrices[group // per_half][:, (group % per_half) * LANES :][:, :LANES]
        row = (step * groups + group) * 8
        for chunk in range(chunks):
            out_ref[chunk, row : row + 8, :] = part[chunk * 8 : chunk * 8 + 8]
        slot = step * groups + group
        base = out_ref.shape[1] - 8
        out_ref[slot // 8, base + slot % 8 : base + slot % 8 + 1, :] = sums[
            :, group * LANES : (group + 1) * LANES
        ]


def load_summary(in_ref, step, groups):
    chunks = in_ref.shape[0]
    columns, sums = [], []
    for group in range(groups):
        slot = step * groups + group
        row = slot * 8
        columns.append(
            jnp.concatenate([in_ref[c, row : row + 8, :] for c in range(chunks)], 0)
        )
        base = in_ref.shape[1] - 8
        sums.append(in_ref[slot // 8, base + slot % 8 : base + slot % 8 + 1, :])
    whole = jnp.concatenate(columns, -1)
    return halves(whole), jnp.concatenate(sums, -1)


def outer_sums(a, b, size):
    out = []
    for x, y in zip(halves(a), halves(b)):
        xh, xl = split(x)
        yh, yl = split(y)
        whole = dot(
            jnp.concatenate([xh, xh, xl], 0), jnp.concatenate([yh, yl, yh], 0), TN
        )
        out.append(gather_diagonal(whole, size))
    return out


def key_kernel(steps, factor, live_ref, x_ref, wk_ref, wv_ref, proj_ref, u_ref, v_ref, f_ref, s_ref, x32_ref):
    size = proj_ref.shape[1]
    x = x_ref[...]
    x32_ref[...] = x.astype(F32)
    rows = x.shape[0] // steps
    mask = head_mask(size)
    ones = jnp.where(mask, 1.0, 0.0).astype(BF16)
    scaled = dot(x, wk_ref[...]) * factor
    values = dot(x, wv_ref[...])
    u_ref[...] = scaled
    v_ref[...] = values
    feat = feature_map(scaled, projection(proj_ref), mask, ones, proj_ref.shape[2])
    place = lax.broadcasted_iota(jnp.int32, feat.shape, 0) % rows
    feat = jnp.where(place < live_ref[0], feat, 0.0)
    f_ref[...] = feat
    base = s_ref.shape[1] - 8
    for chunk in range(s_ref.shape[0]):
        s_ref[chunk, base:, :] = jnp.zeros((8, LANES), F32)
    for step in range(steps):
        part = slice(step * rows, (step + 1) * rows)
        store_summary(
            s_ref,
            step,
            outer_sums(feat[part], values[part], size),
            jnp.sum(feat[part], 0, keepdims=True),
        )


def query_kernel(steps, factor, live_ref, x_ref, cot_ref, wq_ref, wd_ref, proj_ref, u_ref, f_ref, gh_ref):
    size = proj_ref.shape[1]
    mask = head_mask(size)
    ones = jnp.where(mask, 1.0, 0.0).astype(BF16)
    scaled = dot(x_ref[...], wq_ref[...]) * factor
    u_ref[...] = scaled
    f_ref[...] = feature_map(scaled, projection(proj_ref), mask, ones, proj_ref.shape[2])
    rows = x_ref.shape[0] // steps
    hidden = dot(cot_ref[...], wd_ref[...], NT)
    place = lax.broadcasted_iota(jnp.int32, hidden.shape, 0) % rows
    gh_ref[...] = jnp.where(place < live_ref[0], hidden, 0.0)


def sum_kernel(in_ref, out_ref):
    total = in_ref[0]
    for chunk in range(1, in_ref.shape[0]):
        total = total + in_ref[chunk]
    for chunk in range(out_ref.shape[0]):
        out_ref[chunk] = total


def middle_kernel(steps, size, s_ref, f_ref, gh_ref, wu_ref, num_ref, den_ref, g_ref):
    mask = head_mask(size)
    ones = jnp.where(mask, 1.0, 0.0).astype(BF16)
    feat = f_ref[...]
    width = feat.shape[1]
    rows = feat.shape[0] // steps
    groups = width // LANES
    numer, weighted = [], []
    for step in range(steps):
        matrices, sums = load_summary(s_ref, step, groups)
        part = feat[step * rows : (step + 1) * rows]
        numer.append(
            jnp.concatenate(
                [dot3(split(f), split(spread(m, mask))) for f, m in zip(halves(part), matrices)],
                -1,
            )
        )
        weighted.append(part * sums)
    numer = jnp.concatenate(numer, 0)
    weighted = jnp.concatenate(weighted, 0)
    denom = jnp.concatenate([head_sums(w, ones) for w in halves(weighted)], -1)
    inverse = 1.0 / denom
    attended = numer * inverse
    scale = lax.rsqrt(jnp.mean(attended * attended, -1, keepdims=True) + 1e-06)
    normed = attended * scale
    wu = wu_ref[...]
    pre = dot(normed.astype(BF16), wu)
    c = math.sqrt(2.0 / math.pi)
    square = pre * pre
    t = jnp.tanh(c * pre * (1.0 + 0.044715 * square))
    slope = 0.5 * (1.0 + t) + 0.5 * pre * (1.0 - t * t) * (c * (1.0 + 3 * 0.044715 * square))
    grad_pre = (gh_ref[...] * slope).astype(BF16)
    grad_normed = dot(grad_pre, wu, NT)
    grad_att = (grad_normed - normed * jnp.mean(grad_normed * normed, -1, keepdims=True)) * scale
    grad_num = grad_att * inverse
    along = grad_att * attended
    grad_den = -jnp.concatenate([head_sums(a, ones) for a in halves(along)], -1) * inverse
    num_ref[...] = grad_num
    den_ref[...] = grad_den
    base = g_ref.shape[1] - 8
    for chunk in range(g_ref.shape[0]):
        g_ref[chunk, base:, :] = jnp.zeros((8, LANES), F32)
    for step in range(steps):
        part = slice(step * rows, (step + 1) * rows)
        store_summary(
            g_ref,
            step,
            outer_sums(feat[part], grad_num[part], size),
            jnp.sum(feat[part] * grad_den[part], 0, keepdims=True),
        )


def send_columns(grads, send_refs, own_ref, me, size):
    count = len(send_refs) + 1
    for shift, ref in enumerate([own_ref] + list(send_refs)):
        target = lax.rem(me + shift, count)
        for place, g in enumerate(grads):
            ref[:, place * size : (place + 1) * size] = g[:, pl.ds(pl.multiple_of(target * size, size), size)]


def query_back_kernel(steps, factor, axis, cols, s_ref, num_ref, den_ref, f_ref, u_ref, proj_ref, g_ref, own_ref, *rest):
    send_refs, scratch = rest[:-1], rest[-1]
    size = proj_ref.shape[1]
    mask = head_mask(size)
    ones = jnp.where(mask, 1.0, 0.0).astype(BF16)
    feat = f_ref[...]
    rows = feat.shape[0] // steps
    groups = feat.shape[1] // LANES
    out = []
    for step in range(steps):
        matrices, sums = load_summary(s_ref, step, groups)
        part = slice(step * rows, (step + 1) * rows)
        back = jnp.concatenate(
            [
                dot3(split(n), split(spread(m, mask)), NT)
                for n, m in zip(halves(num_ref[part, :]), matrices)
            ],
            -1,
        )
        out.append(back + den_ref[part, :] * sums)
    weighted = jnp.concatenate(out, 0) * feat
    grad = (feature_back(weighted, u_ref[...], projection(proj_ref), mask, ones) * factor).astype(BF16)
    g_ref[...] = grad
    scratch[...] = grad.astype(F32)
    send_columns([scratch], send_refs, own_ref, lax.axis_index(axis), cols)


def key_back_kernel(steps, factor, axis, cols, g_ref, v_ref, f_ref, u_ref, proj_ref, gk_ref, gv_ref, own_ref, *rest):
    send_refs, scratch_k, scratch_v = rest[:-2], rest[-2], rest[-1]
    size = proj_ref.shape[1]
    mask = head_mask(size)
    ones = jnp.where(mask, 1.0, 0.0).astype(BF16)
    feat = f_ref[...]
    rows = feat.shape[0] // steps
    groups = feat.shape[1] // LANES
    back, grad_v = [], []
    for step in range(steps):
        matrices, sums = load_summary(g_ref, step, groups)
        spreads = [split(spread(m, mask)) for m in matrices]
        part = slice(step * rows, (step + 1) * rows)
        back.append(
            jnp.concatenate(
                [dot3(split(v), m, NT) for v, m in zip(halves(v_ref[part, :]), spreads)], -1
            )
            + sums
        )
        grad_v.append(
            jnp.concatenate([dot3(split(f), m) for f, m in zip(halves(feat[part]), spreads)], -1)
        )
    weighted = jnp.concatenate(back, 0) * feat
    grad_k = (feature_back(weighted, u_ref[...], projection(proj_ref), mask, ones) * factor).astype(BF16)
    grad_v = jnp.concatenate(grad_v, 0).astype(BF16)
    gk_ref[...] = grad_k
    gv_ref[...] = grad_v
    scratch_k[...] = grad_k.astype(F32)
    scratch_v[...] = grad_v.astype(F32)
    send_columns([scratch_k, scratch_v], send_refs, own_ref, lax.axis_index(axis), cols)


def rows_kernel(gq_ref, gk_ref, gv_ref, wq_ref, wk_ref, wv_ref, out_ref):
    total = dot(gq_ref[...], wq_ref[...], NT)
    total = total + dot(gk_ref[...], wk_ref[...], NT)
    out_ref[...] = (total + dot(gv_ref[...], wv_ref[...], NT)).astype(BF16)


def outer_kernel(count, *refs):
    xs, gq, gkv, out_ref = refs[:count], refs[count : 2 * count], refs[2 * count : 3 * count], refs[-1]
    x = jnp.concatenate([r[...].astype(BF16) for r in xs], 0)
    q = jnp.concatenate([r[...].astype(BF16) for r in gq], 0)
    kv = jnp.concatenate([r[...].astype(BF16) for r in gkv], 0)
    total = dot(x, jnp.concatenate([q, kv], -1), TN)
    chunks, rows = out_ref.shape[:2]
    for chunk in range(chunks):
        out_ref[chunk] = total[chunk * rows : (chunk + 1) * rows]


def final_kernel(scale, in_ref, *outs):
    total = in_ref[0]
    for chunk in range(1, in_ref.shape[0]):
        total = total + in_ref[chunk]
    cols = outs[0].shape[1]
    for place, ref in enumerate(outs):
        ref[...] = total[:, place * cols : (place + 1) * cols] * scale


def call(kernel, name, outs, args, flops=0, smem=0, scratch=()):
    size = lambda a: math.prod(a.shape) * a.dtype.itemsize
    return pl.pallas_call(
        kernel,
        name=name,
        out_shape=outs,
        in_specs=[SMEM] * smem + [VMEM] * (len(args) - smem),
        out_specs=jax.tree.map(lambda _: VMEM, outs),
        scratch_shapes=list(scratch),
        cost_estimate=pl.CostEstimate(
            flops=flops,
            bytes_accessed=sum(size(a) for a in list(args) + list(jax.tree.leaves(outs))),
            transcendentals=0,
        ),
        compiler_params=pltpu.CompilerParams(vmem_limit_bytes=40 * 1024 * 1024),
    )(*args)


def shape(dims, kind=F32):
    return jax.ShapeDtypeStruct(dims, kind)


def reduce_summary(chunks):
    n = lax.axis_size("sensor")
    if n != chunks.shape[0]:
        return lax.psum(chunks, "sensor")
    parts = lax.all_to_all(chunks, "sensor", 0, 0, tiled=True)
    total = call(sum_kernel, "sum_chunks", shape(chunks.shape), (parts,))
    return lax.all_to_all(total, "sensor", 0, 0, tiled=True)


def shift_all(arrays, count):
    return [
        lax.ppermute(a, "step", [(i, (i + shift) % count) for i in range(count)])
        for shift, a in enumerate(arrays, 1)
    ]


def shards(inputs, cotangent, w_query, w_key, w_value, w_up, w_down, feature_proj, live_count):
    steps, sensors, width = inputs.shape
    heads, size, feats = feature_proj.shape
    hidden = w_up.shape[1]
    factor = size ** (-0.25)
    rows = steps * sensors
    count = lax.axis_size("step")
    devices = lax.axis_size("sensor")
    cols = width // count
    x = inputs.reshape(rows, width)
    cot = cotangent.reshape(rows, width)
    whole = shape((rows, width))
    half = shape((rows, width), BF16)
    packed = shape((feats // 8, (steps * width // LANES) * 8 + 8, LANES))
    product = 2 * rows * width * width

    key, value, feat_key, local, x32 = call(
        functools.partial(key_kernel, steps, factor),
        "keys",
        (whole, whole, whole, packed, whole),
        (live_count, x, w_key, w_value, feature_proj),
        flops=3 * product,
        smem=1,
    )
    summary = reduce_summary(local)
    query, feat_query, grad_hidden = call(
        functools.partial(query_kernel, steps, factor),
        "queries",
        (whole, whole, shape((rows, hidden))),
        (live_count, x, cot, w_query, w_down, feature_proj),
        flops=3 * product,
        smem=1,
    )
    xs = [x] + shift_all([x32] * (count - 1), count)
    grad_num, grad_den, local_grad = call(
        functools.partial(middle_kernel, steps, size),
        "middle",
        (whole, whole, packed),
        (summary, feat_query, grad_hidden, w_up),
        flops=4 * product,
    )
    grad_summary = reduce_summary(local_grad)
    grad_q, own_q, *send_q = call(
        functools.partial(query_back_kernel, steps, factor, "step", cols),
        "query_back",
        (half,) + (shape((rows, cols)),) * count,
        (summary, grad_num, grad_den, feat_query, query, feature_proj),
        flops=3 * product,
        scratch=[pltpu.VMEM((rows, width), F32)],
    )
    got_q = [own_q] + shift_all(send_q, count)
    grad_k, grad_v, own_kv, *send_kv = call(
        functools.partial(key_back_kernel, steps, factor, "step", cols),
        "key_back",
        (half, half) + (shape((rows, 2 * cols)),) * count,
        (grad_summary, value, feat_key, key, feature_proj),
        flops=4 * product,
        scratch=[pltpu.VMEM((rows, width), F32)] * 2,
    )
    got_kv = [own_kv] + shift_all(send_kv, count)
    grad_in = call(
        rows_kernel,
        "input_rows",
        half,
        (grad_q, grad_k, grad_v, w_query, w_key, w_value),
        flops=3 * product,
    )
    partial = call(
        functools.partial(outer_kernel, count),
        "weight_partials",
        shape((devices, width // devices, 3 * cols)),
        (*xs, *got_q, *got_kv),
        flops=3 * product,
    )
    parts = lax.all_to_all(partial, "sensor", 0, 0, tiled=True)
    scale = 1.0 / math.sqrt(rows * count * devices)
    out = shape((width // devices, cols))
    grads = call(functools.partial(final_kernel, scale), "weight_sums", (out, out, out), (parts,))
    return (grad_in.reshape(inputs.shape), *grads)


def solution(mesh):
    return jax.shard_map(
        shards,
        mesh=mesh,
        in_specs=(P("step", "sensor", None),) * 2 + (P(),) * 6 + (P("sensor"),),
        out_specs=(P("step", "sensor", None),) + (P("sensor", "step"),) * 3,
        check_vma=False,
    )
```

```python
import functools
import math

import jax
import jax.numpy as jnp
from jax import lax
from jax.experimental import pallas as pl
from jax.experimental.pallas import tpu as pltpu
from jax.sharding import PartitionSpec as P

F32 = jnp.float32
BF16 = jnp.bfloat16
NN = (((1,), (0,)), ((), ()))
NT = (((1,), (1,)), ((), ()))
TN = (((0,), (0,)), ((), ()))
VMEM = pl.BlockSpec(memory_space=pltpu.VMEM)
SMEM = pl.BlockSpec(memory_space=pltpu.SMEM)
LANES = 128
WIDE = 256


def dot(a, b, dims=NN):
    return lax.dot_general(a, b, dims, preferred_element_type=F32)


def split(x):
    high = x.astype(BF16)
    return high, (x - high.astype(F32)).astype(BF16)


def dot3(a, b, dims=NN):
    return dot(a[0], b[0], dims) + (dot(a[0], b[1], dims) + dot(a[1], b[0], dims))


def head_mask(size):
    rows = lax.broadcasted_iota(jnp.int32, (WIDE, WIDE), 0) // size
    cols = lax.broadcasted_iota(jnp.int32, (WIDE, WIDE), 1) // size
    return rows == cols


def spread(x, mask):
    return jnp.where(mask, jnp.concatenate([x] * (WIDE // x.shape[0]), 0), 0.0)


def gather_diagonal(x, size):
    head = lax.broadcasted_iota(jnp.int32, (size, WIDE), 1) // size
    out = x[:size]
    for g in range(1, WIDE // size):
        out = jnp.where(head == g, x[g * size : (g + 1) * size], out)
    return out


def head_sums(x, ones):
    high, low = split(x)
    return dot(high, ones) + dot(low, ones)


def halves(x):
    return [x[:, h : h + WIDE] for h in range(0, x.shape[1], WIDE)]


def projection(proj_ref):
    heads = proj_ref.shape[0]
    per = WIDE // proj_ref.shape[1]
    return [
        jnp.concatenate([proj_ref[g + h] for h in range(per)], -1) for g in range(0, heads, per)
    ]


def feature_map(scaled, proj, mask, ones, size):
    out = []
    for u, p in zip(halves(scaled), proj):
        projected = dot3(split(u), split(spread(p, mask)))
        out.append(jnp.exp(projected - 0.5 * head_sums(u * u, ones)) * size ** (-0.5))
    return jnp.concatenate(out, -1)


def feature_back(weighted, scaled, proj, mask, ones):
    out = []
    for w, u, p in zip(halves(weighted), halves(scaled), proj):
        high, low = split(w)
        back = dot3((high, low), split(spread(p, mask)), NT)
        out.append(back - u * (dot(high, ones) + dot(low, ones)))
    return jnp.concatenate(out, -1)


def store_summary(out_ref, step, steps, matrices, sums):
    quarters = out_ref.shape[0]
    high = matrices[0].shape[0] // quarters
    groups = sums.shape[1] // LANES
    per_half = WIDE // LANES
    for group in range(groups):
        part = matrices[group // per_half][:, (group % per_half) * LANES :][:, :LANES]
        row = (step * groups + group) * high
        for quarter in range(quarters):
            out_ref[quarter, row : row + high, :] = part[quarter * high : (quarter + 1) * high]
        slot = step * groups + group
        place = steps * groups * high + slot // quarters
        out_ref[slot % quarters, place : place + 1, :] = sums[:, group * LANES : (group + 1) * LANES]


def clear_tail(out_ref):
    tail = out_ref.shape[1] - 8
    for quarter in range(out_ref.shape[0]):
        out_ref[quarter, tail:, :] = jnp.zeros((8, LANES), F32)


def load_summary(in_ref, step, steps, groups, high):
    quarters = in_ref.shape[0]
    columns, sums = [], []
    for group in range(groups):
        slot = step * groups + group
        row = slot * high
        columns.append(
            jnp.concatenate([in_ref[q, row : row + high, :] for q in range(quarters)], 0)
        )
        place = steps * groups * high + slot // quarters
        sums.append(in_ref[slot % quarters, place : place + 1, :])
    return halves(jnp.concatenate(columns, -1)), jnp.concatenate(sums, -1)


def deal(scratch, refs, me):
    for partner, ref in enumerate(refs):
        ref[...] = scratch[(me ^ partner) % len(refs)]


def collect(scratch, refs, me):
    for partner, ref in enumerate(refs):
        scratch[(me ^ partner) % len(refs)] = ref[...]


def outer_sums(a, b, size):
    out = []
    for x, y in zip(halves(a), halves(b)):
        xh, xl = split(x)
        yh, yl = split(y)
        whole = dot(
            jnp.concatenate([xh, xh, xl], 0), jnp.concatenate([yh, yl, yh], 0), TN
        )
        out.append(gather_diagonal(whole, size))
    return out


def key_kernel(steps, factor, live_ref, x_ref, wk_ref, wv_ref, proj_ref, u_ref, v_ref, f_ref, x32_ref, *rest):
    out_refs, s_ref = rest[:-1], rest[-1]
    size = proj_ref.shape[1]
    x = x_ref[...]
    x32_ref[...] = x.astype(F32)
    rows = x.shape[0] // steps
    mask = head_mask(size)
    ones = jnp.where(mask, 1.0, 0.0).astype(BF16)
    scaled = dot(x, wk_ref[...]) * factor
    values = dot(x, wv_ref[...])
    u_ref[...] = scaled
    v_ref[...] = values
    feat = feature_map(scaled, projection(proj_ref), mask, ones, proj_ref.shape[2])
    place = lax.broadcasted_iota(jnp.int32, feat.shape, 0) % rows
    feat = jnp.where(place < live_ref[0], feat, 0.0)
    f_ref[...] = feat
    clear_tail(s_ref)
    for step in range(steps):
        part = slice(step * rows, (step + 1) * rows)
        store_summary(
            s_ref,
            step,
            steps,
            outer_sums(feat[part], values[part], size),
            jnp.sum(feat[part], 0, keepdims=True),
        )
    deal(s_ref, out_refs, lax.axis_index("sensor"))


def query_kernel(steps, factor, live_ref, x_ref, cot_ref, wq_ref, wd_ref, proj_ref, u_ref, f_ref, gh_ref):
    size = proj_ref.shape[1]
    mask = head_mask(size)
    ones = jnp.where(mask, 1.0, 0.0).astype(BF16)
    scaled = dot(x_ref[...], wq_ref[...]) * factor
    u_ref[...] = scaled
    f_ref[...] = feature_map(scaled, projection(proj_ref), mask, ones, proj_ref.shape[2])
    rows = x_ref.shape[0] // steps
    hidden = dot(cot_ref[...], wd_ref[...], NT)
    place = lax.broadcasted_iota(jnp.int32, hidden.shape, 0) % rows
    gh_ref[...] = jnp.where(place < live_ref[0], hidden, 0.0)


def middle_kernel(steps, size, *refs):
    in_refs, (f_ref, gh_ref, wu_ref, num_ref, den_ref) = refs[:4], refs[4:9]
    out_refs, s_ref, g_ref = refs[9:13], refs[13], refs[14]
    me = lax.axis_index("sensor")
    collect(s_ref, in_refs, me)
    mask = head_mask(size)
    ones = jnp.where(mask, 1.0, 0.0).astype(BF16)
    feat = f_ref[...]
    width = feat.shape[1]
    rows = feat.shape[0] // steps
    groups = width // LANES
    numer, weighted = [], []
    for step in range(steps):
        matrices, sums = load_summary(s_ref, step, steps, groups, size // 4)
        part = feat[step * rows : (step + 1) * rows]
        numer.append(
            jnp.concatenate(
                [dot3(split(f), split(spread(m, mask))) for f, m in zip(halves(part), matrices)],
                -1,
            )
        )
        weighted.append(part * sums)
    numer = jnp.concatenate(numer, 0)
    weighted = jnp.concatenate(weighted, 0)
    denom = jnp.concatenate([head_sums(w, ones) for w in halves(weighted)], -1)
    inverse = 1.0 / denom
    attended = numer * inverse
    scale = lax.rsqrt(jnp.mean(attended * attended, -1, keepdims=True) + 1e-06)
    normed = attended * scale
    wu = wu_ref[...]
    pre = dot(normed.astype(BF16), wu)
    c = math.sqrt(2.0 / math.pi)
    square = pre * pre
    t = jnp.tanh(c * pre * (1.0 + 0.044715 * square))
    slope = 0.5 * (1.0 + t) + 0.5 * pre * (1.0 - t * t) * (c * (1.0 + 3 * 0.044715 * square))
    grad_pre = (gh_ref[...] * slope).astype(BF16)
    grad_normed = dot(grad_pre, wu, NT)
    grad_att = (grad_normed - normed * jnp.mean(grad_normed * normed, -1, keepdims=True)) * scale
    grad_num = grad_att * inverse
    along = grad_att * attended
    grad_den = -jnp.concatenate([head_sums(a, ones) for a in halves(along)], -1) * inverse
    num_ref[...] = grad_num
    den_ref[...] = grad_den
    clear_tail(g_ref)
    for step in range(steps):
        part = slice(step * rows, (step + 1) * rows)
        store_summary(
            g_ref,
            step,
            steps,
            outer_sums(feat[part], grad_num[part], size),
            jnp.sum(feat[part] * grad_den[part], 0, keepdims=True),
        )
    deal(g_ref, out_refs, me)


def send_columns(grads, send_refs, own_ref, me, size):
    count = len(send_refs) + 1
    for shift, ref in enumerate([own_ref] + list(send_refs)):
        target = lax.rem(me + shift, count)
        for place, g in enumerate(grads):
            ref[:, place * size : (place + 1) * size] = g[:, pl.ds(pl.multiple_of(target * size, size), size)]


def query_back_kernel(steps, factor, axis, cols, s0, s1, s2, s3, num_ref, den_ref, f_ref, u_ref, proj_ref, g_ref, own_ref, *rest):
    send_refs, scratch, s_ref = rest[:-2], rest[-2], rest[-1]
    collect(s_ref, (s0, s1, s2, s3), lax.axis_index("sensor"))
    size = proj_ref.shape[1]
    mask = head_mask(size)
    ones = jnp.where(mask, 1.0, 0.0).astype(BF16)
    feat = f_ref[...]
    rows = feat.shape[0] // steps
    groups = feat.shape[1] // LANES
    out = []
    for step in range(steps):
        matrices, sums = load_summary(s_ref, step, steps, groups, size // 4)
        part = slice(step * rows, (step + 1) * rows)
        back = jnp.concatenate(
            [
                dot3(split(n), split(spread(m, mask)), NT)
                for n, m in zip(halves(num_ref[part, :]), matrices)
            ],
            -1,
        )
        out.append(back + den_ref[part, :] * sums)
    weighted = jnp.concatenate(out, 0) * feat
    grad = (feature_back(weighted, u_ref[...], projection(proj_ref), mask, ones) * factor).astype(BF16)
    g_ref[...] = grad
    scratch[...] = grad.astype(F32)
    send_columns([scratch], send_refs, own_ref, lax.axis_index(axis), cols)


def key_back_kernel(steps, factor, axis, cols, g0, g1, g2, g3, v_ref, f_ref, u_ref, proj_ref, gk_ref, gv_ref, own_ref, *rest):
    send_refs, scratch_k, scratch_v, g_ref = rest[:-3], rest[-3], rest[-2], rest[-1]
    collect(g_ref, (g0, g1, g2, g3), lax.axis_index("sensor"))
    size = proj_ref.shape[1]
    mask = head_mask(size)
    ones = jnp.where(mask, 1.0, 0.0).astype(BF16)
    feat = f_ref[...]
    rows = feat.shape[0] // steps
    groups = feat.shape[1] // LANES
    back, grad_v = [], []
    for step in range(steps):
        matrices, sums = load_summary(g_ref, step, steps, groups, size // 4)
        spreads = [split(spread(m, mask)) for m in matrices]
        part = slice(step * rows, (step + 1) * rows)
        back.append(
            jnp.concatenate(
                [dot3(split(v), m, NT) for v, m in zip(halves(v_ref[part, :]), spreads)], -1
            )
            + sums
        )
        grad_v.append(
            jnp.concatenate([dot3(split(f), m) for f, m in zip(halves(feat[part]), spreads)], -1)
        )
    weighted = jnp.concatenate(back, 0) * feat
    grad_k = (feature_back(weighted, u_ref[...], projection(proj_ref), mask, ones) * factor).astype(BF16)
    grad_v = jnp.concatenate(grad_v, 0).astype(BF16)
    gk_ref[...] = grad_k
    gv_ref[...] = grad_v
    scratch_k[...] = grad_k.astype(F32)
    scratch_v[...] = grad_v.astype(F32)
    send_columns([scratch_k, scratch_v], send_refs, own_ref, lax.axis_index(axis), cols)


def rows_kernel(gq_ref, gk_ref, gv_ref, wq_ref, wk_ref, wv_ref, out_ref):
    total = dot(gq_ref[...], wq_ref[...], NT)
    total = total + dot(gk_ref[...], wk_ref[...], NT)
    out_ref[...] = (total + dot(gv_ref[...], wv_ref[...], NT)).astype(BF16)


def outer_kernel(count, *refs):
    xs, gq, gkv, out_ref = refs[:count], refs[count : 2 * count], refs[2 * count : 3 * count], refs[-1]
    x = jnp.concatenate([r[...].astype(BF16) for r in xs], 0)
    q = jnp.concatenate([r[...].astype(BF16) for r in gq], 0)
    kv = jnp.concatenate([r[...].astype(BF16) for r in gkv], 0)
    total = dot(x, jnp.concatenate([q, kv], -1), TN)
    chunks, rows = out_ref.shape[0], out_ref.shape[-2]
    for chunk in range(total.shape[0] // rows):
        part = total[chunk * rows : (chunk + 1) * rows]
        if len(out_ref.shape) == 4:
            out_ref[chunk % chunks, chunk // chunks] = part
        else:
            out_ref[chunk] = part


def halve_kernel(in_ref, own_ref, away_ref):
    mine = lax.axis_index("sensor") // in_ref.shape[0]
    for ref, block in ((own_ref, mine), (away_ref, 1 - mine)):
        total = in_ref[0, block]
        for part in range(1, in_ref.shape[0]):
            total = total + in_ref[part, block]
        ref[...] = total


def final_kernel(scale, in_ref, *outs):
    total = in_ref[0]
    for chunk in range(1, in_ref.shape[0]):
        total = total + in_ref[chunk]
    cols = outs[0].shape[1]
    for place, ref in enumerate(outs):
        ref[...] = total[:, place * cols : (place + 1) * cols] * scale


def call(kernel, name, outs, args, flops=0, smem=0, scratch=()):
    size = lambda a: math.prod(a.shape) * a.dtype.itemsize
    return pl.pallas_call(
        kernel,
        name=name,
        out_shape=outs,
        in_specs=[SMEM] * smem + [VMEM] * (len(args) - smem),
        out_specs=jax.tree.map(lambda _: VMEM, outs),
        scratch_shapes=list(scratch),
        cost_estimate=pl.CostEstimate(
            flops=flops,
            bytes_accessed=sum(size(a) for a in list(args) + list(jax.tree.leaves(outs))),
            transcendentals=0,
        ),
        compiler_params=pltpu.CompilerParams(vmem_limit_bytes=16 * 1024 * 1024),
    )(*args)


def shape(dims, kind=F32):
    return jax.ShapeDtypeStruct(dims, kind)


def trade(parts, axis):
    count = lax.axis_size(axis)
    return [parts[0]] + [
        lax.ppermute(a, axis, [(i, i ^ d) for i in range(count)]) for d, a in enumerate(parts) if d
    ]


def reduce_summary(parts):
    count = lax.axis_size("sensor")
    total = sum(trade(parts, "sensor"))
    bit = len(parts)
    while bit < count:
        total = total + lax.ppermute(total, "sensor", [(i, i ^ bit) for i in range(count)])
        bit *= 2
    return trade([total] * len(parts), "sensor")


def shift_all(arrays, count):
    return [
        lax.ppermute(a, "step", [(i, (i + shift) % count) for i in range(count)])
        for shift, a in enumerate(arrays, 1)
    ]


def shards(inputs, cotangent, w_query, w_key, w_value, w_up, w_down, feature_proj, live_count):
    steps, sensors, width = inputs.shape
    heads, size, feats = feature_proj.shape
    hidden = w_up.shape[1]
    factor = size ** (-0.25)
    rows = steps * sensors
    count = lax.axis_size("step")
    devices = lax.axis_size("sensor")
    cols = width // count
    x = inputs.reshape(rows, width)
    cot = cotangent.reshape(rows, width)
    whole = shape((rows, width))
    half = shape((rows, width), BF16)
    quarter = (steps * (width // LANES) * (size // 4) + 8, LANES)
    packed = (shape(quarter),) * 4
    held = pltpu.VMEM((4, *quarter), F32)
    product = 2 * rows * width * width

    key, value, feat_key, x32, *local = call(
        functools.partial(key_kernel, steps, factor),
        "keys",
        (whole,) * 4 + packed,
        (live_count, x, w_key, w_value, feature_proj),
        flops=3 * product,
        smem=1,
        scratch=[held],
    )
    summary = reduce_summary(local)
    query, feat_query, grad_hidden = call(
        functools.partial(query_kernel, steps, factor),
        "queries",
        (whole, whole, shape((rows, hidden))),
        (live_count, x, cot, w_query, w_down, feature_proj),
        flops=3 * product,
        smem=1,
    )
    xs = [x] + shift_all([x32] * (count - 1), count)
    grad_num, grad_den, *local_grad = call(
        functools.partial(middle_kernel, steps, size),
        "middle",
        (whole, whole) + packed,
        (*summary, feat_query, grad_hidden, w_up),
        flops=4 * product,
        scratch=[held] * 2,
    )
    grad_summary = reduce_summary(local_grad)
    grad_q, own_q, *send_q = call(
        functools.partial(query_back_kernel, steps, factor, "step", cols),
        "query_back",
        (half,) + (shape((rows, cols)),) * count,
        (*summary, grad_num, grad_den, feat_query, query, feature_proj),
        flops=3 * product,
        scratch=[pltpu.VMEM((rows, width), F32), held],
    )
    got_q = [own_q] + shift_all(send_q, count)
    grad_k, grad_v, own_kv, *send_kv = call(
        functools.partial(key_back_kernel, steps, factor, "step", cols),
        "key_back",
        (half, half) + (shape((rows, 2 * cols)),) * count,
        (*grad_summary, value, feat_key, key, feature_proj),
        flops=4 * product,
        scratch=[pltpu.VMEM((rows, width), F32)] * 2 + [held],
    )
    got_kv = [own_kv] + shift_all(send_kv, count)
    grad_in = call(
        rows_kernel,
        "input_rows",
        half,
        (grad_q, grad_k, grad_v, w_query, w_key, w_value),
        flops=3 * product,
    )
    tile = (width // devices, 3 * cols)
    partial = call(
        functools.partial(outer_kernel, count),
        "weight_partials",
        shape((4, 2, *tile) if devices == 8 else (devices, *tile)),
        (*xs, *got_q, *got_kv),
        flops=3 * product,
    )
    if devices == 8:
        quads = [[0, 1, 2, 3], [4, 5, 6, 7]]
        far = [(i, i ^ 4) for i in range(devices)]
        parts = lax.all_to_all(partial, "sensor", 0, 0, tiled=True, axis_index_groups=quads)
        total, away = call(halve_kernel, "quarter_sums", (shape(tile), shape(tile)), (parts,))
        parts = jnp.stack([total, lax.ppermute(away, "sensor", far)])
    else:
        parts = lax.all_to_all(partial, "sensor", 0, 0, tiled=True)
    scale = 1.0 / math.sqrt(rows * count * devices)
    out = shape((width // devices, cols))
    grads = call(functools.partial(final_kernel, scale), "weight_sums", (out, out, out), (parts,))
    return (grad_in.reshape(inputs.shape), *grads)


def solution(mesh):
    return jax.shard_map(
        shards,
        mesh=mesh,
        in_specs=(P("step", "sensor", None),) * 2 + (P(),) * 6 + (P("sensor"),),
        out_specs=(P("step", "sensor", None),) + (P("sensor", "step"),) * 3,
        check_vma=False,
    )
```

```python
import functools
import math

import jax
import jax.numpy as jnp
from jax import lax
from jax.experimental import pallas as pl
from jax.experimental.pallas import tpu as pltpu
from jax.sharding import PartitionSpec as P

F32 = jnp.float32
BF16 = jnp.bfloat16
NN = (((1,), (0,)), ((), ()))
NT = (((1,), (1,)), ((), ()))
TN = (((0,), (0,)), ((), ()))
VMEM = pl.BlockSpec(memory_space=pltpu.VMEM)
SMEM = pl.BlockSpec(memory_space=pltpu.SMEM)
LANES = 128
WIDE = 256


def dot(a, b, dims=NN):
    return lax.dot_general(a, b, dims, preferred_element_type=F32)


def split(x):
    high = x.astype(BF16)
    return high, (x - high.astype(F32)).astype(BF16)


def dot3(a, b, dims=NN):
    return dot(a[0], b[0], dims) + (dot(a[0], b[1], dims) + dot(a[1], b[0], dims))


def head_mask(size, width):
    rows = lax.broadcasted_iota(jnp.int32, (width, width), 0) // size
    cols = lax.broadcasted_iota(jnp.int32, (width, width), 1) // size
    return rows == cols


def head_ones(mask):
    return jnp.where(mask, 1.0, 0.0).astype(BF16)


def spread(x, mask):
    return jnp.where(mask, jnp.concatenate([x] * (x.shape[1] // x.shape[0]), 0), 0.0)


def gather_diagonal(x, size):
    head = lax.broadcasted_iota(jnp.int32, (size, x.shape[1]), 1) // size
    out = x[:size]
    for g in range(1, x.shape[1] // size):
        out = jnp.where(head == g, x[g * size : (g + 1) * size], out)
    return out


def head_sums(x, ones):
    high, low = split(x)
    return dot(high, ones) + dot(low, ones)


def pieces(x, width=WIDE):
    return [x[:, h : h + width] for h in range(0, x.shape[1], width)]


def projection(proj_ref, heads=None, width=WIDE):
    heads = range(proj_ref.shape[0]) if heads is None else heads
    blocks = [proj_ref[h] for h in heads]
    per = width // proj_ref.shape[2]
    return [jnp.concatenate(blocks[g : g + per], -1) for g in range(0, len(blocks), per)]


def feature_map(scaled, proj, mask, ones, feats):
    out = []
    for u, p in zip(pieces(scaled, mask.shape[0]), proj):
        projected = dot3(split(u), split(spread(p, mask)))
        out.append(jnp.exp(projected - 0.5 * head_sums(u * u, ones)) * feats ** (-0.5))
    return jnp.concatenate(out, -1)


def feature_back(weighted, scaled, proj, mask, ones):
    out = []
    width = mask.shape[0]
    for w, u, p in zip(pieces(weighted, width), pieces(scaled, width), proj):
        high, low = split(w)
        back = dot3((high, low), split(spread(p, mask)), NT)
        out.append(back - u * (dot(high, ones) + dot(low, ones)))
    return jnp.concatenate(out, -1)


def store_summary(out_ref, matrices, sums):
    size = matrices[0].shape[0]
    base = size * len(matrices)
    out_ref[base:, :] = jnp.zeros((out_ref.shape[0] - base, LANES), F32)
    for step, (matrix, row) in enumerate(zip(matrices, sums)):
        out_ref[step * size : (step + 1) * size, :] = matrix
        out_ref[base + step : base + step + 1, :] = row


def load_summary(refs, steps, size):
    total = refs[0][...]
    for ref in refs[1:]:
        total = total + ref[...]
    base = steps * size
    return [
        (total[step * size : (step + 1) * size], total[base + step : base + step + 1])
        for step in range(steps)
    ]


def outer_sums(a, b, size):
    ah, al = split(a)
    bh, bl = split(b)
    whole = dot(ah, bh, TN) + (dot(ah, bl, TN) + dot(al, bh, TN))
    return gather_diagonal(whole, size)


def summaries(a, b, weighted, steps, size):
    high = a.shape[0] // steps
    parts = [slice(step * high, (step + 1) * high) for step in range(steps)]
    matrices = [outer_sums(a[p], b[p], size) for p in parts]
    return matrices, [jnp.sum(weighted[p], 0, keepdims=True) for p in parts]


def columns(group):
    return pl.ds(pl.multiple_of(group * LANES, LANES), LANES)


def send_columns(sources, refs, me):
    for partner, ref in enumerate(refs):
        own = columns((me ^ partner) % len(refs))
        for place, source in enumerate(sources):
            rows = source.shape[0]
            ref[:rows, place * LANES : (place + 1) * LANES] = source[:, own]


def place_rows(target, refs, steps, column=0):
    rows = target.shape[0] // (steps * len(refs))
    lanes = slice(column * LANES, column * LANES + target.shape[1])
    for partner, ref in enumerate(refs):
        for step in range(steps):
            start = (step * len(refs) + partner) * rows
            target[start : start + rows, :] = ref[step * rows : (step + 1) * rows, lanes].astype(
                target.dtype
            )


def take_rows(values, partner, count, steps):
    rows = values.shape[0] // (steps * count)
    starts = [(step * count + partner) * rows for step in range(steps)]
    return jnp.concatenate([values[s : s + rows] for s in starts], 0)


def widen_kernel(live_ref, x_any, top_ref, low_ref, x_ref, sem):
    copy = pltpu.make_async_copy(x_any, x_ref, sem)
    copy.start()
    half = x_ref.shape[0] // 2
    for ref in (top_ref, low_ref):
        tail = ref.shape[0] - half
        ref[half:, :] = jnp.full((tail, ref.shape[1]), live_ref[0]).astype(F32)
    copy.wait()
    top_ref[:half, :] = x_ref[:half].astype(F32)
    low_ref[:half, :] = x_ref[half:].astype(F32)


def own_columns(count):
    return columns(lax.axis_index("sensor") % count)


def pick_kernel(count, *refs):
    w_refs, proj_ref = refs[:3], refs[3]
    out_refs, p_ref, h_ref, sems = refs[4:7], refs[7], refs[8], refs[9]
    per = h_ref.shape[0]
    start = (lax.axis_index("sensor") % count) * per
    copies = [
        pltpu.make_async_copy(ref.at[:, own_columns(count)], out, sems.at[place])
        for place, (ref, out) in enumerate(zip(w_refs, out_refs))
    ]
    copies.append(pltpu.make_async_copy(proj_ref.at[pl.ds(start, per)], h_ref, sems.at[3]))
    for copy in copies:
        copy.start()
    for copy in copies:
        copy.wait()
    p_ref[...] = jnp.concatenate([h_ref[h] for h in range(per)], -1)


def key_kernel(steps, factor, count, *refs):
    tops, lows = refs[:count], refs[count : 2 * count]
    wk_ref, wv_ref, proj_ref, x_ref, u_ref, v_ref, f_ref, s_ref = refs[2 * count :]
    size = proj_ref.shape[0]
    mask = head_mask(size, LANES)
    rows = x_ref.shape[0] // (steps * count)
    half = steps * rows // 2
    piece = math.gcd(half, rows)
    for partner in range(count):
        for ref, base in ((tops[partner], 0), (lows[partner], half)):
            for row in range(0, half, piece):
                step, inner = divmod(base + row, rows)
                start = (step * count + partner) * rows + inner
                x_ref[start : start + piece, :] = ref[row : row + piece, :].astype(BF16)
    x = x_ref[...]
    scaled = dot(x, wk_ref[...]) * factor
    values = dot(x, wv_ref[...])
    u_ref[...] = scaled
    v_ref[...] = values
    feat = feature_map(scaled, [proj_ref[...]], mask, head_ones(mask), size)
    place = lax.broadcasted_iota(jnp.int32, (rows, LANES), 0).astype(F32)
    keep = jnp.concatenate([place < ref[half : half + 1, :LANES] for ref in tops] * steps, 0)
    feat = jnp.where(keep, feat, 0.0)
    f_ref[...] = feat
    store_summary(s_ref, *summaries(feat, values, feat, steps, size))


def query_kernel(steps, factor, count, live_ref, x_ref, cot_ref, wq_ref, wd_ref, proj_ref, u_ref, f_ref, gh_ref):
    size = proj_ref.shape[0]
    mask = head_mask(size, LANES)
    scaled = dot(x_ref[...], wq_ref[...]) * factor
    u_ref[...] = scaled
    f_ref[...] = feature_map(
        scaled, [proj_ref[...]], mask, head_ones(mask), size
    )
    hidden = dot(cot_ref[...], wd_ref[...], NT)
    place = lax.broadcasted_iota(jnp.int32, hidden.shape, 0) % (hidden.shape[0] // steps)
    gh_ref[...] = jnp.where(place < live_ref[0], hidden, 0.0)


def attend_kernel(steps, size, parts, *refs):
    s_refs, (f_ref, att_ref, inv_ref), out_refs = refs[:parts], refs[parts : parts + 3], refs[parts + 3 :]
    mask = head_mask(size, LANES)
    feat = f_ref[...]
    high = feat.shape[0] // steps
    numer, weighted = [], []
    for step, (matrix, row) in enumerate(load_summary(s_refs, steps, size)):
        part = feat[step * high : (step + 1) * high]
        numer.append(dot3(split(part), split(spread(matrix, mask))))
        weighted.append(part * row)
    inverse = 1.0 / head_sums(jnp.concatenate(weighted, 0), head_ones(mask))
    attended = jnp.concatenate(numer, 0) * inverse
    att_ref[...] = attended
    inv_ref[...] = inverse
    for partner, ref in enumerate(out_refs):
        ref[...] = take_rows(attended, partner, len(out_refs), steps)


def forward_kernel(count, *refs):
    in_refs, (gh_ref, wu_ref) = refs[:count], refs[count : count + 2]
    out_refs, scratch = refs[count + 2 : -1], refs[-1]
    me = lax.axis_index("sensor") % count
    for partner, ref in enumerate(in_refs):
        scratch[:, columns((me ^ partner) % count)] = ref[...]
    attended = scratch[...]
    scale = lax.rsqrt(jnp.mean(attended * attended, -1, keepdims=True) + 1e-06)
    normed = attended * scale
    wu = wu_ref[...]
    pre = dot(normed.astype(BF16), wu)
    c = math.sqrt(2.0 / math.pi)
    square = pre * pre
    t = jnp.tanh(c * pre * (1.0 + 0.044715 * square))
    slope = 0.5 * (1.0 + t) + 0.5 * pre * (1.0 - t * t) * (c * (1.0 + 3 * 0.044715 * square))
    grad_pre = (gh_ref[...] * slope).astype(BF16)
    grad_normed = dot(grad_pre, wu, NT)
    scratch[...] = (
        grad_normed - normed * jnp.mean(grad_normed * normed, -1, keepdims=True)
    ) * scale
    send_columns([scratch], out_refs, me)


def grad_summary_kernel(steps, size, count, *refs):
    in_refs, (att_ref, inv_ref, f_ref) = refs[:count], refs[count : count + 3]
    num_ref, den_ref, g_ref, scratch = refs[count + 3 :]
    place_rows(scratch, in_refs, steps)
    mask = head_mask(size, LANES)
    grad_att = scratch[...]
    inverse = inv_ref[...]
    feat = f_ref[...]
    grad_num = grad_att * inverse
    grad_den = -head_sums(grad_att * att_ref[...], head_ones(mask)) * inverse
    num_ref[...] = grad_num
    den_ref[...] = grad_den
    store_summary(g_ref, *summaries(feat, grad_num, feat * grad_den, steps, size))


def query_back_kernel(steps, factor, count, parts, *refs):
    s_refs, (num_ref, den_ref, f_ref, u_ref, proj_ref, g_ref) = refs[:parts], refs[parts : parts + 6]
    size = proj_ref.shape[0]
    mask = head_mask(size, LANES)
    high = f_ref.shape[0] // steps
    out = []
    for step, (matrix, row) in enumerate(load_summary(s_refs, steps, size)):
        part = slice(step * high, (step + 1) * high)
        back = dot3(split(num_ref[part, :]), split(spread(matrix, mask)), NT)
        out.append(back + den_ref[part, :] * row)
    weighted = jnp.concatenate(out, 0) * f_ref[...]
    grad = feature_back(
        weighted, u_ref[...], [proj_ref[...]], mask, head_ones(mask)
    )
    grad = (grad * factor).astype(BF16)
    g_ref[...] = grad
    for partner, ref in enumerate(refs[parts + 6 :]):
        ref[...] = take_rows(grad, partner, count, steps).astype(F32)


def key_back_kernel(steps, factor, count, parts, devices, *refs):
    g_refs, (u_ref, v_ref, f_ref, proj_ref, gq_ref) = refs[:parts], refs[parts : parts + 5]
    x_all, rest = refs[parts + 5], refs[parts + 6 :]
    back_refs, out_refs, p_ref = rest[:count], rest[count:-1], rest[-1]
    size = proj_ref.shape[0]
    mask = head_mask(size, LANES)
    high = f_ref.shape[0] // steps
    back, grad_v = [], []
    for step, (matrix, row) in enumerate(load_summary(g_refs, steps, size)):
        part = slice(step * high, (step + 1) * high)
        matrix = split(spread(matrix, mask))
        back.append(dot3(split(v_ref[part, :]), matrix, NT) + row)
        grad_v.append(dot3(split(f_ref[part, :]), matrix))
    weighted = jnp.concatenate(back, 0) * f_ref[...]
    grad_k = feature_back(
        weighted, u_ref[...], [proj_ref[...]], mask, head_ones(mask)
    )
    grad = jnp.concatenate([grad_k * factor, jnp.concatenate(grad_v, 0)], -1).astype(BF16)
    for partner, ref in enumerate(back_refs):
        ref[...] = take_rows(grad, partner, count, steps).astype(F32)
    grad = jnp.concatenate([gq_ref[...], grad], -1)
    total = dot(x_all[...], grad, TN)
    block = total.shape[0] // devices
    for place in range(devices):
        p_ref[place % count, place // count] = total[place * block : (place + 1) * block]
    me = lax.axis_index("step")
    for partner, ref in enumerate(out_refs):
        ref[...] = p_ref[(me ^ partner) % count]


def quarter_kernel(count, *refs):
    in_refs, out_refs = refs[:count], refs[count:]
    mine = lax.axis_index("sensor") // count
    for place, ref in enumerate(out_refs):
        block = (mine ^ place) % len(out_refs)
        total = in_refs[0][block]
        for part in in_refs[1:]:
            total = total + part[block]
        ref[...] = total


def rows_kernel(count, *refs):
    q_refs, kv_refs = refs[:count], refs[count : 2 * count]
    wq_ref, wk_ref, wv_ref, out_ref, q_ref, k_ref, v_ref = refs[2 * count :]
    me = lax.axis_index("sensor") % count
    for partner, (q, kv) in enumerate(zip(q_refs, kv_refs)):
        own = columns((me ^ partner) % count)
        q_ref[:, own] = q[...].astype(BF16)
        k_ref[:, own] = kv[:, :LANES].astype(BF16)
        v_ref[:, own] = kv[:, LANES:].astype(BF16)
    total = dot(q_ref[...], wq_ref[...], NT)
    total = total + dot(k_ref[...], wk_ref[...], NT)
    out_ref[...] = (total + dot(v_ref[...], wv_ref[...], NT)).astype(BF16)


def final_kernel(scale, parts, *refs):
    in_refs, outs = refs[:parts], refs[parts:]
    total = in_refs[0][...]
    for ref in in_refs[1:]:
        total = total + ref[...]
    cols = outs[0].shape[1]
    for place, ref in enumerate(outs):
        ref[...] = total[:, place * cols : (place + 1) * cols] * scale


def call(kernel, name, outs, args, flops=0, smem=0, hbm=0, scratch=(), limit=20):
    size = lambda a: math.prod(a.shape) * a.dtype.itemsize
    rest = len(args) - smem - hbm
    return pl.pallas_call(
        kernel,
        name=name,
        out_shape=outs,
        in_specs=[SMEM] * smem + [pl.BlockSpec(memory_space=pl.ANY)] * hbm + [VMEM] * rest,
        out_specs=jax.tree.map(lambda _: VMEM, outs),
        scratch_shapes=list(scratch),
        cost_estimate=pl.CostEstimate(
            flops=flops,
            bytes_accessed=sum(size(a) for a in list(args) + list(jax.tree.leaves(outs))),
            transcendentals=0,
        ),
        compiler_params=pltpu.CompilerParams(vmem_limit_bytes=limit * 1024 * 1024),
    )(*args)


def shape(dims, kind=F32):
    return jax.ShapeDtypeStruct(dims, kind)


def swap(a, axis, bit):
    return lax.ppermute(a, axis, [(i, i ^ bit) for i in range(lax.axis_size(axis))])


def trade(parts, axis):
    return [parts[0]] + [swap(a, axis, d) for d, a in enumerate(parts) if d]


def gather_halves(top, low, axis):
    near_low, next_top = swap(low, axis, 2), swap(top, axis, 1)
    near_top, next_low = swap(top, axis, 2), swap(low, axis, 1)
    across_top, across_low = swap(next_top, axis, 2), swap(near_low, axis, 1)
    return (top, next_top, near_top, across_top), (low, next_low, near_low, across_low)


def far_sum(a, count):
    bit = count
    while bit * 2 < lax.axis_size("sensor"):
        a = a + swap(a, "sensor", bit)
        bit *= 2
    return a, swap(a, "sensor", bit)


def after(a, *others):
    return lax.optimization_barrier((a, others))[0]


def shards(inputs, cotangent, w_query, w_key, w_value, w_up, w_down, feature_proj, live_count):
    steps, sensors, width = inputs.shape
    heads, size, feats = feature_proj.shape
    hidden = w_up.shape[1]
    factor = size ** (-0.25)
    rows = steps * sensors
    devices = lax.axis_size("sensor")
    count = width // LANES
    quads = devices // count
    x = inputs.reshape(rows, width)
    cot = cotangent.reshape(rows, width)
    narrow = shape((rows, LANES))
    tall = shape((rows * count, LANES))
    packed = shape((steps * size + 8, LANES))
    product = 2 * rows * width * width
    kinds = lambda *arrays: [pltpu.VMEM(a.shape, a.dtype) for a in arrays]
    wide = pltpu.VMEM((rows, width), F32)

    top, low = call(
        widen_kernel,
        "widen",
        (shape((rows // 2 + 8, width)),) * 2,
        (live_count, x),
        smem=1,
        hbm=1,
        limit=60,
        scratch=kinds(x) + [pltpu.SemaphoreType.DMA],
    )
    tops, lows = gather_halves(top, low, "sensor")
    narrow_w = shape((width, LANES), BF16)
    own_query, own_key, own_value, proj = call(
        functools.partial(pick_kernel, count),
        "pick_columns",
        (narrow_w,) * 3 + (shape((size, LANES)),),
        (w_query, w_key, w_value, feature_proj),
        hbm=4,
        scratch=[pltpu.VMEM((LANES // feats, size, feats), F32), pltpu.SemaphoreType.DMA((4,))],
    )
    x_all, key, value, feat_key, summary = call(
        functools.partial(key_kernel, steps, factor, count),
        "keys",
        (shape((rows * count, width), BF16),) + (tall,) * 3 + (packed,),
        (*tops, *lows, own_key, own_value, proj),
        flops=3 * product,
    )
    query, feat_query, grad_hidden = call(
        functools.partial(query_kernel, steps, factor, count),
        "queries",
        (tall, tall, shape((rows, hidden))),
        (live_count, x_all, cot, own_query, w_down, proj),
        flops=2 * product,
        smem=1,
    )
    summary = far_sum(summary, count)
    attended, inverse, *local_att = call(
        functools.partial(attend_kernel, steps, size, len(summary)),
        "attend",
        (tall, tall) + (narrow,) * count,
        (*summary, feat_query),
        flops=product,
    )
    local_grad = call(
        functools.partial(forward_kernel, count),
        "feed_forward",
        (narrow,) * count,
        (*trade(local_att, "sensor"), grad_hidden, w_up),
        flops=product,
        scratch=[wide],
    )
    grad_num, grad_den, grad_summary = call(
        functools.partial(grad_summary_kernel, steps, size, count),
        "grad_summary",
        (tall, tall, packed),
        (*trade(local_grad, "sensor"), attended, inverse, feat_query),
        flops=product,
        scratch=kinds(tall),
    )
    grad_summary = far_sum(grad_summary, count)
    grad_q, *local_gq = call(
        functools.partial(query_back_kernel, steps, factor, count, len(summary)),
        "query_back",
        (shape(tall.shape, BF16),) + (narrow,) * count,
        (*summary, grad_num, grad_den, feat_query, query, proj),
        flops=product,
    )
    quad_gq = trade(local_gq, "sensor")
    tile = (width // devices, 3 * LANES)
    back = call(
        functools.partial(key_back_kernel, steps, factor, count, len(grad_summary), devices),
        "key_back",
        (shape((rows, 2 * LANES)),) * count + (shape((quads, *tile)),) * count,
        (*grad_summary, key, value, feat_key, proj, after(grad_q, *quad_gq), x_all),
        flops=4 * product,
        scratch=[pltpu.VMEM((count, quads, *tile), F32)],
    )
    partial = trade(back[count:], "step")

    def turn(a, bit):
        pairs = []
        for k in range(quads):
            for q in range(count):
                for j in range(count):
                    target = (k ^ bit) * count + j
                    pairs.append(((k * count + q) * count + j, target * count + q))
        return lax.ppermute(a, ("sensor", "step"), pairs)

    if quads == 2:
        kept, away = call(
            functools.partial(quarter_kernel, count), "quarter_sums", (shape(tile),) * 2, partial
        )
        parts = (turn(kept, 0), turn(away, 1))
    else:
        groups = [[q + count * k for k in range(quads)] for q in range(count)]
        blocks = lax.all_to_all(sum(partial), "sensor", 0, 0, tiled=True, axis_index_groups=groups)
        parts = (turn(blocks.sum(0), 0),)
    grad_in = call(
        functools.partial(rows_kernel, count),
        "input_rows",
        shape((rows, width), BF16),
        (*quad_gq, *trade(back[:count], "sensor"), w_query, w_key, w_value),
        flops=3 * product,
        scratch=[pltpu.VMEM((rows, width), BF16)] * 3,
    )
    scale = 1.0 / math.sqrt(rows * lax.axis_size("step") * devices)
    out = shape((width // devices, LANES))
    grads = call(
        functools.partial(final_kernel, scale, len(parts)), "weight_sums", (out,) * 3, parts
    )
    return (grad_in.reshape(inputs.shape), *grads)


def solution(mesh):
    return jax.shard_map(
        shards,
        mesh=mesh,
        in_specs=(P("step", "sensor", None),) * 2 + (P(),) * 6 + (P("sensor"),),
        out_specs=(P("step", "sensor", None),) + (P("sensor", "step"),) * 3,
        check_vma=False,
    )
```

```python
import functools
import math

import jax
import jax.numpy as jnp
from jax import lax
from jax.experimental import pallas as pl
from jax.experimental.pallas import tpu as pltpu
from jax.sharding import PartitionSpec as P

F32 = jnp.float32
BF16 = jnp.bfloat16
NN = (((1,), (0,)), ((), ()))
NT = (((1,), (1,)), ((), ()))
TN = (((0,), (0,)), ((), ()))
VMEM = pl.BlockSpec(memory_space=pltpu.VMEM)
SMEM = pl.BlockSpec(memory_space=pltpu.SMEM)
LANES = 128
WIDE = 256


def dot(a, b, dims=NN):
    return lax.dot_general(a, b, dims, preferred_element_type=F32)


def split(x):
    high = x.astype(BF16)
    return high, (x - high.astype(F32)).astype(BF16)


def dot3(a, b, dims=NN):
    return dot(a[0], b[0], dims) + (dot(a[0], b[1], dims) + dot(a[1], b[0], dims))


def head_mask(size, width):
    rows = lax.broadcasted_iota(jnp.int32, (width, width), 0) // size
    cols = lax.broadcasted_iota(jnp.int32, (width, width), 1) // size
    return rows == cols


def head_ones(mask):
    return jnp.where(mask, 1.0, 0.0).astype(BF16)


def spread(x, mask):
    return jnp.where(mask, jnp.concatenate([x] * (x.shape[1] // x.shape[0]), 0), 0.0)


def gather_diagonal(x, size):
    head = lax.broadcasted_iota(jnp.int32, (size, x.shape[1]), 1) // size
    out = x[:size]
    for g in range(1, x.shape[1] // size):
        out = jnp.where(head == g, x[g * size : (g + 1) * size], out)
    return out


def head_sums(x, ones):
    high, low = split(x)
    return dot(high, ones) + dot(low, ones)


def pieces(x, width=WIDE):
    return [x[:, h : h + width] for h in range(0, x.shape[1], width)]


def projection(proj_ref, heads=None, width=WIDE):
    heads = range(proj_ref.shape[0]) if heads is None else heads
    blocks = [proj_ref[h] for h in heads]
    per = width // proj_ref.shape[2]
    return [jnp.concatenate(blocks[g : g + per], -1) for g in range(0, len(blocks), per)]


def feature_map(scaled, proj, mask, ones, feats):
    out = []
    for u, p in zip(pieces(scaled, mask.shape[0]), proj):
        projected = dot3(split(u), split(spread(p, mask)))
        out.append(jnp.exp(projected - 0.5 * head_sums(u * u, ones)) * feats ** (-0.5))
    return jnp.concatenate(out, -1)


def feature_back(weighted, scaled, proj, mask, ones):
    out = []
    width = mask.shape[0]
    for w, u, p in zip(pieces(weighted, width), pieces(scaled, width), proj):
        high, low = split(w)
        back = dot3((high, low), split(spread(p, mask)), NT)
        out.append(back - u * (dot(high, ones) + dot(low, ones)))
    return jnp.concatenate(out, -1)


def store_summary(out_ref, matrices, sums):
    size = matrices[0].shape[0]
    base = size * len(matrices)
    out_ref[base:, :] = jnp.zeros((out_ref.shape[0] - base, LANES), F32)
    for step, (matrix, row) in enumerate(zip(matrices, sums)):
        out_ref[step * size : (step + 1) * size, :] = matrix
        out_ref[base + step : base + step + 1, :] = row


def load_summary(refs, steps, size):
    total = refs[0][...]
    for ref in refs[1:]:
        total = total + ref[...]
    base = steps * size
    return [
        (total[step * size : (step + 1) * size], total[base + step : base + step + 1])
        for step in range(steps)
    ]


def outer_sums(a, b, size):
    ah, al = split(a)
    bh, bl = split(b)
    whole = dot(ah, bh, TN) + (dot(ah, bl, TN) + dot(al, bh, TN))
    return gather_diagonal(whole, size)


def summaries(a, b, weighted, steps, size):
    high = a.shape[0] // steps
    parts = [slice(step * high, (step + 1) * high) for step in range(steps)]
    matrices = [outer_sums(a[p], b[p], size) for p in parts]
    return matrices, [jnp.sum(weighted[p], 0, keepdims=True) for p in parts]


def columns(group):
    return pl.ds(pl.multiple_of(group * LANES, LANES), LANES)


def send_columns(sources, refs, me):
    for partner, ref in enumerate(refs):
        own = columns((me ^ partner) % len(refs))
        for place, source in enumerate(sources):
            rows = source.shape[0]
            ref[:rows, place * LANES : (place + 1) * LANES] = source[:, own]


def place_rows(target, refs, steps, column=0):
    rows = target.shape[0] // (steps * len(refs))
    lanes = slice(column * LANES, column * LANES + target.shape[1])
    for partner, ref in enumerate(refs):
        for step in range(steps):
            start = (step * len(refs) + partner) * rows
            target[start : start + rows, :] = ref[step * rows : (step + 1) * rows, lanes].astype(
                target.dtype
            )


def take_rows(values, partner, count, steps):
    rows = values.shape[0] // (steps * count)
    starts = [(step * count + partner) * rows for step in range(steps)]
    return jnp.concatenate([values[s : s + rows] for s in starts], 0)


def widen_kernel(live_ref, x_any, top_ref, low_ref, x_ref, sem):
    copy = pltpu.make_async_copy(x_any, x_ref, sem)
    copy.start()
    half = x_ref.shape[0] // 2
    for ref in (top_ref, low_ref):
        tail = ref.shape[0] - half
        ref[half:, :] = jnp.full((tail, ref.shape[1]), live_ref[0]).astype(F32)
    copy.wait()
    top_ref[:half, :] = x_ref[:half].astype(F32)
    low_ref[:half, :] = x_ref[half:].astype(F32)


def own_columns(count):
    return columns(lax.axis_index("sensor") % count)


def own_heads(proj_ref, count):
    per = proj_ref.shape[0] // count
    start = (lax.axis_index("sensor") % count) * per
    return jnp.concatenate([proj_ref[start + h] for h in range(per)], -1)


def all_heads(proj_ref):
    per = WIDE // proj_ref.shape[2]
    return [
        jnp.concatenate([proj_ref[g + h] for h in range(per)], -1)
        for g in range(0, proj_ref.shape[0], per)
    ]


def local_kernel(steps, factor, count, live_ref, x_ref, wq_ref, wk_ref, wv_ref, proj_ref, *refs):
    oq_ref, ok_ref, ov_ref, op_ref, u_ref, v_ref, f_ref = refs
    own = own_columns(count)
    oq_ref[...] = wq_ref[:, own]
    ok_ref[...] = wk_ref[:, own]
    ov_ref[...] = wv_ref[:, own]
    op_ref[...] = own_heads(proj_ref, count)
    mask = head_mask(proj_ref.shape[1], WIDE)
    x = x_ref[...]
    scaled = dot(x, wk_ref[...]) * factor
    u_ref[...] = scaled
    v_ref[...] = dot(x, wv_ref[...])
    feat = feature_map(scaled, all_heads(proj_ref), mask, head_ones(mask), proj_ref.shape[2])
    place = lax.broadcasted_iota(jnp.int32, feat.shape, 0) % (feat.shape[0] // steps)
    f_ref[...] = jnp.where(place < live_ref[0], feat, 0.0)


def key_kernel(steps, factor, count, *refs):
    tops, lows = refs[:count], refs[count : 2 * count]
    wk_ref, wv_ref, proj_ref, x_ref, u_ref, v_ref, f_ref, s_ref = refs[2 * count :]
    size = proj_ref.shape[0]
    mask = head_mask(size, LANES)
    rows = x_ref.shape[0] // (steps * count)
    half = steps * rows // 2
    piece = math.gcd(half, rows)
    for partner in range(count):
        for ref, base in ((tops[partner], 0), (lows[partner], half)):
            for row in range(0, half, piece):
                step, inner = divmod(base + row, rows)
                start = (step * count + partner) * rows + inner
                x_ref[start : start + piece, :] = ref[row : row + piece, :].astype(BF16)
    x = x_ref[...]
    scaled = dot(x, wk_ref[...]) * factor
    values = dot(x, wv_ref[...])
    u_ref[...] = scaled
    v_ref[...] = values
    feat = feature_map(scaled, [proj_ref[...]], mask, head_ones(mask), size)
    place = lax.broadcasted_iota(jnp.int32, (rows, LANES), 0).astype(F32)
    keep = jnp.concatenate([place < ref[half : half + 1, :LANES] for ref in tops] * steps, 0)
    feat = jnp.where(keep, feat, 0.0)
    f_ref[...] = feat
    store_summary(s_ref, *summaries(feat, values, feat, steps, size))


def query_kernel(steps, factor, count, live_ref, x_ref, cot_ref, wq_ref, wd_ref, proj_ref, u_ref, f_ref, gh_ref):
    size = proj_ref.shape[0]
    mask = head_mask(size, LANES)
    scaled = dot(x_ref[...], wq_ref[...]) * factor
    u_ref[...] = scaled
    f_ref[...] = feature_map(
        scaled, [proj_ref[...]], mask, head_ones(mask), size
    )
    hidden = dot(cot_ref[...], wd_ref[...], NT)
    place = lax.broadcasted_iota(jnp.int32, hidden.shape, 0) % (hidden.shape[0] // steps)
    gh_ref[...] = jnp.where(place < live_ref[0], hidden, 0.0)


def attend_kernel(steps, size, parts, *refs):
    s_refs, (f_ref, att_ref, inv_ref), out_refs = refs[:parts], refs[parts : parts + 3], refs[parts + 3 :]
    mask = head_mask(size, LANES)
    feat = f_ref[...]
    high = feat.shape[0] // steps
    numer, weighted = [], []
    for step, (matrix, row) in enumerate(load_summary(s_refs, steps, size)):
        part = feat[step * high : (step + 1) * high]
        numer.append(dot3(split(part), split(spread(matrix, mask))))
        weighted.append(part * row)
    inverse = 1.0 / head_sums(jnp.concatenate(weighted, 0), head_ones(mask))
    attended = jnp.concatenate(numer, 0) * inverse
    att_ref[...] = attended
    inv_ref[...] = inverse
    for partner, ref in enumerate(out_refs):
        ref[...] = take_rows(attended, partner, len(out_refs), steps)


def forward_kernel(count, *refs):
    in_refs, (gh_ref, wu_ref) = refs[:count], refs[count : count + 2]
    out_refs, scratch = refs[count + 2 : -1], refs[-1]
    me = lax.axis_index("sensor") % count
    for partner, ref in enumerate(in_refs):
        scratch[:, columns((me ^ partner) % count)] = ref[...]
    attended = scratch[...]
    scale = lax.rsqrt(jnp.mean(attended * attended, -1, keepdims=True) + 1e-06)
    normed = attended * scale
    wu = wu_ref[...]
    pre = dot(normed.astype(BF16), wu)
    c = math.sqrt(2.0 / math.pi)
    square = pre * pre
    t = jnp.tanh(c * pre * (1.0 + 0.044715 * square))
    slope = 0.5 * (1.0 + t) + 0.5 * pre * (1.0 - t * t) * (c * (1.0 + 3 * 0.044715 * square))
    grad_pre = (gh_ref[...] * slope).astype(BF16)
    grad_normed = dot(grad_pre, wu, NT)
    scratch[...] = (
        grad_normed - normed * jnp.mean(grad_normed * normed, -1, keepdims=True)
    ) * scale
    send_columns([scratch], out_refs, me)


def grad_summary_kernel(steps, size, count, *refs):
    in_refs, (att_ref, inv_ref, f_ref) = refs[:count], refs[count : count + 3]
    num_ref, den_ref, g_ref, scratch = refs[count + 3 :]
    place_rows(scratch, in_refs, steps)
    mask = head_mask(size, LANES)
    grad_att = scratch[...]
    inverse = inv_ref[...]
    feat = f_ref[...]
    grad_num = grad_att * inverse
    grad_den = -head_sums(grad_att * att_ref[...], head_ones(mask)) * inverse
    num_ref[...] = grad_num
    den_ref[...] = grad_den
    store_summary(g_ref, *summaries(feat, grad_num, feat * grad_den, steps, size))


def query_back_kernel(steps, factor, count, parts, *refs):
    s_refs, (num_ref, den_ref, f_ref, u_ref, proj_ref, g_ref) = refs[:parts], refs[parts:]
    size = proj_ref.shape[0]
    mask = head_mask(size, LANES)
    high = f_ref.shape[0] // steps
    out = []
    for step, (matrix, row) in enumerate(load_summary(s_refs, steps, size)):
        part = slice(step * high, (step + 1) * high)
        back = dot3(split(num_ref[part, :]), split(spread(matrix, mask)), NT)
        out.append(back + den_ref[part, :] * row)
    weighted = jnp.concatenate(out, 0) * f_ref[...]
    grad = feature_back(
        weighted, u_ref[...], [proj_ref[...]], mask, head_ones(mask)
    )
    g_ref[...] = (grad * factor).astype(BF16)


def key_back_kernel(steps, factor, count, parts, devices, *refs):
    g_refs, (u_ref, v_ref, f_ref, proj_ref, gq_ref) = refs[:parts], refs[parts : parts + 5]
    x_all, rest = refs[parts + 5], refs[parts + 6 :]
    back_refs, (keep_ref, send_ref, p_ref) = rest[:count], rest[count:]
    size = proj_ref.shape[0]
    mask = head_mask(size, LANES)
    high = f_ref.shape[0] // steps
    total = g_refs[0][...]
    for ref in g_refs[1:]:
        total = total + ref[...]
    high_g = total.shape[0]
    for partner, ref in enumerate(back_refs):
        ref[:high_g, :] = total
        ref[high_g:, :] = take_rows(gq_ref[...], partner, count, steps).astype(F32)
    back, grad_v = [], []
    for step, (matrix, row) in enumerate(load_summary(back_refs[:1], steps, size)):
        part = slice(step * high, (step + 1) * high)
        matrix = split(spread(matrix, mask))
        back.append(dot3(split(v_ref[part, :]), matrix, NT) + row)
        grad_v.append(dot3(split(f_ref[part, :]), matrix))
    weighted = jnp.concatenate(back, 0) * f_ref[...]
    grad_k = feature_back(
        weighted, u_ref[...], [proj_ref[...]], mask, head_ones(mask)
    )
    grad = jnp.concatenate([grad_k * factor, jnp.concatenate(grad_v, 0)], -1).astype(BF16)
    total = dot(x_all[...], jnp.concatenate([gq_ref[...], grad], -1), TN)
    block = total.shape[0] // devices
    for place in range(devices):
        p_ref[place % 2, place // 2 % 2, place // 4] = total[place * block : (place + 1) * block]
    low = lax.axis_index("step") % 2
    keep_ref[...] = p_ref[low]
    send_ref[...] = p_ref[1 - low]


def core_kernel(own_ref, got_ref, keep_ref, send_ref):
    high = lax.axis_index("step") // 2 % 2
    keep_ref[...] = own_ref[high] + got_ref[high]
    send_ref[...] = own_ref[1 - high] + got_ref[1 - high]


def half_kernel(count, own_ref, got_ref, keep_ref, send_ref):
    mine = lax.axis_index("sensor") // count
    keep_ref[...] = own_ref[mine] + got_ref[mine]
    send_ref[...] = own_ref[1 - mine] + got_ref[1 - mine]


def rows_kernel(steps, factor, count, *refs):
    in_refs, (u_ref, v_ref, f_ref, proj_ref) = refs[:count], refs[count : count + 4]
    wq_ref, wk_ref, wv_ref, out_ref, q_ref, g_ref = refs[count + 4 :]
    size = proj_ref.shape[1]
    high_g = g_ref.shape[0]
    me = lax.axis_index("sensor") % count
    for partner, ref in enumerate(in_refs):
        own = columns((me ^ partner) % count)
        g_ref[:, own] = ref[:high_g, :]
        q_ref[:, own] = ref[high_g:, :].astype(BF16)
    total = dot(q_ref[...], wq_ref[...], NT)
    mask = head_mask(size, WIDE)
    rows = f_ref.shape[0] // steps
    back, grad_v = [], []
    for step in range(steps):
        part = slice(step * rows, (step + 1) * rows)
        matrix = g_ref[step * size : (step + 1) * size, :]
        spreads = [split(spread(m, mask)) for m in pieces(matrix)]
        values = [split(v) for v in pieces(v_ref[part, :])]
        feats = [split(f) for f in pieces(f_ref[part, :])]
        row = g_ref[steps * size + step : steps * size + step + 1, :]
        back.append(
            jnp.concatenate([dot3(v, m, NT) for v, m in zip(values, spreads)], -1) + row
        )
        grad_v.append(jnp.concatenate([dot3(f, m) for f, m in zip(feats, spreads)], -1))
    weighted = jnp.concatenate(back, 0) * f_ref[...]
    grad_k = feature_back(weighted, u_ref[...], all_heads(proj_ref), mask, head_ones(mask))
    total = total + dot((grad_k * factor).astype(BF16), wk_ref[...], NT)
    grad_v = jnp.concatenate(grad_v, 0).astype(BF16)
    out_ref[...] = (total + dot(grad_v, wv_ref[...], NT)).astype(BF16)


def final_kernel(scale, parts, *refs):
    in_refs, outs = refs[:parts], refs[parts:]
    total = in_refs[0][...]
    for ref in in_refs[1:]:
        total = total + ref[...]
    cols = outs[0].shape[1]
    for place, ref in enumerate(outs):
        ref[...] = total[:, place * cols : (place + 1) * cols] * scale


def call(kernel, name, outs, args, flops=0, smem=0, hbm=0, scratch=(), limit=20):
    size = lambda a: math.prod(a.shape) * a.dtype.itemsize
    rest = len(args) - smem - hbm
    return pl.pallas_call(
        kernel,
        name=name,
        out_shape=outs,
        in_specs=[SMEM] * smem + [pl.BlockSpec(memory_space=pl.ANY)] * hbm + [VMEM] * rest,
        out_specs=jax.tree.map(lambda _: VMEM, outs),
        scratch_shapes=list(scratch),
        cost_estimate=pl.CostEstimate(
            flops=flops,
            bytes_accessed=sum(size(a) for a in list(args) + list(jax.tree.leaves(outs))),
            transcendentals=0,
        ),
        compiler_params=pltpu.CompilerParams(vmem_limit_bytes=limit * 1024 * 1024),
    )(*args)


def shape(dims, kind=F32):
    return jax.ShapeDtypeStruct(dims, kind)


def swap(a, axis, bit):
    return lax.ppermute(a, axis, [(i, i ^ bit) for i in range(lax.axis_size(axis))])


def trade(parts, axis):
    return [parts[0]] + [swap(a, axis, d) for d, a in enumerate(parts) if d]


def gather_halves(top, low, axis):
    near_low, next_top = swap(low, axis, 2), swap(top, axis, 1)
    near_top, next_low = swap(top, axis, 2), swap(low, axis, 1)
    across_top, across_low = swap(next_top, axis, 2), swap(near_low, axis, 1)
    return (top, next_top, near_top, across_top), (low, next_low, near_low, across_low)


def far_sum(a, count):
    bit = count
    while bit * 2 < lax.axis_size("sensor"):
        a = a + swap(a, "sensor", bit)
        bit *= 2
    return a, swap(a, "sensor", bit)


def after(a, *others):
    return lax.optimization_barrier((a, others))[0]


def shards(inputs, cotangent, w_query, w_key, w_value, w_up, w_down, feature_proj, live_count):
    steps, sensors, width = inputs.shape
    heads, size, feats = feature_proj.shape
    hidden = w_up.shape[1]
    factor = size ** (-0.25)
    rows = steps * sensors
    devices = lax.axis_size("sensor")
    count = width // LANES
    quads = devices // count
    x = inputs.reshape(rows, width)
    cot = cotangent.reshape(rows, width)
    narrow = shape((rows, LANES))
    tall = shape((rows * count, LANES))
    packed = shape((steps * size + 8, LANES))
    product = 2 * rows * width * width
    kinds = lambda *arrays: [pltpu.VMEM(a.shape, a.dtype) for a in arrays]
    wide = pltpu.VMEM((rows, width), F32)

    top, low = call(
        widen_kernel,
        "widen",
        (shape((rows // 2 + 8, width)),) * 2,
        (live_count, x),
        smem=1,
        hbm=1,
        limit=60,
        scratch=kinds(x) + [pltpu.SemaphoreType.DMA],
    )
    tops, lows = gather_halves(top, low, "sensor")
    narrow_w = shape((width, LANES), BF16)
    own_query, own_key, own_value, proj, *local_keys = call(
        functools.partial(local_kernel, steps, factor, count),
        "local_keys",
        (narrow_w,) * 3 + (shape((size, LANES)),) + (shape((rows, width)),) * 3,
        (live_count, x, w_query, w_key, w_value, feature_proj),
        flops=3 * product,
        smem=1,
    )
    x_all, key, value, feat_key, summary = call(
        functools.partial(key_kernel, steps, factor, count),
        "keys",
        (shape((rows * count, width), BF16),) + (tall,) * 3 + (packed,),
        (*tops, *lows, own_key, own_value, proj),
        flops=3 * product,
    )
    query, feat_query, grad_hidden = call(
        functools.partial(query_kernel, steps, factor, count),
        "queries",
        (tall, tall, shape((rows, hidden))),
        (live_count, x_all, cot, own_query, w_down, proj),
        flops=2 * product,
        smem=1,
    )
    summary = far_sum(summary, count)
    attended, inverse, *local_att = call(
        functools.partial(attend_kernel, steps, size, len(summary)),
        "attend",
        (tall, tall) + (narrow,) * count,
        (*summary, feat_query),
        flops=product,
    )
    local_grad = call(
        functools.partial(forward_kernel, count),
        "feed_forward",
        (narrow,) * count,
        (*trade(local_att, "sensor"), grad_hidden, w_up),
        flops=product,
        scratch=[wide],
    )
    grad_num, grad_den, grad_summary = call(
        functools.partial(grad_summary_kernel, steps, size, count),
        "grad_summary",
        (tall, tall, packed),
        (*trade(local_grad, "sensor"), attended, inverse, feat_query),
        flops=product,
        scratch=kinds(tall),
    )
    grad_summary = far_sum(grad_summary, count)
    grad_q = call(
        functools.partial(query_back_kernel, steps, factor, count, len(summary)),
        "query_back",
        shape(tall.shape, BF16),
        (*summary, grad_num, grad_den, feat_query, query, proj),
        flops=product,
    )
    tile = (width // devices, 3 * LANES)
    half = shape((2, quads, *tile))
    *messages, own_half, send_half = call(
        functools.partial(key_back_kernel, steps, factor, count, len(grad_summary), devices),
        "key_back",
        (shape((packed.shape[0] + rows, LANES)),) * count + (half, half),
        (*grad_summary, key, value, feat_key, proj, grad_q, x_all),
        flops=4 * product,
        scratch=[pltpu.VMEM((2, *half.shape), F32)],
    )
    quarter = (shape(half.shape[1:]),) * 2
    own_quarter, send_quarter = call(
        core_kernel, "core_sums", quarter, (own_half, swap(send_half, "step", 1))
    )
    got_quarter = swap(send_quarter, "step", 2)
    messages = trade(after(messages, own_quarter), "sensor")

    def turn(a, bit):
        pairs = []
        for k in range(quads):
            for q in range(count):
                for j in range(count):
                    target = (k ^ bit) * count + j
                    pairs.append(((k * count + q) * count + j, target * count + q))
        return lax.ppermute(a, ("sensor", "step"), pairs)

    if quads == 2:
        kept, away = call(
            functools.partial(half_kernel, count),
            "half_sums",
            (shape(tile),) * 2,
            (own_quarter, got_quarter),
        )
        parts = (turn(kept, 0), turn(away, 1))
    else:
        groups = [[q + count * k for k in range(quads)] for q in range(count)]
        blocks = lax.all_to_all(
            own_quarter + got_quarter, "sensor", 0, 0, tiled=True, axis_index_groups=groups
        )
        parts = (turn(blocks.sum(0), 0),)
    grad_in = call(
        functools.partial(rows_kernel, steps, factor, count),
        "input_rows",
        shape((rows, width), BF16),
        (*messages, *local_keys, feature_proj, w_query, w_key, w_value),
        flops=5 * product,
        scratch=[pltpu.VMEM((rows, width), BF16), pltpu.VMEM((packed.shape[0], width), F32)],
    )
    scale = 1.0 / math.sqrt(rows * lax.axis_size("step") * devices)
    out = shape((width // devices, LANES))
    grads = call(
        functools.partial(final_kernel, scale, len(parts)), "weight_sums", (out,) * 3, parts
    )
    return (grad_in.reshape(inputs.shape), *grads)


def solution(mesh):
    return jax.shard_map(
        shards,
        mesh=mesh,
        in_specs=(P("step", "sensor", None),) * 2 + (P(),) * 6 + (P("sensor"),),
        out_specs=(P("step", "sensor", None),) + (P("sensor", "step"),) * 3,
        check_vma=False,
    )
```

```python
import functools
import math

import jax
import jax.numpy as jnp
from jax import lax
from jax.experimental import pallas as pl
from jax.experimental.pallas import tpu as pltpu
from jax.sharding import PartitionSpec as P

F32 = jnp.float32
BF16 = jnp.bfloat16
NN = (((1,), (0,)), ((), ()))
NT = (((1,), (1,)), ((), ()))
TN = (((0,), (0,)), ((), ()))
VMEM = pl.BlockSpec(memory_space=pltpu.VMEM)
SMEM = pl.BlockSpec(memory_space=pltpu.SMEM)
LANES = 128
WIDE = 256


def dot(a, b, dims=NN):
    return lax.dot_general(a, b, dims, preferred_element_type=F32)


def split(x):
    high = x.astype(BF16)
    return high, (x - high.astype(F32)).astype(BF16)


def dot3(a, b, dims=NN):
    if a[0].shape[1] == LANES:
        axis = 1 if dims == NN else 0
        parts = [jnp.concatenate([b[0], b[1]], axis), jnp.concatenate([b[0], 0 * b[1]], axis)]
        out = dot(jnp.concatenate(a, 1), jnp.concatenate(parts, 1 - axis), dims)
        return out[:, :LANES] + out[:, LANES:]
    rows = a[0].shape[0]
    out = dot(jnp.concatenate(a, 0), b[0], dims)
    return out[:rows] + (out[rows:] + dot(a[0], b[1], dims))


def dot2(a, b, dims=NN):
    rows = a[0].shape[0]
    out = dot(jnp.concatenate(a, 0), b, dims)
    return out[:rows] + out[rows:]


def head_mask(size, width):
    rows = lax.broadcasted_iota(jnp.int32, (width, width), 0) // size
    cols = lax.broadcasted_iota(jnp.int32, (width, width), 1) // size
    return rows == cols


def head_ones(mask):
    return jnp.where(mask, 1.0, 0.0).astype(BF16)


def spread(x, mask):
    return jnp.where(mask, jnp.concatenate([x] * (x.shape[1] // x.shape[0]), 0), 0.0)


def gather_diagonal(x, size):
    head = lax.broadcasted_iota(jnp.int32, (size, x.shape[1]), 1) // size
    out = x[:size]
    for g in range(1, x.shape[1] // size):
        out = jnp.where(head == g, x[g * size : (g + 1) * size], out)
    return out


def head_sums(x, ones):
    high, low = split(x)
    if x.shape[1] == LANES:
        return dot(jnp.concatenate([high, low], 1), jnp.concatenate([ones, ones], 0))
    return dot2((high, low), ones)


def pieces(x, width=WIDE):
    return [x[:, h : h + width] for h in range(0, x.shape[1], width)]


def projection(proj_ref, heads=None, width=WIDE):
    heads = range(proj_ref.shape[0]) if heads is None else heads
    blocks = [proj_ref[h] for h in heads]
    per = width // proj_ref.shape[2]
    return [jnp.concatenate(blocks[g : g + per], -1) for g in range(0, len(blocks), per)]


def feature_map(scaled, proj, mask, ones, feats):
    out = []
    for u, p in zip(pieces(scaled, mask.shape[0]), proj):
        projected = dot3(split(u), split(spread(p, mask)))
        out.append(jnp.exp(projected - 0.5 * head_sums(u * u, ones)) * feats ** (-0.5))
    return jnp.concatenate(out, -1)


def feature_back(weighted, scaled, proj, mask, ones):
    out = []
    width = mask.shape[0]
    for w, u, p in zip(pieces(weighted, width), pieces(scaled, width), proj):
        back = dot3(split(w), split(spread(p, mask)), NT)
        out.append(back - u * head_sums(w, ones))
    return jnp.concatenate(out, -1)


def store_summary(out_ref, matrices, sums):
    size = matrices[0].shape[0]
    base = size * len(matrices)
    out_ref[base:, :] = jnp.zeros((out_ref.shape[0] - base, LANES), F32)
    for step, (matrix, row) in enumerate(zip(matrices, sums)):
        out_ref[step * size : (step + 1) * size, :] = matrix
        out_ref[base + step : base + step + 1, :] = row


def load_summary(refs, steps, size):
    total = refs[0][...]
    for ref in refs[1:]:
        total = total + ref[...]
    base = steps * size
    return [
        (total[step * size : (step + 1) * size], total[base + step : base + step + 1])
        for step in range(steps)
    ]


def outer_sums(a, b, size):
    out = dot(jnp.concatenate(split(a), 1), jnp.concatenate(split(b), 1), TN)
    whole = out[:LANES, :LANES] + (out[:LANES, LANES:] + out[LANES:, :LANES])
    return gather_diagonal(whole, size)


def summaries(a, b, weighted, steps, size):
    high = a.shape[0] // steps
    parts = [slice(step * high, (step + 1) * high) for step in range(steps)]
    matrices = [outer_sums(a[p], b[p], size) for p in parts]
    return matrices, [jnp.sum(weighted[p], 0, keepdims=True) for p in parts]


def columns(group):
    return pl.ds(pl.multiple_of(group * LANES, LANES), LANES)


def send_columns(sources, refs, me):
    for partner, ref in enumerate(refs):
        own = columns((me ^ partner) % len(refs))
        for place, source in enumerate(sources):
            rows = source.shape[0]
            ref[:rows, place * LANES : (place + 1) * LANES] = source[:, own]


def place_rows(target, refs, steps, column=0):
    rows = target.shape[0] // (steps * len(refs))
    lanes = slice(column * LANES, column * LANES + target.shape[1])
    for partner, ref in enumerate(refs):
        for step in range(steps):
            start = (step * len(refs) + partner) * rows
            target[start : start + rows, :] = ref[step * rows : (step + 1) * rows, lanes].astype(
                target.dtype
            )


def take_rows(values, partner, count, steps):
    rows = values.shape[0] // (steps * count)
    starts = [(step * count + partner) * rows for step in range(steps)]
    return jnp.concatenate([values[s : s + rows] for s in starts], 0)


def widen_kernel(live_ref, x_ref, top_ref, low_ref):
    half = x_ref.shape[0] // 2
    for ref, base in ((top_ref, 0), (low_ref, half)):
        ref[:half, :] = x_ref[base : base + half].astype(F32)
        ref[half:, :] = jnp.full((ref.shape[0] - half, ref.shape[1]), live_ref[0]).astype(F32)


def own_columns(count):
    return columns(lax.axis_index("sensor") % count)


def own_heads(proj_ref, count):
    per = proj_ref.shape[0] // count
    start = (lax.axis_index("sensor") % count) * per
    return jnp.concatenate([proj_ref[start + h] for h in range(per)], -1)


def all_heads(proj_ref):
    per = WIDE // proj_ref.shape[2]
    return [
        jnp.concatenate([proj_ref[g + h] for h in range(per)], -1)
        for g in range(0, proj_ref.shape[0], per)
    ]


def local_kernel(steps, factor, count, live_ref, x_ref, wq_ref, wk_ref, wv_ref, proj_ref, *refs):
    oq_ref, ok_ref, ov_ref, op_ref, u_ref, v_ref, f_ref = refs
    own = own_columns(count)
    oq_ref[...] = wq_ref[:, own]
    ok_ref[...] = wk_ref[:, own]
    ov_ref[...] = wv_ref[:, own]
    op_ref[...] = own_heads(proj_ref, count)
    mask = head_mask(proj_ref.shape[1], WIDE)
    x = x_ref[...]
    scaled = dot(x, wk_ref[...]) * factor
    u_ref[...] = scaled
    v_ref[...] = dot(x, wv_ref[...])
    feat = feature_map(scaled, all_heads(proj_ref), mask, head_ones(mask), proj_ref.shape[2])
    place = lax.broadcasted_iota(jnp.int32, feat.shape, 0) % (feat.shape[0] // steps)
    f_ref[...] = jnp.where(place < live_ref[0], feat, 0.0)


def key_kernel(steps, factor, count, *refs):
    tops, lows = refs[:count], refs[count : 2 * count]
    wk_ref, wv_ref, proj_ref, x_ref, u_ref, v_ref, f_ref, s_ref = refs[2 * count :]
    size = proj_ref.shape[0]
    mask = head_mask(size, LANES)
    rows = x_ref.shape[0] // (steps * count)
    half = steps * rows // 2
    piece = math.gcd(half, rows)
    for partner in range(count):
        for ref, base in ((tops[partner], 0), (lows[partner], half)):
            for row in range(0, half, piece):
                step, inner = divmod(base + row, rows)
                start = (step * count + partner) * rows + inner
                x_ref[start : start + piece, :] = ref[row : row + piece, :].astype(BF16)
    x = x_ref[...]
    scaled = dot(x, wk_ref[...]) * factor
    values = dot(x, wv_ref[...])
    u_ref[...] = scaled
    v_ref[...] = values
    feat = feature_map(scaled, [proj_ref[...]], mask, head_ones(mask), size)
    place = lax.broadcasted_iota(jnp.int32, (rows, LANES), 0).astype(F32)
    keep = jnp.concatenate([place < ref[half : half + 1, :LANES] for ref in tops] * steps, 0)
    feat = jnp.where(keep, feat, 0.0)
    f_ref[...] = feat
    store_summary(s_ref, *summaries(feat, values, feat, steps, size))


def transpose_kernel(*refs):
    half = len(refs) // 2
    for source, target in zip(refs[:half], refs[half:]):
        target[...] = source[...].T


def query_kernel(steps, factor, count, live_ref, x_ref, cot_ref, wq_ref, wd_ref, proj_ref, u_ref, f_ref, gh_ref):
    size = proj_ref.shape[0]
    mask = head_mask(size, LANES)
    scaled = dot(x_ref[...], wq_ref[...]) * factor
    u_ref[...] = scaled
    f_ref[...] = feature_map(
        scaled, [proj_ref[...]], mask, head_ones(mask), size
    )
    hidden = dot(cot_ref[...], wd_ref[...], NT)
    place = lax.broadcasted_iota(jnp.int32, hidden.shape, 0) % (hidden.shape[0] // steps)
    gh_ref[...] = jnp.where(place < live_ref[0], hidden, 0.0)


def attend_kernel(steps, size, parts, *refs):
    s_refs, (f_ref, att_ref, inv_ref), out_refs = refs[:parts], refs[parts : parts + 3], refs[parts + 3 :]
    mask = head_mask(size, LANES)
    feat = f_ref[...]
    high = feat.shape[0] // steps
    numer, weighted = [], []
    for step, (matrix, row) in enumerate(load_summary(s_refs, steps, size)):
        part = feat[step * high : (step + 1) * high]
        numer.append(dot3(split(part), split(spread(matrix, mask))))
        weighted.append(part * row)
    inverse = 1.0 / head_sums(jnp.concatenate(weighted, 0), head_ones(mask))
    attended = jnp.concatenate(numer, 0) * inverse
    att_ref[...] = attended
    inv_ref[...] = inverse
    for partner, ref in enumerate(out_refs):
        ref[...] = take_rows(attended, partner, len(out_refs), steps)


def forward_kernel(count, *refs):
    in_refs, (gh_ref, wu_ref, wt_ref) = refs[:count], refs[count : count + 3]
    out_refs, scratch = refs[count + 3 : -1], refs[-1]
    me = lax.axis_index("sensor") % count
    for partner, ref in enumerate(in_refs):
        scratch[:, columns((me ^ partner) % count)] = ref[...]
    attended = scratch[...]
    scale = lax.rsqrt(jnp.mean(attended * attended, -1, keepdims=True) + 1e-06)
    normed = attended * scale
    pre = dot(normed.astype(BF16), wu_ref[...])
    c = math.sqrt(2.0 / math.pi)
    square = pre * pre
    t = jnp.tanh(c * pre * (1.0 + 0.044715 * square))
    slope = 0.5 * (1.0 + t) + 0.5 * pre * (1.0 - t * t) * (c * (1.0 + 3 * 0.044715 * square))
    grad_pre = (gh_ref[...] * slope).astype(BF16)
    grad_normed = dot(grad_pre, wt_ref[...])
    scratch[...] = (
        grad_normed - normed * jnp.mean(grad_normed * normed, -1, keepdims=True)
    ) * scale
    send_columns([scratch], out_refs, me)


def grad_summary_kernel(steps, size, count, *refs):
    in_refs, (att_ref, inv_ref, f_ref) = refs[:count], refs[count : count + 3]
    num_ref, den_ref, g_ref, scratch = refs[count + 3 :]
    place_rows(scratch, in_refs, steps)
    mask = head_mask(size, LANES)
    grad_att = scratch[...]
    inverse = inv_ref[...]
    feat = f_ref[...]
    grad_num = grad_att * inverse
    grad_den = -head_sums(grad_att * att_ref[...], head_ones(mask)) * inverse
    num_ref[...] = grad_num
    den_ref[...] = grad_den
    store_summary(g_ref, *summaries(feat, grad_num, feat * grad_den, steps, size))


def query_back_kernel(steps, factor, count, parts, *refs):
    s_refs, (num_ref, den_ref, f_ref, u_ref, proj_ref, g_ref) = refs[:parts], refs[parts:]
    size = proj_ref.shape[0]
    mask = head_mask(size, LANES)
    high = f_ref.shape[0] // steps
    out = []
    for step, (matrix, row) in enumerate(load_summary(s_refs, steps, size)):
        part = slice(step * high, (step + 1) * high)
        back = dot3(split(num_ref[part, :]), split(spread(matrix, mask)), NT)
        out.append(back + den_ref[part, :] * row)
    weighted = jnp.concatenate(out, 0) * f_ref[...]
    grad = feature_back(
        weighted, u_ref[...], [proj_ref[...]], mask, head_ones(mask)
    )
    g_ref[...] = (grad * factor).astype(BF16)


def key_back_kernel(steps, factor, count, parts, devices, *refs):
    g_refs, (u_ref, v_ref, f_ref, proj_ref, gq_ref) = refs[:parts], refs[parts : parts + 5]
    x_all, rest = refs[parts + 5], refs[parts + 6 :]
    back_refs, (keep_ref, send_ref, p_ref) = rest[:count], rest[count:]
    size = proj_ref.shape[0]
    mask = head_mask(size, LANES)
    high = f_ref.shape[0] // steps
    total = g_refs[0][...]
    for ref in g_refs[1:]:
        total = total + ref[...]
    high_g = total.shape[0]
    for partner, ref in enumerate(back_refs):
        ref[:high_g, :] = total
        ref[high_g:, :] = take_rows(gq_ref[...], partner, count, steps).astype(F32)
    back, grad_v = [], []
    for step, (matrix, row) in enumerate(load_summary(back_refs[:1], steps, size)):
        part = slice(step * high, (step + 1) * high)
        matrix = split(spread(matrix, mask))
        back.append(dot3(split(v_ref[part, :]), matrix, NT) + row)
        grad_v.append(dot3(split(f_ref[part, :]), matrix))
    weighted = jnp.concatenate(back, 0) * f_ref[...]
    grad_k = feature_back(
        weighted, u_ref[...], [proj_ref[...]], mask, head_ones(mask)
    )
    grad = jnp.concatenate([grad_k * factor, jnp.concatenate(grad_v, 0)], -1).astype(BF16)
    total = dot(x_all[...], jnp.concatenate([gq_ref[...], grad], -1))
    block = total.shape[0] // devices
    for place in range(devices):
        p_ref[place % 2, place // 2 % 2, place // 4] = total[place * block : (place + 1) * block]
    low = lax.axis_index("step") % 2
    keep_ref[...] = p_ref[low]
    send_ref[...] = p_ref[1 - low]


def core_kernel(count, own_ref, got_ref, *refs):
    high = lax.axis_index("step") // 2 % 2
    mine = lax.axis_index("sensor") // count
    per = len(refs) // 2
    for place, ref in enumerate(refs):
        part = high ^ (place // per)
        if per == 2:
            block = mine ^ (place % 2)
            ref[...] = own_ref[part, block] + got_ref[part, block]
        else:
            ref[...] = own_ref[part] + got_ref[part]


def rows_kernel(steps, factor, count, *refs):
    in_refs, (u_ref, v_ref, f_ref, proj_ref) = refs[:count], refs[count : count + 4]
    wq_ref, wk_ref, wv_ref, out_ref, q_ref, g_ref = refs[count + 4 :]
    size = proj_ref.shape[1]
    high_g = g_ref.shape[0]
    me = lax.axis_index("sensor") % count
    for partner, ref in enumerate(in_refs):
        own = columns((me ^ partner) % count)
        g_ref[:, own] = ref[:high_g, :]
        q_ref[:, own] = ref[high_g:, :].astype(BF16)
    total = dot(q_ref[...], wq_ref[...])
    mask = head_mask(size, WIDE)
    rows = f_ref.shape[0] // steps
    back, grad_v = [], []
    for step in range(steps):
        part = slice(step * rows, (step + 1) * rows)
        matrix = g_ref[step * size : (step + 1) * size, :]
        spreads = [split(spread(m, mask)) for m in pieces(matrix)]
        values = [split(v) for v in pieces(v_ref[part, :])]
        feats = [split(f) for f in pieces(f_ref[part, :])]
        row = g_ref[steps * size + step : steps * size + step + 1, :]
        back.append(
            jnp.concatenate([dot3(v, m, NT) for v, m in zip(values, spreads)], -1) + row
        )
        grad_v.append(jnp.concatenate([dot3(f, m) for f, m in zip(feats, spreads)], -1))
    weighted = jnp.concatenate(back, 0) * f_ref[...]
    grad_k = feature_back(weighted, u_ref[...], all_heads(proj_ref), mask, head_ones(mask))
    total = total + dot((grad_k * factor).astype(BF16), wk_ref[...])
    grad_v = jnp.concatenate(grad_v, 0).astype(BF16)
    out_ref[...] = (total + dot(grad_v, wv_ref[...])).astype(BF16)


def final_kernel(scale, parts, *refs):
    in_refs, outs = refs[:parts], refs[parts:]
    total = in_refs[0][...]
    for ref in in_refs[1:]:
        total = total + ref[...]
    cols = outs[0].shape[1]
    for place, ref in enumerate(outs):
        ref[...] = total[:, place * cols : (place + 1) * cols] * scale


def call(kernel, name, outs, args, flops=0, smem=0, hbm=0, scratch=(), limit=20):
    size = lambda a: math.prod(a.shape) * a.dtype.itemsize
    rest = len(args) - smem - hbm
    return pl.pallas_call(
        kernel,
        name=name,
        out_shape=outs,
        in_specs=[SMEM] * smem + [pl.BlockSpec(memory_space=pl.ANY)] * hbm + [VMEM] * rest,
        out_specs=jax.tree.map(lambda _: VMEM, outs),
        scratch_shapes=list(scratch),
        cost_estimate=pl.CostEstimate(
            flops=flops,
            bytes_accessed=sum(size(a) for a in list(args) + list(jax.tree.leaves(outs))),
            transcendentals=0,
        ),
        compiler_params=pltpu.CompilerParams(vmem_limit_bytes=limit * 1024 * 1024),
    )(*args)


def shape(dims, kind=F32):
    return jax.ShapeDtypeStruct(dims, kind)


def swap(a, axis, bit):
    return lax.ppermute(a, axis, [(i, i ^ bit) for i in range(lax.axis_size(axis))])


def trade(parts, axis):
    got = {d: swap(parts[d], axis, d) for d in reversed(range(1, len(parts)))}
    return [parts[0]] + [got[d] for d in sorted(got)]


def gather_halves(top, low, axis):
    near_low, next_top = swap(low, axis, 2), swap(top, axis, 1)
    near_top, next_low = swap(top, axis, 2), swap(low, axis, 1)
    across_top, across_low = swap(next_top, axis, 2), swap(near_low, axis, 1)
    return (top, next_top, near_top, across_top), (low, next_low, near_low, across_low)


def far_sum(a, count):
    bit = count
    while bit * 2 < lax.axis_size("sensor"):
        a = a + swap(a, "sensor", bit)
        bit *= 2
    return a, swap(a, "sensor", bit)


def after(a, *others):
    return lax.optimization_barrier((a, others))[0]


def shards(inputs, cotangent, w_query, w_key, w_value, w_up, w_down, feature_proj, live_count):
    steps, sensors, width = inputs.shape
    heads, size, feats = feature_proj.shape
    hidden = w_up.shape[1]
    factor = size ** (-0.25)
    rows = steps * sensors
    devices = lax.axis_size("sensor")
    count = width // LANES
    quads = devices // count
    x = inputs.reshape(rows, width)
    cot = cotangent.reshape(rows, width)
    narrow = shape((rows, LANES))
    tall = shape((rows * count, LANES))
    packed = shape((steps * size + 8, LANES))
    product = 2 * rows * width * width
    kinds = lambda *arrays: [pltpu.VMEM(a.shape, a.dtype) for a in arrays]
    wide = pltpu.VMEM((rows, width), F32)

    top, low = call(
        widen_kernel,
        "widen",
        (shape((rows // 2 + 8, width)),) * 2,
        (live_count, x),
        smem=1,
    )
    tops, lows = gather_halves(top, low, "sensor")
    narrow_w = shape((width, LANES), BF16)
    own_query, own_key, own_value, proj, *local_keys = call(
        functools.partial(local_kernel, steps, factor, count),
        "local_keys",
        (narrow_w,) * 3 + (shape((size, LANES)),) + (shape((rows, width)),) * 3,
        (live_count, x, w_query, w_key, w_value, feature_proj),
        flops=3 * product,
        smem=1,
    )
    x_all, key, value, feat_key, summary = call(
        functools.partial(key_kernel, steps, factor, count),
        "keys",
        (shape((rows * count, width), BF16),) + (tall,) * 3 + (packed,),
        (*tops, *lows, own_key, own_value, proj),
        flops=3 * product,
    )
    turned = (x_all, w_query, w_key, w_value, w_up)
    x_turned, wq_turned, wk_turned, wv_turned, wu_turned = call(
        transpose_kernel, "transposes", tuple(shape(a.shape[::-1], BF16) for a in turned), turned
    )
    query, feat_query, grad_hidden = call(
        functools.partial(query_kernel, steps, factor, count),
        "queries",
        (tall, tall, shape((rows, hidden))),
        (live_count, x_all, cot, own_query, w_down, proj),
        flops=2 * product,
        smem=1,
    )
    summary = far_sum(summary, count)
    attended, inverse, *local_att = call(
        functools.partial(attend_kernel, steps, size, len(summary)),
        "attend",
        (tall, tall) + (narrow,) * count,
        (*summary, feat_query),
        flops=product,
    )
    local_grad = call(
        functools.partial(forward_kernel, count),
        "feed_forward",
        (narrow,) * count,
        (*trade(local_att, "sensor"), grad_hidden, w_up, wu_turned),
        flops=product,
        scratch=[wide],
    )
    grad_num, grad_den, grad_summary = call(
        functools.partial(grad_summary_kernel, steps, size, count),
        "grad_summary",
        (tall, tall, packed),
        (*trade(local_grad, "sensor"), attended, inverse, feat_query),
        flops=product,
        scratch=kinds(tall),
    )
    grad_summary = far_sum(grad_summary, count)
    grad_q = call(
        functools.partial(query_back_kernel, steps, factor, count, len(summary)),
        "query_back",
        shape(tall.shape, BF16),
        (*summary, grad_num, grad_den, feat_query, query, proj),
        flops=product,
    )
    tile = (width // devices, 3 * LANES)
    half = shape((2, quads, *tile))
    *messages, own_half, send_half = call(
        functools.partial(key_back_kernel, steps, factor, count, len(grad_summary), devices),
        "key_back",
        (shape((packed.shape[0] + rows, LANES)),) * count + (half, half),
        (*grad_summary, key, value, feat_key, proj, grad_q, x_turned),
        flops=4 * product,
        scratch=[pltpu.VMEM((2, *half.shape), F32)],
    )
    def turn(a, bit):
        pairs = []
        for k in range(quads):
            for q in range(count):
                for j in range(count):
                    target = (k ^ bit) * count + j
                    pairs.append(((k * count + q) * count + j, target * count + q))
        return lax.ppermute(a, ("sensor", "step"), pairs)

    got_half = swap(send_half, "step", 1)
    if quads == 2:
        kept, away, send_kept, send_away = call(
            functools.partial(core_kernel, count),
            "core_sums",
            (shape(tile),) * 4,
            (own_half, got_half),
        )
        ready = kept
        away = away + swap(send_away, "step", 2)
        kept = kept + swap(send_kept, "step", 2)
        parts = (turn(away, 1), turn(kept, 0))
    else:
        kept, sent = call(
            functools.partial(core_kernel, count),
            "core_sums",
            (shape((quads, *tile)),) * 2,
            (own_half, got_half),
        )
        ready = kept
        groups = [[q + count * k for k in range(quads)] for q in range(count)]
        blocks = lax.all_to_all(
            kept + swap(sent, "step", 2), "sensor", 0, 0, tiled=True, axis_index_groups=groups
        )
        parts = (turn(blocks.sum(0), 0),)
    messages = trade(after(messages, ready), "sensor")
    scale = 1.0 / math.sqrt(rows * lax.axis_size("step") * devices)
    out = shape((width // devices, LANES))
    grad_in = call(
        functools.partial(rows_kernel, steps, factor, count),
        "input_rows",
        shape((rows, width), BF16),
        (*messages, *local_keys, feature_proj, wq_turned, wk_turned, wv_turned),
        flops=5 * product,
        scratch=[pltpu.VMEM((rows, width), BF16), pltpu.VMEM((packed.shape[0], width), F32)],
    )
    grads = call(
        functools.partial(final_kernel, scale, len(parts)),
        "weight_sums",
        (out,) * 3,
        (after(parts[0], grad_in), *parts[1:]),
    )
    return (grad_in.reshape(inputs.shape), *grads)


def solution(mesh):
    return jax.shard_map(
        shards,
        mesh=mesh,
        in_specs=(P("step", "sensor", None),) * 2 + (P(),) * 6 + (P("sensor"),),
        out_specs=(P("step", "sensor", None),) + (P("sensor", "step"),) * 3,
        check_vma=False,
    )
```

```python
import functools
import math

import jax
import jax.numpy as jnp
from jax import lax
from jax.experimental import pallas as pl
from jax.experimental.pallas import tpu as pltpu
from jax.sharding import PartitionSpec as P

F32 = jnp.float32
BF16 = jnp.bfloat16
NN = (((1,), (0,)), ((), ()))
NT = (((1,), (1,)), ((), ()))
TN = (((0,), (0,)), ((), ()))
VMEM = pl.BlockSpec(memory_space=pltpu.VMEM)
SMEM = pl.BlockSpec(memory_space=pltpu.SMEM)
LANES = 128
WIDE = 256


def dot(a, b, dims=NN):
    return lax.dot_general(a, b, dims, preferred_element_type=F32)


def split(x):
    high = x.astype(BF16)
    return high, (x - high.astype(F32)).astype(BF16)


def dot3(a, b, dims=NN):
    if a[0].shape[1] == LANES:
        axis = 1 if dims == NN else 0
        parts = [jnp.concatenate([b[0], b[1]], axis), jnp.concatenate([b[0], 0 * b[1]], axis)]
        out = dot(jnp.concatenate(a, 1), jnp.concatenate(parts, 1 - axis), dims)
        return out[:, :LANES] + out[:, LANES:]
    rows = a[0].shape[0]
    out = dot(jnp.concatenate(a, 0), b[0], dims)
    return out[:rows] + (out[rows:] + dot(a[0], b[1], dims))


def dot2(a, b, dims=NN):
    rows = a[0].shape[0]
    out = dot(jnp.concatenate(a, 0), b, dims)
    return out[:rows] + out[rows:]


def head_mask(size, width):
    rows = lax.broadcasted_iota(jnp.int32, (width, width), 0) // size
    cols = lax.broadcasted_iota(jnp.int32, (width, width), 1) // size
    return rows == cols


def head_ones(mask):
    return jnp.where(mask, 1.0, 0.0).astype(BF16)


def spread(x, mask):
    return jnp.where(mask, jnp.concatenate([x] * (x.shape[1] // x.shape[0]), 0), 0.0)


def gather_diagonal(x, size):
    head = lax.broadcasted_iota(jnp.int32, (size, x.shape[1]), 1) // size
    out = x[:size]
    for g in range(1, x.shape[1] // size):
        out = jnp.where(head == g, x[g * size : (g + 1) * size], out)
    return out


def head_sums(x, ones):
    high, low = split(x)
    if x.shape[1] == LANES:
        return dot(jnp.concatenate([high, low], 1), jnp.concatenate([ones, ones], 0))
    return dot2((high, low), ones)


def pieces(x, width=WIDE):
    return [x[:, h : h + width] for h in range(0, x.shape[1], width)]


def projection(proj_ref, heads=None, width=WIDE):
    heads = range(proj_ref.shape[0]) if heads is None else heads
    blocks = [proj_ref[h] for h in heads]
    per = width // proj_ref.shape[2]
    return [jnp.concatenate(blocks[g : g + per], -1) for g in range(0, len(blocks), per)]


def feature_map(scaled, proj, mask, ones, feats):
    out = []
    for u, p in zip(pieces(scaled, mask.shape[0]), proj):
        projected = dot3(split(u), split(spread(p, mask)))
        out.append(jnp.exp(projected - 0.5 * head_sums(u * u, ones)) * feats ** (-0.5))
    return jnp.concatenate(out, -1)


def feature_back(weighted, scaled, proj, mask, ones):
    out = []
    width = mask.shape[0]
    for w, u, p in zip(pieces(weighted, width), pieces(scaled, width), proj):
        back = dot3(split(w), split(spread(p, mask)), NT)
        out.append(back - u * head_sums(w, ones))
    return jnp.concatenate(out, -1)


def store_summary(out_ref, matrices, sums):
    size = matrices[0].shape[0]
    base = size * len(matrices)
    out_ref[base:, :] = jnp.zeros((out_ref.shape[0] - base, LANES), F32)
    for step, (matrix, row) in enumerate(zip(matrices, sums)):
        out_ref[step * size : (step + 1) * size, :] = matrix
        out_ref[base + step : base + step + 1, :] = row


def load_summary(refs, steps, size):
    total = refs[0][...]
    for ref in refs[1:]:
        total = total + ref[...]
    base = steps * size
    return [
        (total[step * size : (step + 1) * size], total[base + step : base + step + 1])
        for step in range(steps)
    ]


def outer_sums(a, b, size):
    out = dot(jnp.concatenate(split(a), 1), jnp.concatenate(split(b), 1), TN)
    whole = out[:LANES, :LANES] + (out[:LANES, LANES:] + out[LANES:, :LANES])
    return gather_diagonal(whole, size)


def summaries(a, b, weighted, steps, size):
    high = a.shape[0] // steps
    parts = [slice(step * high, (step + 1) * high) for step in range(steps)]
    matrices = [outer_sums(a[p], b[p], size) for p in parts]
    return matrices, [jnp.sum(weighted[p], 0, keepdims=True) for p in parts]


def columns(group):
    return pl.ds(pl.multiple_of(group * LANES, LANES), LANES)


def send_columns(sources, refs, me):
    for partner, ref in enumerate(refs):
        own = columns((me ^ partner) % len(refs))
        for place, source in enumerate(sources):
            rows = source.shape[0]
            ref[:rows, place * LANES : (place + 1) * LANES] = source[:, own]


def place_rows(target, refs, steps, column=0):
    rows = target.shape[0] // (steps * len(refs))
    lanes = slice(column * LANES, column * LANES + target.shape[1])
    for partner, ref in enumerate(refs):
        for step in range(steps):
            start = (step * len(refs) + partner) * rows
            target[start : start + rows, :] = ref[step * rows : (step + 1) * rows, lanes].astype(
                target.dtype
            )


def take_rows(values, partner, count, steps):
    rows = values.shape[0] // (steps * count)
    starts = [(step * count + partner) * rows for step in range(steps)]
    return jnp.concatenate([values[s : s + rows] for s in starts], 0)


def widen_kernel(live_ref, x_ref, top_ref, low_ref):
    half = x_ref.shape[0] // 2
    for ref, base in ((top_ref, 0), (low_ref, half)):
        ref[:half, :] = x_ref[base : base + half].astype(F32)
        ref[half:, :] = jnp.full((ref.shape[0] - half, ref.shape[1]), live_ref[0]).astype(F32)


def own_columns(count):
    return columns(lax.axis_index("sensor") % count)


def own_heads(proj_ref, count):
    per = proj_ref.shape[0] // count
    start = (lax.axis_index("sensor") % count) * per
    return jnp.concatenate([proj_ref[start + h] for h in range(per)], -1)


def all_heads(proj_ref):
    per = WIDE // proj_ref.shape[2]
    return [
        jnp.concatenate([proj_ref[g + h] for h in range(per)], -1)
        for g in range(0, proj_ref.shape[0], per)
    ]


def local_kernel(steps, factor, count, live_ref, x_ref, wq_ref, wk_ref, wv_ref, proj_ref, *refs):
    oq_ref, ok_ref, ov_ref, op_ref, u_ref, v_ref, f_ref = refs
    own = own_columns(count)
    oq_ref[...] = wq_ref[:, own]
    ok_ref[...] = wk_ref[:, own]
    ov_ref[...] = wv_ref[:, own]
    op_ref[...] = own_heads(proj_ref, count)
    mask = head_mask(proj_ref.shape[1], WIDE)
    x = x_ref[...]
    scaled = dot(x, wk_ref[...]) * factor
    u_ref[...] = scaled
    v_ref[...] = dot(x, wv_ref[...])
    feat = feature_map(scaled, all_heads(proj_ref), mask, head_ones(mask), proj_ref.shape[2])
    place = lax.broadcasted_iota(jnp.int32, feat.shape, 0) % (feat.shape[0] // steps)
    f_ref[...] = jnp.where(place < live_ref[0], feat, 0.0)


def key_kernel(steps, factor, count, *refs):
    tops, lows = refs[:count], refs[count : 2 * count]
    wk_ref, wv_ref, proj_ref, x_ref, u_ref, v_ref, f_ref, s_ref = refs[2 * count :]
    size = proj_ref.shape[0]
    mask = head_mask(size, LANES)
    rows = x_ref.shape[0] // (steps * count)
    half = steps * rows // 2
    piece = math.gcd(half, rows)
    for partner in range(count):
        for ref, base in ((tops[partner], 0), (lows[partner], half)):
            for row in range(0, half, piece):
                step, inner = divmod(base + row, rows)
                start = (step * count + partner) * rows + inner
                x_ref[start : start + piece, :] = ref[row : row + piece, :].astype(BF16)
    x = x_ref[...]
    scaled = dot(x, wk_ref[...]) * factor
    values = dot(x, wv_ref[...])
    u_ref[...] = scaled
    v_ref[...] = values
    feat = feature_map(scaled, [proj_ref[...]], mask, head_ones(mask), size)
    place = lax.broadcasted_iota(jnp.int32, (rows, LANES), 0).astype(F32)
    keep = jnp.concatenate([place < ref[half : half + 1, :LANES] for ref in tops] * steps, 0)
    feat = jnp.where(keep, feat, 0.0)
    f_ref[...] = feat
    store_summary(s_ref, *summaries(feat, values, feat, steps, size))


def transpose_kernel(*refs):
    half = len(refs) // 2
    for source, target in zip(refs[:half], refs[half:]):
        target[...] = source[...].T


def query_kernel(steps, factor, count, live_ref, x_ref, cot_ref, wq_ref, wd_ref, proj_ref, u_ref, f_ref, gh_ref):
    size = proj_ref.shape[0]
    mask = head_mask(size, LANES)
    scaled = dot(x_ref[...], wq_ref[...]) * factor
    u_ref[...] = scaled
    f_ref[...] = feature_map(
        scaled, [proj_ref[...]], mask, head_ones(mask), size
    )
    hidden = dot(cot_ref[...], wd_ref[...], NT)
    place = lax.broadcasted_iota(jnp.int32, hidden.shape, 0) % (hidden.shape[0] // steps)
    gh_ref[...] = jnp.where(place < live_ref[0], hidden, 0.0)


def attend_kernel(steps, size, parts, *refs):
    s_refs, (f_ref, att_ref, inv_ref), out_refs = refs[:parts], refs[parts : parts + 3], refs[parts + 3 :]
    mask = head_mask(size, LANES)
    feat = f_ref[...]
    high = feat.shape[0] // steps
    numer, weighted = [], []
    for step, (matrix, row) in enumerate(load_summary(s_refs, steps, size)):
        part = feat[step * high : (step + 1) * high]
        numer.append(dot3(split(part), split(spread(matrix, mask))))
        weighted.append(part * row)
    inverse = 1.0 / head_sums(jnp.concatenate(weighted, 0), head_ones(mask))
    attended = jnp.concatenate(numer, 0) * inverse
    att_ref[...] = attended
    inv_ref[...] = inverse
    for partner, ref in enumerate(out_refs):
        ref[...] = take_rows(attended, partner, len(out_refs), steps)


def forward_kernel(count, *refs):
    in_refs, (gh_ref, wu_ref, wt_ref) = refs[:count], refs[count : count + 3]
    out_refs, scratch = refs[count + 3 : -1], refs[-1]
    me = lax.axis_index("sensor") % count
    for partner, ref in enumerate(in_refs):
        scratch[:, columns((me ^ partner) % count)] = ref[...]
    attended = scratch[...]
    scale = lax.rsqrt(jnp.mean(attended * attended, -1, keepdims=True) + 1e-06)
    normed = attended * scale
    pre = dot(normed.astype(BF16), wu_ref[...])
    c = math.sqrt(2.0 / math.pi)
    square = pre * pre
    t = jnp.tanh(c * pre * (1.0 + 0.044715 * square))
    slope = 0.5 * (1.0 + t) + 0.5 * pre * (1.0 - t * t) * (c * (1.0 + 3 * 0.044715 * square))
    grad_pre = (gh_ref[...] * slope).astype(BF16)
    grad_normed = dot(grad_pre, wt_ref[...])
    scratch[...] = (
        grad_normed - normed * jnp.mean(grad_normed * normed, -1, keepdims=True)
    ) * scale
    send_columns([scratch], out_refs, me)


def grad_summary_kernel(steps, size, count, *refs):
    in_refs, (att_ref, inv_ref, f_ref) = refs[:count], refs[count : count + 3]
    num_ref, den_ref, g_ref, scratch = refs[count + 3 :]
    place_rows(scratch, in_refs, steps)
    mask = head_mask(size, LANES)
    grad_att = scratch[...]
    inverse = inv_ref[...]
    feat = f_ref[...]
    grad_num = grad_att * inverse
    grad_den = -head_sums(grad_att * att_ref[...], head_ones(mask)) * inverse
    num_ref[...] = grad_num
    den_ref[...] = grad_den
    store_summary(g_ref, *summaries(feat, grad_num, feat * grad_den, steps, size))


def query_back_kernel(steps, factor, count, parts, *refs):
    s_refs, (num_ref, den_ref, f_ref, u_ref, proj_ref, g_ref) = refs[:parts], refs[parts:]
    size = proj_ref.shape[0]
    mask = head_mask(size, LANES)
    high = f_ref.shape[0] // steps
    out = []
    for step, (matrix, row) in enumerate(load_summary(s_refs, steps, size)):
        part = slice(step * high, (step + 1) * high)
        back = dot3(split(num_ref[part, :]), split(spread(matrix, mask)), NT)
        out.append(back + den_ref[part, :] * row)
    weighted = jnp.concatenate(out, 0) * f_ref[...]
    grad = feature_back(
        weighted, u_ref[...], [proj_ref[...]], mask, head_ones(mask)
    )
    g_ref[...] = (grad * factor).astype(BF16)


def key_back_kernel(steps, factor, count, parts, devices, *refs):
    g_refs, (u_ref, v_ref, f_ref, proj_ref, gq_ref) = refs[:parts], refs[parts : parts + 5]
    x_all, rest = refs[parts + 5], refs[parts + 6 :]
    back_refs, (keep_ref, send_ref, p_ref) = rest[:count], rest[count:]
    size = proj_ref.shape[0]
    mask = head_mask(size, LANES)
    high = f_ref.shape[0] // steps
    total = g_refs[0][...]
    for ref in g_refs[1:]:
        total = total + ref[...]
    high_g = total.shape[0]
    for partner, ref in enumerate(back_refs):
        ref[:high_g, :] = total
        ref[high_g:, :] = take_rows(gq_ref[...], partner, count, steps).astype(F32)
    back, grad_v = [], []
    for step, (matrix, row) in enumerate(load_summary(back_refs[:1], steps, size)):
        part = slice(step * high, (step + 1) * high)
        matrix = split(spread(matrix, mask))
        back.append(dot3(split(v_ref[part, :]), matrix, NT) + row)
        grad_v.append(dot3(split(f_ref[part, :]), matrix))
    weighted = jnp.concatenate(back, 0) * f_ref[...]
    grad_k = feature_back(
        weighted, u_ref[...], [proj_ref[...]], mask, head_ones(mask)
    )
    grad = jnp.concatenate([grad_k * factor, jnp.concatenate(grad_v, 0)], -1).astype(BF16)
    total = dot(x_all[...], jnp.concatenate([gq_ref[...], grad], -1))
    block = total.shape[0] // devices
    for place in range(devices):
        p_ref[place % 2, place // 2 % 2, place // 4] = total[place * block : (place + 1) * block]
    low = lax.axis_index("step") % 2
    keep_ref[...] = p_ref[low]
    send_ref[...] = p_ref[1 - low]


def core_kernel(count, own_ref, got_ref, *refs):
    high = lax.axis_index("step") // 2 % 2
    mine = lax.axis_index("sensor") // count
    per = len(refs) // 2
    for place, ref in enumerate(refs):
        part = high ^ (place // per)
        if per == 2:
            block = mine ^ (place % 2)
            ref[...] = own_ref[part, block] + got_ref[part, block]
        else:
            ref[...] = own_ref[part] + got_ref[part]


def rows_kernel(steps, factor, count, *refs):
    in_refs, (u_ref, v_ref, f_ref, proj_ref) = refs[:count], refs[count : count + 4]
    wq_ref, wk_ref, wv_ref, out_ref, q_ref, g_ref = refs[count + 4 :]
    size = proj_ref.shape[1]
    high_g = g_ref.shape[0]
    me = lax.axis_index("sensor") % count
    for partner, ref in enumerate(in_refs):
        own = columns((me ^ partner) % count)
        g_ref[:, own] = ref[:high_g, :]
        q_ref[:, own] = ref[high_g:, :].astype(BF16)
    total = dot(q_ref[...], wq_ref[...])
    mask = head_mask(size, WIDE)
    rows = f_ref.shape[0] // steps
    back, grad_v = [], []
    for step in range(steps):
        part = slice(step * rows, (step + 1) * rows)
        matrix = g_ref[step * size : (step + 1) * size, :]
        spreads = [split(spread(m, mask)) for m in pieces(matrix)]
        values = [split(v) for v in pieces(v_ref[part, :])]
        feats = [split(f) for f in pieces(f_ref[part, :])]
        row = g_ref[steps * size + step : steps * size + step + 1, :]
        back.append(
            jnp.concatenate([dot3(v, m, NT) for v, m in zip(values, spreads)], -1) + row
        )
        grad_v.append(jnp.concatenate([dot3(f, m) for f, m in zip(feats, spreads)], -1))
    weighted = jnp.concatenate(back, 0) * f_ref[...]
    grad_k = feature_back(weighted, u_ref[...], all_heads(proj_ref), mask, head_ones(mask))
    total = total + dot((grad_k * factor).astype(BF16), wk_ref[...])
    grad_v = jnp.concatenate(grad_v, 0).astype(BF16)
    out_ref[...] = (total + dot(grad_v, wv_ref[...])).astype(BF16)


def final_kernel(scale, parts, *refs):
    in_refs, outs = refs[:parts], refs[parts:]
    total = in_refs[0][...]
    for ref in in_refs[1:]:
        total = total + ref[...]
    cols = outs[0].shape[1]
    for place, ref in enumerate(outs):
        ref[...] = total[:, place * cols : (place + 1) * cols] * scale


def call(kernel, name, outs, args, flops=0, smem=0, hbm=0, scratch=(), limit=20):
    size = lambda a: math.prod(a.shape) * a.dtype.itemsize
    rest = len(args) - smem - hbm
    return pl.pallas_call(
        kernel,
        name=name,
        out_shape=outs,
        in_specs=[SMEM] * smem + [pl.BlockSpec(memory_space=pl.ANY)] * hbm + [VMEM] * rest,
        out_specs=jax.tree.map(lambda _: VMEM, outs),
        scratch_shapes=list(scratch),
        cost_estimate=pl.CostEstimate(
            flops=flops,
            bytes_accessed=sum(size(a) for a in list(args) + list(jax.tree.leaves(outs))),
            transcendentals=0,
        ),
        compiler_params=pltpu.CompilerParams(vmem_limit_bytes=limit * 1024 * 1024),
    )(*args)


def shape(dims, kind=F32):
    return jax.ShapeDtypeStruct(dims, kind)


def swap(a, axis, bit):
    return lax.ppermute(a, axis, [(i, i ^ bit) for i in range(lax.axis_size(axis))])


def trade(parts, axis):
    got = {d: swap(parts[d], axis, d) for d in reversed(range(1, len(parts)))}
    return [parts[0]] + [got[d] for d in sorted(got)]


def gather_halves(top, low, axis):
    near_low, next_top = swap(low, axis, 2), swap(top, axis, 1)
    near_top, next_low = swap(top, axis, 2), swap(low, axis, 1)
    across_top, across_low = swap(next_top, axis, 2), swap(near_low, axis, 1)
    return (top, next_top, near_top, across_top), (low, next_low, near_low, across_low)


def far_sum(a, count):
    bit = count
    while bit * 2 < lax.axis_size("sensor"):
        a = a + swap(a, "sensor", bit)
        bit *= 2
    return a, swap(a, "sensor", bit)


def after(a, *others):
    return lax.optimization_barrier((a, others))[0]


def shards(inputs, cotangent, w_query, w_key, w_value, w_up, w_down, feature_proj, live_count):
    steps, sensors, width = inputs.shape
    heads, size, feats = feature_proj.shape
    hidden = w_up.shape[1]
    factor = size ** (-0.25)
    rows = steps * sensors
    devices = lax.axis_size("sensor")
    count = width // LANES
    quads = devices // count
    x = inputs.reshape(rows, width)
    cot = cotangent.reshape(rows, width)
    narrow = shape((rows, LANES))
    tall = shape((rows * count, LANES))
    packed = shape((steps * size + 8, LANES))
    product = 2 * rows * width * width
    kinds = lambda *arrays: [pltpu.VMEM(a.shape, a.dtype) for a in arrays]
    wide = pltpu.VMEM((rows, width), F32)

    top, low = call(
        widen_kernel,
        "widen",
        (shape((rows // 2 + 8, width)),) * 2,
        (live_count, x),
        smem=1,
    )
    tops, lows = gather_halves(top, low, "sensor")
    narrow_w = shape((width, LANES), BF16)
    own_query, own_key, own_value, proj, *local_keys = call(
        functools.partial(local_kernel, steps, factor, count),
        "local_keys",
        (narrow_w,) * 3 + (shape((size, LANES)),) + (shape((rows, width)),) * 3,
        (live_count, x, w_query, w_key, w_value, feature_proj),
        flops=3 * product,
        smem=1,
    )
    x_all, key, value, feat_key, summary = call(
        functools.partial(key_kernel, steps, factor, count),
        "keys",
        (shape((rows * count, width), BF16),) + (tall,) * 3 + (packed,),
        (*tops, *lows, own_key, own_value, proj),
        flops=3 * product,
    )
    turned = (x_all, w_query, w_key, w_value, w_up)
    x_turned, wq_turned, wk_turned, wv_turned, wu_turned = call(
        transpose_kernel, "transposes", tuple(shape(a.shape[::-1], BF16) for a in turned), turned
    )
    query, feat_query, grad_hidden = call(
        functools.partial(query_kernel, steps, factor, count),
        "queries",
        (tall, tall, shape((rows, hidden))),
        (live_count, x_all, cot, own_query, w_down, proj),
        flops=2 * product,
        smem=1,
    )
    summary = far_sum(summary, count)
    attended, inverse, *local_att = call(
        functools.partial(attend_kernel, steps, size, len(summary)),
        "attend",
        (tall, tall) + (narrow,) * count,
        (*summary, feat_query),
        flops=product,
    )
    local_grad = call(
        functools.partial(forward_kernel, count),
        "feed_forward",
        (narrow,) * count,
        (*trade(local_att, "sensor"), grad_hidden, w_up, wu_turned),
        flops=product,
        scratch=[wide],
    )
    grad_num, grad_den, grad_summary = call(
        functools.partial(grad_summary_kernel, steps, size, count),
        "grad_summary",
        (tall, tall, packed),
        (*trade(local_grad, "sensor"), attended, inverse, feat_query),
        flops=product,
        scratch=kinds(tall),
    )
    grad_summary = far_sum(grad_summary, count)
    grad_q = call(
        functools.partial(query_back_kernel, steps, factor, count, len(summary)),
        "query_back",
        shape(tall.shape, BF16),
        (*summary, grad_num, grad_den, feat_query, query, proj),
        flops=product,
    )
    tile = (width // devices, 3 * LANES)
    half = shape((2, quads, *tile))
    *messages, own_half, send_half = call(
        functools.partial(key_back_kernel, steps, factor, count, len(grad_summary), devices),
        "key_back",
        (shape((packed.shape[0] + rows, LANES)),) * count + (half, half),
        (*grad_summary, key, value, feat_key, proj, grad_q, x_turned),
        flops=4 * product,
        scratch=[pltpu.VMEM((2, *half.shape), F32)],
    )
    def turn(a, bit):
        pairs = []
        for k in range(quads):
            for q in range(count):
                for j in range(count):
                    target = (k ^ bit) * count + j
                    pairs.append(((k * count + q) * count + j, target * count + q))
        return lax.ppermute(a, ("sensor", "step"), pairs)

    got_half = swap(send_half, "step", 1)
    if quads == 2:
        kept, away, send_kept, send_away = call(
            functools.partial(core_kernel, count),
            "core_sums",
            (shape(tile),) * 4,
            (own_half, got_half),
        )
        away = away + swap(send_away, "step", 2)
        kept = kept + swap(send_kept, "step", 2)
        parts = (turn(away, 1), turn(kept, 0))
    else:
        kept, sent = call(
            functools.partial(core_kernel, count),
            "core_sums",
            (shape((quads, *tile)),) * 2,
            (own_half, got_half),
        )
        groups = [[q + count * k for k in range(quads)] for q in range(count)]
        blocks = lax.all_to_all(
            kept + swap(sent, "step", 2), "sensor", 0, 0, tiled=True, axis_index_groups=groups
        )
        parts = (turn(blocks.sum(0), 0),)
    messages = trade(messages, "sensor")
    scale = 1.0 / math.sqrt(rows * lax.axis_size("step") * devices)
    out = shape((width // devices, LANES))
    grad_in = call(
        functools.partial(rows_kernel, steps, factor, count),
        "input_rows",
        shape((rows, width), BF16),
        (*messages, *local_keys, feature_proj, wq_turned, wk_turned, wv_turned),
        flops=30 * product,
        scratch=[pltpu.VMEM((rows, width), BF16), pltpu.VMEM((packed.shape[0], width), F32)],
    )
    grads = call(
        functools.partial(final_kernel, scale, len(parts)),
        "weight_sums",
        (out,) * 3,
        (after(parts[0], grad_in), *parts[1:]),
    )
    return (grad_in.reshape(inputs.shape), *grads)


def solution(mesh):
    return jax.shard_map(
        shards,
        mesh=mesh,
        in_specs=(P("step", "sensor", None),) * 2 + (P(),) * 6 + (P("sensor"),),
        out_specs=(P("step", "sensor", None),) + (P("sensor", "step"),) * 3,
        check_vma=False,
    )
```

```python
import functools
import math

import jax
import jax.numpy as jnp
from jax import lax
from jax.experimental import pallas as pl
from jax.experimental.pallas import tpu as pltpu
from jax.sharding import PartitionSpec as P

F32 = jnp.float32
BF16 = jnp.bfloat16
NN = (((1,), (0,)), ((), ()))
NT = (((1,), (1,)), ((), ()))
TN = (((0,), (0,)), ((), ()))
VMEM = pl.BlockSpec(memory_space=pltpu.VMEM)
SMEM = pl.BlockSpec(memory_space=pltpu.SMEM)
LANES = 128
WIDE = 256


def dot(a, b, dims=NN):
    return lax.dot_general(a, b, dims, preferred_element_type=F32)


def split(x):
    high = x.astype(BF16)
    return high, (x - high.astype(F32)).astype(BF16)


def dot3(a, b, dims=NN):
    if a[0].shape[1] == LANES:
        axis = 1 if dims == NN else 0
        parts = [jnp.concatenate([b[0], b[1]], axis), jnp.concatenate([b[0], 0 * b[1]], axis)]
        out = dot(jnp.concatenate(a, 1), jnp.concatenate(parts, 1 - axis), dims)
        return out[:, :LANES] + out[:, LANES:]
    rows = a[0].shape[0]
    out = dot(jnp.concatenate(a, 0), b[0], dims)
    return out[:rows] + (out[rows:] + dot(a[0], b[1], dims))


def dot2(a, b, dims=NN):
    rows = a[0].shape[0]
    out = dot(jnp.concatenate(a, 0), b, dims)
    return out[:rows] + out[rows:]


def head_mask(size, width):
    rows = lax.broadcasted_iota(jnp.int32, (width, width), 0) // size
    cols = lax.broadcasted_iota(jnp.int32, (width, width), 1) // size
    return rows == cols


def head_ones(mask):
    return jnp.where(mask, 1.0, 0.0).astype(BF16)


def spread(x, mask):
    return jnp.where(mask, jnp.concatenate([x] * (x.shape[1] // x.shape[0]), 0), 0.0)


def gather_diagonal(x, size):
    head = lax.broadcasted_iota(jnp.int32, (size, x.shape[1]), 1) // size
    out = x[:size]
    for g in range(1, x.shape[1] // size):
        out = jnp.where(head == g, x[g * size : (g + 1) * size], out)
    return out


def head_sums(x, ones):
    high, low = split(x)
    if x.shape[1] == LANES:
        return dot(jnp.concatenate([high, low], 1), jnp.concatenate([ones, ones], 0))
    return dot2((high, low), ones)


def pieces(x, width=WIDE):
    return [x[:, h : h + width] for h in range(0, x.shape[1], width)]


def projection(proj_ref, heads=None, width=WIDE):
    heads = range(proj_ref.shape[0]) if heads is None else heads
    blocks = [proj_ref[h] for h in heads]
    per = width // proj_ref.shape[2]
    return [jnp.concatenate(blocks[g : g + per], -1) for g in range(0, len(blocks), per)]


def feature_map(scaled, proj, mask, ones, feats):
    out = []
    for u, p in zip(pieces(scaled, mask.shape[0]), proj):
        projected = dot3(split(u), split(spread(p, mask)))
        out.append(jnp.exp(projected - 0.5 * head_sums(u * u, ones)) * feats ** (-0.5))
    return jnp.concatenate(out, -1)


def feature_back(weighted, scaled, proj, mask, ones):
    out = []
    width = mask.shape[0]
    for w, u, p in zip(pieces(weighted, width), pieces(scaled, width), proj):
        back = dot3(split(w), split(spread(p, mask)), NT)
        out.append(back - u * head_sums(w, ones))
    return jnp.concatenate(out, -1)


def store_summary(out_ref, matrices, sums):
    size = matrices[0].shape[0]
    base = size * len(matrices)
    out_ref[base:, :] = jnp.zeros((out_ref.shape[0] - base, LANES), F32)
    for step, (matrix, row) in enumerate(zip(matrices, sums)):
        out_ref[step * size : (step + 1) * size, :] = matrix
        out_ref[base + step : base + step + 1, :] = row


def load_summary(refs, steps, size):
    total = refs[0][...]
    for ref in refs[1:]:
        total = total + ref[...]
    base = steps * size
    return [
        (total[step * size : (step + 1) * size], total[base + step : base + step + 1])
        for step in range(steps)
    ]


def outer_sums(a, b, size):
    out = dot(jnp.concatenate(split(a), 1), jnp.concatenate(split(b), 1), TN)
    whole = out[:LANES, :LANES] + (out[:LANES, LANES:] + out[LANES:, :LANES])
    return gather_diagonal(whole, size)


def summaries(a, b, weighted, steps, size):
    high = a.shape[0] // steps
    parts = [slice(step * high, (step + 1) * high) for step in range(steps)]
    matrices = [outer_sums(a[p], b[p], size) for p in parts]
    return matrices, [jnp.sum(weighted[p], 0, keepdims=True) for p in parts]


def columns(group):
    return pl.ds(pl.multiple_of(group * LANES, LANES), LANES)


def send_columns(sources, refs, me):
    for partner, ref in enumerate(refs):
        own = columns((me ^ partner) % len(refs))
        for place, source in enumerate(sources):
            rows = source.shape[0]
            ref[:rows, place * LANES : (place + 1) * LANES] = source[:, own]


def place_rows(target, refs, steps, column=0):
    rows = target.shape[0] // (steps * len(refs))
    lanes = slice(column * LANES, column * LANES + target.shape[1])
    for partner, ref in enumerate(refs):
        for step in range(steps):
            start = (step * len(refs) + partner) * rows
            target[start : start + rows, :] = ref[step * rows : (step + 1) * rows, lanes].astype(
                target.dtype
            )


def take_rows(values, partner, count, steps):
    rows = values.shape[0] // (steps * count)
    starts = [(step * count + partner) * rows for step in range(steps)]
    return jnp.concatenate([values[s : s + rows] for s in starts], 0)


def widen_kernel(live_ref, x_ref, top_ref, low_ref):
    half = x_ref.shape[0] // 2
    for ref, base in ((top_ref, 0), (low_ref, half)):
        ref[:half, :] = x_ref[base : base + half].astype(F32)
        ref[half:, :] = jnp.full((ref.shape[0] - half, ref.shape[1]), live_ref[0]).astype(F32)


def own_columns(count):
    return columns(lax.axis_index("sensor") % count)


def own_heads(proj_ref, count):
    per = proj_ref.shape[0] // count
    start = (lax.axis_index("sensor") % count) * per
    return jnp.concatenate([proj_ref[start + h] for h in range(per)], -1)


def all_heads(proj_ref):
    per = WIDE // proj_ref.shape[2]
    return [
        jnp.concatenate([proj_ref[g + h] for h in range(per)], -1)
        for g in range(0, proj_ref.shape[0], per)
    ]


def local_kernel(steps, factor, count, live_ref, x_ref, wq_ref, wk_ref, wv_ref, proj_ref, *refs):
    oq_ref, ok_ref, ov_ref, op_ref, u_ref, v_ref, f_ref = refs
    own = own_columns(count)
    oq_ref[...] = wq_ref[:, own]
    ok_ref[...] = wk_ref[:, own]
    ov_ref[...] = wv_ref[:, own]
    op_ref[...] = own_heads(proj_ref, count)
    mask = head_mask(proj_ref.shape[1], WIDE)
    x = x_ref[...]
    scaled = dot(x, wk_ref[...]) * factor
    u_ref[...] = scaled
    v_ref[...] = dot(x, wv_ref[...])
    feat = feature_map(scaled, all_heads(proj_ref), mask, head_ones(mask), proj_ref.shape[2])
    place = lax.broadcasted_iota(jnp.int32, feat.shape, 0) % (feat.shape[0] // steps)
    f_ref[...] = jnp.where(place < live_ref[0], feat, 0.0)


def key_kernel(steps, factor, count, *refs):
    tops, lows = refs[:count], refs[count : 2 * count]
    wk_ref, wv_ref, proj_ref, x_ref, u_ref, v_ref, f_ref, s_ref = refs[2 * count :]
    size = proj_ref.shape[0]
    mask = head_mask(size, LANES)
    rows = x_ref.shape[0] // (steps * count)
    half = steps * rows // 2
    piece = math.gcd(half, rows)
    for partner in range(count):
        for ref, base in ((tops[partner], 0), (lows[partner], half)):
            for row in range(0, half, piece):
                step, inner = divmod(base + row, rows)
                start = (step * count + partner) * rows + inner
                x_ref[start : start + piece, :] = ref[row : row + piece, :].astype(BF16)
    x = x_ref[...]
    scaled = dot(x, wk_ref[...]) * factor
    values = dot(x, wv_ref[...])
    u_ref[...] = scaled
    v_ref[...] = values
    feat = feature_map(scaled, [proj_ref[...]], mask, head_ones(mask), size)
    place = lax.broadcasted_iota(jnp.int32, (rows, LANES), 0).astype(F32)
    keep = jnp.concatenate([place < ref[half : half + 1, :LANES] for ref in tops] * steps, 0)
    feat = jnp.where(keep, feat, 0.0)
    f_ref[...] = feat
    store_summary(s_ref, *summaries(feat, values, feat, steps, size))


def transpose_kernel(*refs):
    half = len(refs) // 2
    for source, target in zip(refs[:half], refs[half:]):
        target[...] = source[...].T


def query_kernel(steps, factor, count, live_ref, x_ref, cot_ref, wq_ref, wd_ref, proj_ref, u_ref, f_ref, gh_ref):
    size = proj_ref.shape[0]
    mask = head_mask(size, LANES)
    scaled = dot(x_ref[...], wq_ref[...]) * factor
    u_ref[...] = scaled
    f_ref[...] = feature_map(
        scaled, [proj_ref[...]], mask, head_ones(mask), size
    )
    hidden = dot(cot_ref[...], wd_ref[...], NT)
    place = lax.broadcasted_iota(jnp.int32, hidden.shape, 0) % (hidden.shape[0] // steps)
    gh_ref[...] = jnp.where(place < live_ref[0], hidden, 0.0)


def attend_kernel(steps, size, parts, *refs):
    s_refs, (f_ref, att_ref, inv_ref), out_refs = refs[:parts], refs[parts : parts + 3], refs[parts + 3 :]
    mask = head_mask(size, LANES)
    feat = f_ref[...]
    high = feat.shape[0] // steps
    numer, weighted = [], []
    for step, (matrix, row) in enumerate(load_summary(s_refs, steps, size)):
        part = feat[step * high : (step + 1) * high]
        numer.append(dot3(split(part), split(spread(matrix, mask))))
        weighted.append(part * row)
    inverse = 1.0 / head_sums(jnp.concatenate(weighted, 0), head_ones(mask))
    attended = jnp.concatenate(numer, 0) * inverse
    att_ref[...] = attended
    inv_ref[...] = inverse
    for partner, ref in enumerate(out_refs):
        ref[...] = take_rows(attended, partner, len(out_refs), steps)


def forward_kernel(count, *refs):
    in_refs, (gh_ref, wu_ref, wt_ref) = refs[:count], refs[count : count + 3]
    out_refs, scratch = refs[count + 3 : -1], refs[-1]
    me = lax.axis_index("sensor") % count
    for partner, ref in enumerate(in_refs):
        scratch[:, columns((me ^ partner) % count)] = ref[...]
    attended = scratch[...]
    scale = lax.rsqrt(jnp.mean(attended * attended, -1, keepdims=True) + 1e-06)
    normed = attended * scale
    pre = dot(normed.astype(BF16), wu_ref[...])
    c = math.sqrt(2.0 / math.pi)
    square = pre * pre
    t = jnp.tanh(c * pre * (1.0 + 0.044715 * square))
    slope = 0.5 * (1.0 + t) + 0.5 * pre * (1.0 - t * t) * (c * (1.0 + 3 * 0.044715 * square))
    grad_pre = (gh_ref[...] * slope).astype(BF16)
    grad_normed = dot(grad_pre, wt_ref[...])
    scratch[...] = (
        grad_normed - normed * jnp.mean(grad_normed * normed, -1, keepdims=True)
    ) * scale
    send_columns([scratch], out_refs, me)


def grad_summary_kernel(steps, size, count, *refs):
    in_refs, (att_ref, inv_ref, f_ref) = refs[:count], refs[count : count + 3]
    num_ref, den_ref, g_ref, scratch = refs[count + 3 :]
    place_rows(scratch, in_refs, steps)
    mask = head_mask(size, LANES)
    grad_att = scratch[...]
    inverse = inv_ref[...]
    feat = f_ref[...]
    grad_num = grad_att * inverse
    grad_den = -head_sums(grad_att * att_ref[...], head_ones(mask)) * inverse
    num_ref[...] = grad_num
    den_ref[...] = grad_den
    store_summary(g_ref, *summaries(feat, grad_num, feat * grad_den, steps, size))


def query_back_kernel(steps, factor, count, parts, *refs):
    s_refs, (num_ref, den_ref, f_ref, u_ref, proj_ref, g_ref) = refs[:parts], refs[parts:]
    size = proj_ref.shape[0]
    mask = head_mask(size, LANES)
    high = f_ref.shape[0] // steps
    out = []
    for step, (matrix, row) in enumerate(load_summary(s_refs, steps, size)):
        part = slice(step * high, (step + 1) * high)
        back = dot3(split(num_ref[part, :]), split(spread(matrix, mask)), NT)
        out.append(back + den_ref[part, :] * row)
    weighted = jnp.concatenate(out, 0) * f_ref[...]
    grad = feature_back(
        weighted, u_ref[...], [proj_ref[...]], mask, head_ones(mask)
    )
    g_ref[...] = (grad * factor).astype(BF16)


def key_back_kernel(steps, factor, count, parts, devices, *refs):
    g_refs, (u_ref, v_ref, f_ref, proj_ref, gq_ref) = refs[:parts], refs[parts : parts + 5]
    x_all, rest = refs[parts + 5], refs[parts + 6 :]
    back_refs, (keep_ref, send_ref, p_ref) = rest[:count], rest[count:]
    size = proj_ref.shape[0]
    mask = head_mask(size, LANES)
    high = f_ref.shape[0] // steps
    total = g_refs[0][...]
    for ref in g_refs[1:]:
        total = total + ref[...]
    high_g = total.shape[0]
    for partner, ref in enumerate(back_refs):
        ref[:high_g, :] = total
        ref[high_g:, :] = take_rows(gq_ref[...], partner, count, steps).astype(F32)
    back, grad_v = [], []
    for step, (matrix, row) in enumerate(load_summary(back_refs[:1], steps, size)):
        part = slice(step * high, (step + 1) * high)
        matrix = split(spread(matrix, mask))
        back.append(dot3(split(v_ref[part, :]), matrix, NT) + row)
        grad_v.append(dot3(split(f_ref[part, :]), matrix))
    weighted = jnp.concatenate(back, 0) * f_ref[...]
    grad_k = feature_back(
        weighted, u_ref[...], [proj_ref[...]], mask, head_ones(mask)
    )
    grad = jnp.concatenate([grad_k * factor, jnp.concatenate(grad_v, 0)], -1).astype(BF16)
    total = dot(x_all[...], jnp.concatenate([gq_ref[...], grad], -1))
    block = total.shape[0] // devices
    for place in range(devices):
        p_ref[place % 2, place // 2 % 2, place // 4] = total[place * block : (place + 1) * block]
    low = lax.axis_index("step") % 2
    keep_ref[...] = p_ref[low]
    send_ref[...] = p_ref[1 - low]


def core_kernel(count, own_ref, got_ref, *refs):
    high = lax.axis_index("step") // 2 % 2
    mine = lax.axis_index("sensor") // count
    per = len(refs) // 2
    for place, ref in enumerate(refs):
        part = high ^ (place // per)
        if per == 2:
            block = mine ^ (place % 2)
            ref[...] = own_ref[part, block] + got_ref[part, block]
        else:
            ref[...] = own_ref[part] + got_ref[part]


def rows_kernel(steps, factor, count, *refs):
    in_refs, (u_ref, v_ref, f_ref, proj_ref) = refs[:count], refs[count : count + 4]
    wq_ref, wk_ref, wv_ref, out_ref, q_ref, g_ref = refs[count + 4 :]
    size = proj_ref.shape[1]
    high_g = g_ref.shape[0]
    me = lax.axis_index("sensor") % count
    for partner, ref in enumerate(reversed(in_refs)):
        own = columns((me ^ partner) % count)
        g_ref[:, own] = ref[:high_g, :]
        q_ref[:, own] = ref[high_g:, :].astype(BF16)
    total = dot(q_ref[...], wq_ref[...])
    mask = head_mask(size, WIDE)
    rows = f_ref.shape[0] // steps
    back, grad_v = [], []
    for step in range(steps):
        part = slice(step * rows, (step + 1) * rows)
        matrix = g_ref[step * size : (step + 1) * size, :]
        spreads = [split(spread(m, mask)) for m in pieces(matrix)]
        values = [split(v) for v in pieces(v_ref[part, :])]
        feats = [split(f) for f in pieces(f_ref[part, :])]
        row = g_ref[steps * size + step : steps * size + step + 1, :]
        back.append(
            jnp.concatenate([dot3(v, m, NT) for v, m in zip(values, spreads)], -1) + row
        )
        grad_v.append(jnp.concatenate([dot3(f, m) for f, m in zip(feats, spreads)], -1))
    weighted = jnp.concatenate(back, 0) * f_ref[...]
    grad_k = feature_back(weighted, u_ref[...], all_heads(proj_ref), mask, head_ones(mask))
    total = total + dot((grad_k * factor).astype(BF16), wk_ref[...])
    grad_v = jnp.concatenate(grad_v, 0).astype(BF16)
    out_ref[...] = (total + dot(grad_v, wv_ref[...])).astype(BF16)


def final_kernel(scale, parts, *refs):
    in_refs, outs = refs[:parts], refs[parts:]
    total = in_refs[0][...]
    for ref in in_refs[1:]:
        total = total + ref[...]
    cols = outs[0].shape[1]
    for place, ref in enumerate(outs):
        ref[...] = total[:, place * cols : (place + 1) * cols] * scale


def call(kernel, name, outs, args, flops=0, smem=0, hbm=0, scratch=(), limit=20):
    size = lambda a: math.prod(a.shape) * a.dtype.itemsize
    rest = len(args) - smem - hbm
    return pl.pallas_call(
        kernel,
        name=name,
        out_shape=outs,
        in_specs=[SMEM] * smem + [pl.BlockSpec(memory_space=pl.ANY)] * hbm + [VMEM] * rest,
        out_specs=jax.tree.map(lambda _: VMEM, outs),
        scratch_shapes=list(scratch),
        cost_estimate=pl.CostEstimate(
            flops=flops,
            bytes_accessed=sum(size(a) for a in list(args) + list(jax.tree.leaves(outs))),
            transcendentals=0,
        ),
        compiler_params=pltpu.CompilerParams(vmem_limit_bytes=limit * 1024 * 1024),
    )(*args)


def shape(dims, kind=F32):
    return jax.ShapeDtypeStruct(dims, kind)


def swap(a, axis, bit):
    return lax.ppermute(a, axis, [(i, i ^ bit) for i in range(lax.axis_size(axis))])


def trade(parts, axis, together=True):
    order = [len(parts) - 1, *range(1, len(parts) - 1)]
    got = [swap(parts[d], axis, d) for d in order]
    if together:
        got = lax.optimization_barrier(got)
    return [parts[0], *got[1:], got[0]]


def gather_halves(top, low, axis):
    near_low, next_top = swap(low, axis, 2), swap(top, axis, 1)
    near_top, next_low = swap(top, axis, 2), swap(low, axis, 1)
    across_top, across_low = swap(next_top, axis, 2), swap(near_low, axis, 1)
    return (top, next_top, near_top, across_top), (low, next_low, near_low, across_low)


def far_sum(a, count):
    bit = count
    while bit * 2 < lax.axis_size("sensor"):
        a = a + swap(a, "sensor", bit)
        bit *= 2
    return a, swap(a, "sensor", bit)


def after(a, *others):
    return lax.optimization_barrier((a, others))[0]


def shards(inputs, cotangent, w_query, w_key, w_value, w_up, w_down, feature_proj, live_count):
    steps, sensors, width = inputs.shape
    heads, size, feats = feature_proj.shape
    hidden = w_up.shape[1]
    factor = size ** (-0.25)
    rows = steps * sensors
    devices = lax.axis_size("sensor")
    count = width // LANES
    quads = devices // count
    x = inputs.reshape(rows, width)
    cot = cotangent.reshape(rows, width)
    narrow = shape((rows, LANES))
    tall = shape((rows * count, LANES))
    packed = shape((steps * size + 8, LANES))
    product = 2 * rows * width * width
    kinds = lambda *arrays: [pltpu.VMEM(a.shape, a.dtype) for a in arrays]
    wide = pltpu.VMEM((rows, width), F32)

    top, low = call(
        widen_kernel,
        "widen",
        (shape((rows // 2 + 8, width)),) * 2,
        (live_count, x),
        smem=1,
    )
    tops, lows = gather_halves(top, low, "sensor")
    narrow_w = shape((width, LANES), BF16)
    own_query, own_key, own_value, proj, *local_keys = call(
        functools.partial(local_kernel, steps, factor, count),
        "local_keys",
        (narrow_w,) * 3 + (shape((size, LANES)),) + (shape((rows, width)),) * 3,
        (live_count, x, w_query, w_key, w_value, feature_proj),
        flops=3 * product,
        smem=1,
    )
    x_all, key, value, feat_key, summary = call(
        functools.partial(key_kernel, steps, factor, count),
        "keys",
        (shape((rows * count, width), BF16),) + (tall,) * 3 + (packed,),
        (*tops, *lows, own_key, own_value, proj),
        flops=3 * product,
    )
    turned = (x_all, w_query, w_key, w_value, w_up)
    x_turned, wq_turned, wk_turned, wv_turned, wu_turned = call(
        transpose_kernel, "transposes", tuple(shape(a.shape[::-1], BF16) for a in turned), turned
    )
    query, feat_query, grad_hidden = call(
        functools.partial(query_kernel, steps, factor, count),
        "queries",
        (tall, tall, shape((rows, hidden))),
        (live_count, x_all, cot, own_query, w_down, proj),
        flops=2 * product,
        smem=1,
    )
    summary = far_sum(summary, count)
    attended, inverse, *local_att = call(
        functools.partial(attend_kernel, steps, size, len(summary)),
        "attend",
        (tall, tall) + (narrow,) * count,
        (*summary, feat_query),
        flops=product,
    )
    local_grad = call(
        functools.partial(forward_kernel, count),
        "feed_forward",
        (narrow,) * count,
        (*trade(local_att, "sensor"), grad_hidden, w_up, wu_turned),
        flops=product,
        scratch=[wide],
    )
    grad_num, grad_den, grad_summary = call(
        functools.partial(grad_summary_kernel, steps, size, count),
        "grad_summary",
        (tall, tall, packed),
        (*trade(local_grad, "sensor"), attended, inverse, feat_query),
        flops=product,
        scratch=kinds(tall),
    )
    grad_summary = far_sum(grad_summary, count)
    grad_q = call(
        functools.partial(query_back_kernel, steps, factor, count, len(summary)),
        "query_back",
        shape(tall.shape, BF16),
        (*summary, grad_num, grad_den, feat_query, query, proj),
        flops=product,
    )
    tile = (width // devices, 3 * LANES)
    half = shape((2, quads, *tile))
    *messages, own_half, send_half = call(
        functools.partial(key_back_kernel, steps, factor, count, len(grad_summary), devices),
        "key_back",
        (shape((packed.shape[0] + rows, LANES)),) * count + (half, half),
        (*grad_summary, key, value, feat_key, proj, grad_q, x_turned),
        flops=4 * product,
        scratch=[pltpu.VMEM((2, *half.shape), F32)],
    )
    def turn(a, bit, flip=0):
        pairs = []
        for k in range(quads):
            for q in range(count):
                for j in range(count):
                    target = (k ^ bit) * count + (j ^ flip)
                    pairs.append(((k * count + q) * count + j, target * count + q))
        return lax.ppermute(a, ("sensor", "step"), pairs)

    got_half = swap(send_half, "step", 1)
    if quads == 2:
        kept, away, send_kept, send_away = call(
            functools.partial(core_kernel, count),
            "core_sums",
            (shape(tile),) * 4,
            (own_half, got_half),
        )
        away = away + swap(send_away, "step", 2)
        parts = (turn(away, 1), turn(send_kept, 0, 2), turn(after(kept, away), 0))
    else:
        kept, sent = call(
            functools.partial(core_kernel, count),
            "core_sums",
            (shape((quads, *tile)),) * 2,
            (own_half, got_half),
        )
        groups = [[q + count * k for k in range(quads)] for q in range(count)]
        blocks = lax.all_to_all(
            kept + swap(sent, "step", 2), "sensor", 0, 0, tiled=True, axis_index_groups=groups
        )
        parts = (turn(blocks.sum(0), 0),)
    messages = trade(messages, "sensor", False)
    scale = 1.0 / math.sqrt(rows * lax.axis_size("step") * devices)
    out = shape((width // devices, LANES))
    grad_in = call(
        functools.partial(rows_kernel, steps, factor, count),
        "input_rows",
        shape((rows, width), BF16),
        (*messages[::-1], *local_keys, feature_proj, wq_turned, wk_turned, wv_turned),
        flops=30 * product,
        scratch=[pltpu.VMEM((rows, width), BF16), pltpu.VMEM((packed.shape[0], width), F32)],
    )
    grads = call(
        functools.partial(final_kernel, scale, len(parts)),
        "weight_sums",
        (out,) * 3,
        (after(parts[0], grad_in), *parts[1:]),
    )
    return (grad_in.reshape(inputs.shape), *grads)


def solution(mesh):
    return jax.shard_map(
        shards,
        mesh=mesh,
        in_specs=(P("step", "sensor", None),) * 2 + (P(),) * 6 + (P("sensor"),),
        out_specs=(P("step", "sensor", None),) + (P("sensor", "step"),) * 3,
        check_vma=False,
    )
```

```python
import functools
import math

import jax
import jax.numpy as jnp
from jax import lax
from jax.experimental import pallas as pl
from jax.experimental.pallas import tpu as pltpu
from jax.sharding import PartitionSpec as P

F32 = jnp.float32
BF16 = jnp.bfloat16
NN = (((1,), (0,)), ((), ()))
NT = (((1,), (1,)), ((), ()))
TN = (((0,), (0,)), ((), ()))
VMEM = pl.BlockSpec(memory_space=pltpu.VMEM)
SMEM = pl.BlockSpec(memory_space=pltpu.SMEM)
LANES = 128
WIDE = 256


def dot(a, b, dims=NN):
    return lax.dot_general(a, b, dims, preferred_element_type=F32)


def split(x):
    high = x.astype(BF16)
    return high, (x - high.astype(F32)).astype(BF16)


def dot3(a, b, dims=NN):
    if a[0].shape[1] == LANES:
        axis = 1 if dims == NN else 0
        parts = [jnp.concatenate([b[0], b[1]], axis), jnp.concatenate([b[0], 0 * b[1]], axis)]
        out = dot(jnp.concatenate(a, 1), jnp.concatenate(parts, 1 - axis), dims)
        return out[:, :LANES] + out[:, LANES:]
    rows = a[0].shape[0]
    out = dot(jnp.concatenate(a, 0), b[0], dims)
    return out[:rows] + (out[rows:] + dot(a[0], b[1], dims))


def dot2(a, b, dims=NN):
    rows = a[0].shape[0]
    out = dot(jnp.concatenate(a, 0), b, dims)
    return out[:rows] + out[rows:]


def head_mask(size, width):
    rows = lax.broadcasted_iota(jnp.int32, (width, width), 0) // size
    cols = lax.broadcasted_iota(jnp.int32, (width, width), 1) // size
    return rows == cols


def head_ones(mask):
    return jnp.where(mask, 1.0, 0.0).astype(BF16)


def spread(x, mask):
    return jnp.where(mask, jnp.concatenate([x] * (x.shape[1] // x.shape[0]), 0), 0.0)


def gather_diagonal(x, size):
    head = lax.broadcasted_iota(jnp.int32, (size, x.shape[1]), 1) // size
    out = x[:size]
    for g in range(1, x.shape[1] // size):
        out = jnp.where(head == g, x[g * size : (g + 1) * size], out)
    return out


def head_sums(x, ones):
    high, low = split(x)
    if x.shape[1] == LANES:
        return dot(jnp.concatenate([high, low], 1), jnp.concatenate([ones, ones], 0))
    return dot2((high, low), ones)


def pieces(x, width=WIDE):
    return [x[:, h : h + width] for h in range(0, x.shape[1], width)]


def projection(proj_ref, heads=None, width=WIDE):
    heads = range(proj_ref.shape[0]) if heads is None else heads
    blocks = [proj_ref[h] for h in heads]
    per = width // proj_ref.shape[2]
    return [jnp.concatenate(blocks[g : g + per], -1) for g in range(0, len(blocks), per)]


def feature_map(scaled, proj, mask, ones, feats):
    out = []
    for u, p in zip(pieces(scaled, mask.shape[0]), proj):
        projected = dot3(split(u), split(spread(p, mask)))
        out.append(jnp.exp(projected - 0.5 * head_sums(u * u, ones)) * feats ** (-0.5))
    return jnp.concatenate(out, -1)


def feature_back(weighted, scaled, proj, mask, ones):
    out = []
    width = mask.shape[0]
    for w, u, p in zip(pieces(weighted, width), pieces(scaled, width), proj):
        back = dot3(split(w), split(spread(p, mask)), NT)
        out.append(back - u * head_sums(w, ones))
    return jnp.concatenate(out, -1)


def store_summary(out_ref, matrices, sums):
    size = matrices[0].shape[0]
    base = size * len(matrices)
    out_ref[base:, :] = jnp.zeros((out_ref.shape[0] - base, LANES), F32)
    for step, (matrix, row) in enumerate(zip(matrices, sums)):
        out_ref[step * size : (step + 1) * size, :] = matrix
        out_ref[base + step : base + step + 1, :] = row


def load_summary(refs, steps, size):
    total = refs[0][...]
    for ref in refs[1:]:
        total = total + ref[...]
    base = steps * size
    return [
        (total[step * size : (step + 1) * size], total[base + step : base + step + 1])
        for step in range(steps)
    ]


def outer_sums(a, b, size):
    out = dot(jnp.concatenate(split(a), 1), jnp.concatenate(split(b), 1), TN)
    whole = out[:LANES, :LANES] + (out[:LANES, LANES:] + out[LANES:, :LANES])
    return gather_diagonal(whole, size)


def summaries(a, b, weighted, steps, size):
    high = a.shape[0] // steps
    parts = [slice(step * high, (step + 1) * high) for step in range(steps)]
    matrices = [outer_sums(a[p], b[p], size) for p in parts]
    return matrices, [jnp.sum(weighted[p], 0, keepdims=True) for p in parts]


def columns(group):
    return pl.ds(pl.multiple_of(group * LANES, LANES), LANES)


def send_columns(sources, refs, me):
    for partner, ref in enumerate(refs):
        own = columns((me ^ partner) % len(refs))
        for place, source in enumerate(sources):
            rows = source.shape[0]
            ref[:rows, place * LANES : (place + 1) * LANES] = source[:, own]


def place_rows(target, refs, steps, column=0):
    rows = target.shape[0] // (steps * len(refs))
    lanes = slice(column * LANES, column * LANES + target.shape[1])
    for partner, ref in enumerate(refs):
        for step in range(steps):
            start = (step * len(refs) + partner) * rows
            target[start : start + rows, :] = ref[step * rows : (step + 1) * rows, lanes].astype(
                target.dtype
            )


def take_rows(values, partner, count, steps):
    rows = values.shape[0] // (steps * count)
    starts = [(step * count + partner) * rows for step in range(steps)]
    return jnp.concatenate([values[s : s + rows] for s in starts], 0)


def widen_kernel(live_ref, x_ref, top_ref, low_ref):
    half = x_ref.shape[0] // 2
    for ref, base in ((top_ref, 0), (low_ref, half)):
        ref[:half, :] = x_ref[base : base + half].astype(F32)
        ref[half:, :] = jnp.full((ref.shape[0] - half, ref.shape[1]), live_ref[0]).astype(F32)


def own_columns(count):
    return columns(lax.axis_index("sensor") % count)


def own_heads(proj_ref, count):
    per = proj_ref.shape[0] // count
    start = (lax.axis_index("sensor") % count) * per
    return jnp.concatenate([proj_ref[start + h] for h in range(per)], -1)


def all_heads(proj_ref):
    per = WIDE // proj_ref.shape[2]
    return [
        jnp.concatenate([proj_ref[g + h] for h in range(per)], -1)
        for g in range(0, proj_ref.shape[0], per)
    ]


def local_kernel(steps, factor, count, live_ref, x_ref, wq_ref, wk_ref, wv_ref, proj_ref, *refs):
    oq_ref, ok_ref, ov_ref, op_ref, uq_ref, fq_ref, u_ref, v_ref, f_ref = refs
    own = own_columns(count)
    oq_ref[...] = wq_ref[:, own]
    ok_ref[...] = wk_ref[:, own]
    ov_ref[...] = wv_ref[:, own]
    op_ref[...] = own_heads(proj_ref, count)
    mask = head_mask(proj_ref.shape[1], WIDE)
    x = x_ref[...]
    proj = all_heads(proj_ref)
    scaled = dot(x, wq_ref[...]) * factor
    uq_ref[...] = scaled
    fq_ref[...] = feature_map(scaled, proj, mask, head_ones(mask), proj_ref.shape[2])
    scaled = dot(x, wk_ref[...]) * factor
    u_ref[...] = scaled
    v_ref[...] = dot(x, wv_ref[...])
    feat = feature_map(scaled, proj, mask, head_ones(mask), proj_ref.shape[2])
    place = lax.broadcasted_iota(jnp.int32, feat.shape, 0) % (feat.shape[0] // steps)
    f_ref[...] = jnp.where(place < live_ref[0], feat, 0.0)


def key_kernel(steps, factor, count, *refs):
    tops, lows = refs[:count], refs[count : 2 * count]
    wk_ref, wv_ref, proj_ref, x_ref, u_ref, v_ref, f_ref, s_ref = refs[2 * count :]
    size = proj_ref.shape[0]
    mask = head_mask(size, LANES)
    rows = x_ref.shape[0] // (steps * count)
    half = steps * rows // 2
    piece = math.gcd(half, rows)
    for partner in range(count):
        for ref, base in ((tops[partner], 0), (lows[partner], half)):
            for row in range(0, half, piece):
                step, inner = divmod(base + row, rows)
                start = (step * count + partner) * rows + inner
                x_ref[start : start + piece, :] = ref[row : row + piece, :].astype(BF16)
    x = x_ref[...]
    scaled = dot(x, wk_ref[...]) * factor
    values = dot(x, wv_ref[...])
    u_ref[...] = scaled
    v_ref[...] = values
    feat = feature_map(scaled, [proj_ref[...]], mask, head_ones(mask), size)
    place = lax.broadcasted_iota(jnp.int32, (rows, LANES), 0).astype(F32)
    keep = jnp.concatenate([place < ref[half : half + 1, :LANES] for ref in tops] * steps, 0)
    feat = jnp.where(keep, feat, 0.0)
    f_ref[...] = feat
    store_summary(s_ref, *summaries(feat, values, feat, steps, size))


def transpose_kernel(*refs):
    half = len(refs) // 2
    for source, target in zip(refs[:half], refs[half:]):
        target[...] = source[...].T


def query_kernel(steps, factor, count, live_ref, x_ref, cot_ref, wq_ref, wd_ref, proj_ref, u_ref, f_ref, gh_ref):
    size = proj_ref.shape[0]
    mask = head_mask(size, LANES)
    scaled = dot(x_ref[...], wq_ref[...]) * factor
    u_ref[...] = scaled
    f_ref[...] = feature_map(
        scaled, [proj_ref[...]], mask, head_ones(mask), size
    )
    hidden = dot(cot_ref[...], wd_ref[...], NT)
    place = lax.broadcasted_iota(jnp.int32, hidden.shape, 0) % (hidden.shape[0] // steps)
    gh_ref[...] = jnp.where(place < live_ref[0], hidden, 0.0)


def attend_kernel(steps, size, parts, *refs):
    s_refs, (f_ref, att_ref, inv_ref, s_ref) = refs[:parts], refs[parts : parts + 4]
    out_refs = refs[parts + 4 :]
    total = s_refs[0][...]
    for ref in s_refs[1:]:
        total = total + ref[...]
    s_ref[...] = total
    mask = head_mask(size, LANES)
    feat = f_ref[...]
    high = feat.shape[0] // steps
    numer, weighted = [], []
    for step, (matrix, row) in enumerate(load_summary([s_ref], steps, size)):
        part = feat[step * high : (step + 1) * high]
        numer.append(dot3(split(part), split(spread(matrix, mask))))
        weighted.append(part * row)
    inverse = 1.0 / head_sums(jnp.concatenate(weighted, 0), head_ones(mask))
    attended = jnp.concatenate(numer, 0) * inverse
    att_ref[...] = attended
    inv_ref[...] = inverse
    for partner, ref in enumerate(out_refs):
        ref[...] = take_rows(attended, partner, len(out_refs), steps)


def forward_kernel(count, *refs):
    in_refs, (gh_ref, wu_ref, wt_ref) = refs[:count], refs[count : count + 3]
    att_ref, grad_ref, out_refs = refs[count + 3], refs[count + 4], refs[count + 5 :]
    me = lax.axis_index("sensor") % count
    for partner, ref in enumerate(in_refs):
        att_ref[:, columns((me ^ partner) % count)] = ref[...]
    attended = att_ref[...]
    scale = lax.rsqrt(jnp.mean(attended * attended, -1, keepdims=True) + 1e-06)
    normed = attended * scale
    pre = dot(normed.astype(BF16), wu_ref[...])
    c = math.sqrt(2.0 / math.pi)
    square = pre * pre
    t = jnp.tanh(c * pre * (1.0 + 0.044715 * square))
    slope = 0.5 * (1.0 + t) + 0.5 * pre * (1.0 - t * t) * (c * (1.0 + 3 * 0.044715 * square))
    grad_pre = (gh_ref[...] * slope).astype(BF16)
    grad_normed = dot(grad_pre, wt_ref[...])
    grad_ref[...] = (
        grad_normed - normed * jnp.mean(grad_normed * normed, -1, keepdims=True)
    ) * scale
    send_columns([grad_ref], out_refs, me)


def grad_summary_kernel(steps, size, count, *refs):
    in_refs, (att_ref, inv_ref, f_ref) = refs[:count], refs[count : count + 3]
    num_ref, den_ref, g_ref, scratch = refs[count + 3 :]
    place_rows(scratch, in_refs, steps)
    mask = head_mask(size, LANES)
    grad_att = scratch[...]
    inverse = inv_ref[...]
    feat = f_ref[...]
    grad_num = grad_att * inverse
    grad_den = -head_sums(grad_att * att_ref[...], head_ones(mask)) * inverse
    num_ref[...] = grad_num
    den_ref[...] = grad_den
    store_summary(g_ref, *summaries(feat, grad_num, feat * grad_den, steps, size))


def query_back_kernel(steps, factor, s_ref, num_ref, den_ref, f_ref, u_ref, proj_ref, g_ref):
    size = proj_ref.shape[0]
    mask = head_mask(size, LANES)
    high = f_ref.shape[0] // steps
    out = []
    for step, (matrix, row) in enumerate(load_summary([s_ref], steps, size)):
        part = slice(step * high, (step + 1) * high)
        back = dot3(split(num_ref[part, :]), split(spread(matrix, mask)), NT)
        out.append(back + den_ref[part, :] * row)
    weighted = jnp.concatenate(out, 0) * f_ref[...]
    grad = feature_back(
        weighted, u_ref[...], [proj_ref[...]], mask, head_ones(mask)
    )
    g_ref[...] = (grad * factor).astype(BF16)


def key_back_kernel(steps, factor, parts, devices, *refs):
    g_refs, (u_ref, v_ref, f_ref, proj_ref, gq_ref) = refs[:parts], refs[parts : parts + 5]
    x_all, total_ref, keep_ref, send_ref, p_ref = refs[parts + 5 :]
    size = proj_ref.shape[0]
    mask = head_mask(size, LANES)
    high = f_ref.shape[0] // steps
    total = g_refs[0][...]
    for ref in g_refs[1:]:
        total = total + ref[...]
    total_ref[...] = total
    back, grad_v = [], []
    for step, (matrix, row) in enumerate(load_summary([total_ref], steps, size)):
        part = slice(step * high, (step + 1) * high)
        matrix = split(spread(matrix, mask))
        back.append(dot3(split(v_ref[part, :]), matrix, NT) + row)
        grad_v.append(dot3(split(f_ref[part, :]), matrix))
    weighted = jnp.concatenate(back, 0) * f_ref[...]
    grad_k = feature_back(
        weighted, u_ref[...], [proj_ref[...]], mask, head_ones(mask)
    )
    grad = jnp.concatenate([grad_k * factor, jnp.concatenate(grad_v, 0)], -1).astype(BF16)
    total = dot(x_all[...], jnp.concatenate([gq_ref[...], grad], -1))
    block = total.shape[0] // devices
    for place in range(devices):
        p_ref[place % 2, place // 2 % 2, place // 4] = total[place * block : (place + 1) * block]
    low = lax.axis_index("step") % 2
    keep_ref[...] = p_ref[low]
    send_ref[...] = p_ref[1 - low]


def core_kernel(count, own_ref, got_ref, *refs):
    high = lax.axis_index("step") // 2 % 2
    mine = lax.axis_index("sensor") // count
    per = len(refs) // 2
    for place, ref in enumerate(refs):
        part = high ^ (place // per)
        if per == 2:
            block = mine ^ (place % 2)
            ref[...] = own_ref[part, block] + got_ref[part, block]
        else:
            ref[...] = own_ref[part] + got_ref[part]


def collect_columns(target, refs):
    me = lax.axis_index("sensor") % len(refs)
    for partner, ref in enumerate(refs):
        target[:, columns((me ^ partner) % len(refs))] = ref[...]


def query_rows_kernel(steps, factor, count, *refs):
    in_refs, (f_ref, u_ref, att_ref, grad_ref) = refs[:count], refs[count : count + 4]
    proj_ref, wq_ref, out_ref, s_ref = refs[count + 4 :]
    collect_columns(s_ref, in_refs[::-1])
    size = proj_ref.shape[1]
    mask = head_mask(size, WIDE)
    ones = head_ones(mask)
    rows = f_ref.shape[0] // steps
    feat, grad_att = f_ref[...], grad_ref[...]
    normal = [s_ref[steps * size + t : steps * size + t + 1, :] for t in range(steps)]
    normal = jnp.concatenate([jnp.broadcast_to(n, (rows, n.shape[1])) for n in normal], 0)
    denom = jnp.concatenate([head_sums(w, ones) for w in pieces(feat * normal)], -1)
    inverse = 1.0 / denom
    grad_num = grad_att * inverse
    along = pieces(grad_att * att_ref[...])
    grad_den = -jnp.concatenate([head_sums(a, ones) for a in along], -1) * inverse
    back = []
    for step in range(steps):
        nums = pieces(grad_num[step * rows : (step + 1) * rows])
        matrices = pieces(s_ref[step * size : (step + 1) * size, :])
        parts = [dot3(split(n), split(spread(m, mask)), NT) for n, m in zip(nums, matrices)]
        back.append(jnp.concatenate(parts, -1))
    weighted = (jnp.concatenate(back, 0) + grad_den * normal) * feat
    grad = feature_back(weighted, u_ref[...], all_heads(proj_ref), mask, ones) * factor
    out_ref[...] = dot(grad.astype(BF16), wq_ref[...])


def rows_kernel(steps, factor, count, *refs):
    in_refs, (u_ref, v_ref, f_ref, proj_ref) = refs[:count], refs[count : count + 4]
    q_ref, wk_ref, wv_ref, out_ref, g_ref = refs[count + 4 :]
    size = proj_ref.shape[1]
    collect_columns(g_ref, in_refs)
    total = q_ref[...]
    mask = head_mask(size, WIDE)
    rows = f_ref.shape[0] // steps
    back, grad_v = [], []
    for step in range(steps):
        part = slice(step * rows, (step + 1) * rows)
        matrix = g_ref[step * size : (step + 1) * size, :]
        spreads = [split(spread(m, mask)) for m in pieces(matrix)]
        values = [split(v) for v in pieces(v_ref[part, :])]
        feats = [split(f) for f in pieces(f_ref[part, :])]
        row = g_ref[steps * size + step : steps * size + step + 1, :]
        back.append(
            jnp.concatenate([dot3(v, m, NT) for v, m in zip(values, spreads)], -1) + row
        )
        grad_v.append(jnp.concatenate([dot3(f, m) for f, m in zip(feats, spreads)], -1))
    weighted = jnp.concatenate(back, 0) * f_ref[...]
    grad_k = feature_back(weighted, u_ref[...], all_heads(proj_ref), mask, head_ones(mask))
    total = total + dot((grad_k * factor).astype(BF16), wk_ref[...])
    grad_v = jnp.concatenate(grad_v, 0).astype(BF16)
    out_ref[...] = (total + dot(grad_v, wv_ref[...])).astype(BF16)


def final_kernel(scale, parts, *refs):
    in_refs, outs = refs[:parts], refs[parts:]
    total = in_refs[0][...]
    for ref in in_refs[1:]:
        total = total + ref[...]
    cols = outs[0].shape[1]
    for place, ref in enumerate(outs):
        ref[...] = total[:, place * cols : (place + 1) * cols] * scale


def call(kernel, name, outs, args, flops=0, smem=0, hbm=0, scratch=(), limit=20):
    size = lambda a: math.prod(a.shape) * a.dtype.itemsize
    rest = len(args) - smem - hbm
    return pl.pallas_call(
        kernel,
        name=name,
        out_shape=outs,
        in_specs=[SMEM] * smem + [pl.BlockSpec(memory_space=pl.ANY)] * hbm + [VMEM] * rest,
        out_specs=jax.tree.map(lambda _: VMEM, outs),
        scratch_shapes=list(scratch),
        cost_estimate=pl.CostEstimate(
            flops=flops,
            bytes_accessed=sum(size(a) for a in list(args) + list(jax.tree.leaves(outs))),
            transcendentals=0,
        ),
        compiler_params=pltpu.CompilerParams(vmem_limit_bytes=limit * 1024 * 1024),
    )(*args)


def shape(dims, kind=F32):
    return jax.ShapeDtypeStruct(dims, kind)


def swap(a, axis, bit):
    return lax.ppermute(a, axis, [(i, i ^ bit) for i in range(lax.axis_size(axis))])


def trade(parts, axis, together=True):
    order = [len(parts) - 1, *range(1, len(parts) - 1)]
    got = [swap(parts[d], axis, d) for d in order]
    if together:
        got = lax.optimization_barrier(got)
    return [parts[0], *got[1:], got[0]]


def gather_halves(top, low, axis):
    near_low, next_top = swap(low, axis, 2), swap(top, axis, 1)
    near_top, next_low = swap(top, axis, 2), swap(low, axis, 1)
    across_top, across_low = swap(next_top, axis, 2), swap(near_low, axis, 1)
    return (top, next_top, near_top, across_top), (low, next_low, near_low, across_low)


def far_sum(a, count):
    bit = count
    while bit * 2 < lax.axis_size("sensor"):
        a = a + swap(a, "sensor", bit)
        bit *= 2
    return a, swap(a, "sensor", bit)


def after(a, *others):
    return lax.optimization_barrier((a, others))[0]


def shards(inputs, cotangent, w_query, w_key, w_value, w_up, w_down, feature_proj, live_count):
    steps, sensors, width = inputs.shape
    heads, size, feats = feature_proj.shape
    hidden = w_up.shape[1]
    factor = size ** (-0.25)
    rows = steps * sensors
    devices = lax.axis_size("sensor")
    count = width // LANES
    quads = devices // count
    x = inputs.reshape(rows, width)
    cot = cotangent.reshape(rows, width)
    narrow = shape((rows, LANES))
    tall = shape((rows * count, LANES))
    packed = shape((steps * size + 8, LANES))
    product = 2 * rows * width * width
    kinds = lambda *arrays: [pltpu.VMEM(a.shape, a.dtype) for a in arrays]
    wide = pltpu.VMEM((rows, width), F32)

    top, low = call(
        widen_kernel,
        "widen",
        (shape((rows // 2 + 8, width)),) * 2,
        (live_count, x),
        smem=1,
    )
    tops, lows = gather_halves(top, low, "sensor")
    narrow_w = shape((width, LANES), BF16)
    own_query, own_key, own_value, proj, query_rows, feat_rows, *local_keys = call(
        functools.partial(local_kernel, steps, factor, count),
        "local_keys",
        (narrow_w,) * 3 + (shape((size, LANES)),) + (shape((rows, width)),) * 5,
        (live_count, x, w_query, w_key, w_value, feature_proj),
        flops=3 * product,
        smem=1,
    )
    x_all, key, value, feat_key, summary = call(
        functools.partial(key_kernel, steps, factor, count),
        "keys",
        (shape((rows * count, width), BF16),) + (tall,) * 3 + (packed,),
        (*tops, *lows, own_key, own_value, proj),
        flops=3 * product,
    )
    turned = (x_all, w_query, w_key, w_value, w_up)
    x_turned, wq_turned, wk_turned, wv_turned, wu_turned = call(
        transpose_kernel, "transposes", tuple(shape(a.shape[::-1], BF16) for a in turned), turned
    )
    query, feat_query, grad_hidden = call(
        functools.partial(query_kernel, steps, factor, count),
        "queries",
        (tall, tall, shape((rows, hidden))),
        (live_count, x_all, cot, own_query, w_down, proj),
        flops=2 * product,
        smem=1,
    )
    summary = far_sum(summary, count)
    attended, inverse, summary, *local_att = call(
        functools.partial(attend_kernel, steps, size, len(summary)),
        "attend",
        (tall, tall, packed) + (narrow,) * count,
        (*summary, feat_query),
        flops=product,
    )
    local_att, local_grad_att, *local_grad = call(
        functools.partial(forward_kernel, count),
        "feed_forward",
        (shape((rows, width)),) * 2 + (narrow,) * count,
        (*trade(local_att, "sensor"), grad_hidden, w_up, wu_turned),
        flops=product,
    )
    grad_num, grad_den, grad_summary = call(
        functools.partial(grad_summary_kernel, steps, size, count),
        "grad_summary",
        (tall, tall, packed),
        (*trade(local_grad, "sensor"), attended, inverse, feat_query),
        flops=product,
        scratch=kinds(tall),
    )
    query_part = call(
        functools.partial(query_rows_kernel, steps, factor, count),
        "query_rows",
        shape((rows, width)),
        (
            *trade([summary] * count, "sensor", False)[::-1],
            feat_rows,
            query_rows,
            local_att,
            local_grad_att,
            feature_proj,
            wq_turned,
        ),
        flops=3 * product,
        scratch=[pltpu.VMEM((packed.shape[0], width), F32)],
    )
    grad_summary = far_sum(grad_summary, count)
    grad_q = call(
        functools.partial(query_back_kernel, steps, factor),
        "query_back",
        shape(tall.shape, BF16),
        (summary, grad_num, grad_den, feat_query, query, proj),
        flops=product,
    )
    tile = (width // devices, 3 * LANES)
    half = shape((2, quads, *tile))
    grad_summary, own_half, send_half = call(
        functools.partial(key_back_kernel, steps, factor, len(grad_summary), devices),
        "key_back",
        (packed, half, half),
        (*grad_summary, key, value, feat_key, proj, after(grad_q, query_part), x_turned),
        flops=4 * product,
        scratch=[pltpu.VMEM((2, *half.shape), F32)],
    )
    def turn(a, bit, flip=0):
        pairs = []
        for k in range(quads):
            for q in range(count):
                for j in range(count):
                    target = (k ^ bit) * count + (j ^ flip)
                    pairs.append(((k * count + q) * count + j, target * count + q))
        return lax.ppermute(a, ("sensor", "step"), pairs)

    got_half = swap(send_half, "step", 1)
    if quads == 2:
        kept, away, send_kept, send_away = call(
            functools.partial(core_kernel, count),
            "core_sums",
            (shape(tile),) * 4,
            (own_half, got_half),
        )
        parts = (turn(away, 1), turn(send_away, 1, 2), turn(send_kept, 0, 2), turn(kept, 0))
    else:
        kept, sent = call(
            functools.partial(core_kernel, count),
            "core_sums",
            (shape((quads, *tile)),) * 2,
            (own_half, got_half),
        )
        groups = [[q + count * k for k in range(quads)] for q in range(count)]
        blocks = lax.all_to_all(
            kept + swap(sent, "step", 2), "sensor", 0, 0, tiled=True, axis_index_groups=groups
        )
        parts = (turn(blocks.sum(0), 0),)
    messages = trade([grad_summary] * count, "sensor", False)
    scale = 1.0 / math.sqrt(rows * lax.axis_size("step") * devices)
    out = shape((width // devices, LANES))
    grad_in = call(
        functools.partial(rows_kernel, steps, factor, count),
        "input_rows",
        shape((rows, width), BF16),
        (*messages, *local_keys, feature_proj, query_part, wk_turned, wv_turned),
        flops=30 * product,
        scratch=[pltpu.VMEM((packed.shape[0], width), F32)],
    )
    grads = call(
        functools.partial(final_kernel, scale, len(parts)),
        "weight_sums",
        (out,) * 3,
        (after(parts[0], grad_in), *parts[1:]),
    )
    return (grad_in.reshape(inputs.shape), *grads)


def solution(mesh):
    return jax.shard_map(
        shards,
        mesh=mesh,
        in_specs=(P("step", "sensor", None),) * 2 + (P(),) * 6 + (P("sensor"),),
        out_specs=(P("step", "sensor", None),) + (P("sensor", "step"),) * 3,
        check_vma=False,
    )
```

```python
import functools
import math

import jax
import jax.numpy as jnp
from jax import lax
from jax.experimental import pallas as pl
from jax.experimental.pallas import tpu as pltpu
from jax.sharding import PartitionSpec as P

F32 = jnp.float32
BF16 = jnp.bfloat16
NN = (((1,), (0,)), ((), ()))
NT = (((1,), (1,)), ((), ()))
TN = (((0,), (0,)), ((), ()))
VMEM = pl.BlockSpec(memory_space=pltpu.VMEM)
SMEM = pl.BlockSpec(memory_space=pltpu.SMEM)
LANES = 128
WIDE = 256


def dot(a, b, dims=NN):
    return lax.dot_general(a, b, dims, preferred_element_type=F32)


def split(x):
    high = x.astype(BF16)
    return high, (x - high.astype(F32)).astype(BF16)


def dot3(a, b, dims=NN):
    if a[0].shape[1] == LANES:
        axis = 1 if dims == NN else 0
        parts = [jnp.concatenate([b[0], b[1]], axis), jnp.concatenate([b[0], 0 * b[1]], axis)]
        out = dot(jnp.concatenate(a, 1), jnp.concatenate(parts, 1 - axis), dims)
        return out[:, :LANES] + out[:, LANES:]
    rows = a[0].shape[0]
    out = dot(jnp.concatenate(a, 0), b[0], dims)
    return out[:rows] + (out[rows:] + dot(a[0], b[1], dims))


def dot2(a, b, dims=NN):
    rows = a[0].shape[0]
    out = dot(jnp.concatenate(a, 0), b, dims)
    return out[:rows] + out[rows:]


def head_mask(size, width):
    rows = lax.broadcasted_iota(jnp.int32, (width, width), 0) // size
    cols = lax.broadcasted_iota(jnp.int32, (width, width), 1) // size
    return rows == cols


def head_ones(mask):
    return jnp.where(mask, 1.0, 0.0).astype(BF16)


def spread(x, mask):
    return jnp.where(mask, jnp.concatenate([x] * (x.shape[1] // x.shape[0]), 0), 0.0)


def gather_diagonal(x, size):
    head = lax.broadcasted_iota(jnp.int32, (size, x.shape[1]), 1) // size
    out = x[:size]
    for g in range(1, x.shape[1] // size):
        out = jnp.where(head == g, x[g * size : (g + 1) * size], out)
    return out


def head_sums(x, ones):
    high, low = split(x)
    if x.shape[1] == LANES:
        return dot(jnp.concatenate([high, low], 1), jnp.concatenate([ones, ones], 0))
    return dot2((high, low), ones)


def pieces(x, width=WIDE):
    return [x[:, h : h + width] for h in range(0, x.shape[1], width)]


def projection(proj_ref, heads=None, width=WIDE):
    heads = range(proj_ref.shape[0]) if heads is None else heads
    blocks = [proj_ref[h] for h in heads]
    per = width // proj_ref.shape[2]
    return [jnp.concatenate(blocks[g : g + per], -1) for g in range(0, len(blocks), per)]


def feature_map(scaled, proj, mask, ones, feats):
    out = []
    for u, p in zip(pieces(scaled, mask.shape[0]), proj):
        projected = dot3(split(u), split(spread(p, mask)))
        out.append(jnp.exp(projected - 0.5 * head_sums(u * u, ones)) * feats ** (-0.5))
    return jnp.concatenate(out, -1)


def feature_back(weighted, scaled, proj, mask, ones):
    out = []
    width = mask.shape[0]
    for w, u, p in zip(pieces(weighted, width), pieces(scaled, width), proj):
        back = dot3(split(w), split(spread(p, mask)), NT)
        out.append(back - u * head_sums(w, ones))
    return jnp.concatenate(out, -1)


def store_summary(out_ref, matrices, sums):
    size = matrices[0].shape[0]
    base = size * len(matrices)
    out_ref[base:, :] = jnp.zeros((out_ref.shape[0] - base, LANES), F32)
    for step, (matrix, row) in enumerate(zip(matrices, sums)):
        out_ref[step * size : (step + 1) * size, :] = matrix
        out_ref[base + step : base + step + 1, :] = row


def load_summary(refs, steps, size):
    total = refs[0][...]
    for ref in refs[1:]:
        total = total + ref[...]
    base = steps * size
    return [
        (total[step * size : (step + 1) * size], total[base + step : base + step + 1])
        for step in range(steps)
    ]


def outer_sums(a, b, size):
    out = dot(jnp.concatenate(split(a), 1), jnp.concatenate(split(b), 1), TN)
    whole = out[:LANES, :LANES] + (out[:LANES, LANES:] + out[LANES:, :LANES])
    return gather_diagonal(whole, size)


def summaries(a, b, weighted, steps, size):
    high = a.shape[0] // steps
    parts = [slice(step * high, (step + 1) * high) for step in range(steps)]
    matrices = [outer_sums(a[p], b[p], size) for p in parts]
    return matrices, [jnp.sum(weighted[p], 0, keepdims=True) for p in parts]


def columns(group):
    return pl.ds(pl.multiple_of(group * LANES, LANES), LANES)


def send_columns(sources, refs, me):
    for partner, ref in enumerate(refs):
        own = columns((me ^ partner) % len(refs))
        for place, source in enumerate(sources):
            rows = source.shape[0]
            ref[:rows, place * LANES : (place + 1) * LANES] = source[:, own]


def place_rows(target, refs, steps, column=0):
    rows = target.shape[0] // (steps * len(refs))
    lanes = slice(column * LANES, column * LANES + target.shape[1])
    for partner, ref in enumerate(refs):
        for step in range(steps):
            start = (step * len(refs) + partner) * rows
            target[start : start + rows, :] = ref[step * rows : (step + 1) * rows, lanes].astype(
                target.dtype
            )


def take_rows(values, partner, count, steps):
    rows = values.shape[0] // (steps * count)
    starts = [(step * count + partner) * rows for step in range(steps)]
    return jnp.concatenate([values[s : s + rows] for s in starts], 0)


def widen_kernel(live_ref, x_ref, top_ref, low_ref):
    half = x_ref.shape[0] // 2
    for ref, base in ((top_ref, 0), (low_ref, half)):
        ref[:half, :] = x_ref[base : base + half].astype(F32)
        ref[half:, :] = jnp.full((ref.shape[0] - half, ref.shape[1]), live_ref[0]).astype(F32)


def own_columns(count):
    return columns(lax.axis_index("sensor") % count)


def own_heads(proj_ref, count):
    per = proj_ref.shape[0] // count
    start = (lax.axis_index("sensor") % count) * per
    return jnp.concatenate([proj_ref[start + h] for h in range(per)], -1)


def all_heads(proj_ref):
    per = WIDE // proj_ref.shape[2]
    return [
        jnp.concatenate([proj_ref[g + h] for h in range(per)], -1)
        for g in range(0, proj_ref.shape[0], per)
    ]


def local_kernel(steps, factor, count, live_ref, x_ref, wq_ref, wk_ref, wv_ref, proj_ref, *refs):
    oq_ref, ok_ref, ov_ref, op_ref, uq_ref, fq_ref, u_ref, v_ref, f_ref = refs
    own = own_columns(count)
    oq_ref[...] = wq_ref[:, own]
    ok_ref[...] = wk_ref[:, own]
    ov_ref[...] = wv_ref[:, own]
    op_ref[...] = own_heads(proj_ref, count)
    mask = head_mask(proj_ref.shape[1], WIDE)
    x = x_ref[...]
    proj = all_heads(proj_ref)
    scaled = dot(x, wq_ref[...]) * factor
    uq_ref[...] = scaled
    fq_ref[...] = feature_map(scaled, proj, mask, head_ones(mask), proj_ref.shape[2])
    scaled = dot(x, wk_ref[...]) * factor
    u_ref[...] = scaled
    v_ref[...] = dot(x, wv_ref[...])
    feat = feature_map(scaled, proj, mask, head_ones(mask), proj_ref.shape[2])
    place = lax.broadcasted_iota(jnp.int32, feat.shape, 0) % (feat.shape[0] // steps)
    f_ref[...] = jnp.where(place < live_ref[0], feat, 0.0)


def key_kernel(steps, factor, count, *refs):
    tops, lows = refs[:count], refs[count : 2 * count]
    wk_ref, wv_ref, proj_ref, x_ref, u_ref, v_ref, f_ref, s_ref = refs[2 * count :]
    size = proj_ref.shape[0]
    mask = head_mask(size, LANES)
    rows = x_ref.shape[0] // (steps * count)
    half = steps * rows // 2
    piece = math.gcd(half, rows)
    for partner in range(count):
        for ref, base in ((tops[partner], 0), (lows[partner], half)):
            for row in range(0, half, piece):
                step, inner = divmod(base + row, rows)
                start = (step * count + partner) * rows + inner
                x_ref[start : start + piece, :] = ref[row : row + piece, :].astype(BF16)
    x = x_ref[...]
    scaled = dot(x, wk_ref[...]) * factor
    values = dot(x, wv_ref[...])
    u_ref[...] = scaled
    v_ref[...] = values
    feat = feature_map(scaled, [proj_ref[...]], mask, head_ones(mask), size)
    place = lax.broadcasted_iota(jnp.int32, (rows, LANES), 0).astype(F32)
    keep = jnp.concatenate([place < ref[half : half + 1, :LANES] for ref in tops] * steps, 0)
    feat = jnp.where(keep, feat, 0.0)
    f_ref[...] = feat
    store_summary(s_ref, *summaries(feat, values, feat, steps, size))


def transpose_kernel(*refs):
    half = len(refs) // 2
    for source, target in zip(refs[:half], refs[half:]):
        target[...] = source[...].T


def query_kernel(steps, factor, count, live_ref, x_ref, cot_ref, wq_ref, wd_ref, proj_ref, u_ref, f_ref, gh_ref):
    size = proj_ref.shape[0]
    mask = head_mask(size, LANES)
    scaled = dot(x_ref[...], wq_ref[...]) * factor
    u_ref[...] = scaled
    f_ref[...] = feature_map(
        scaled, [proj_ref[...]], mask, head_ones(mask), size
    )
    hidden = dot(cot_ref[...], wd_ref[...], NT)
    place = lax.broadcasted_iota(jnp.int32, hidden.shape, 0) % (hidden.shape[0] // steps)
    gh_ref[...] = jnp.where(place < live_ref[0], hidden, 0.0)


def attend_kernel(steps, size, parts, *refs):
    s_refs, (f_ref, att_ref, inv_ref, s_ref) = refs[:parts], refs[parts : parts + 4]
    out_refs = refs[parts + 4 :]
    total = s_refs[0][...]
    for ref in s_refs[1:]:
        total = total + ref[...]
    s_ref[...] = total
    mask = head_mask(size, LANES)
    feat = f_ref[...]
    high = feat.shape[0] // steps
    numer, weighted = [], []
    for step, (matrix, row) in enumerate(load_summary([s_ref], steps, size)):
        part = feat[step * high : (step + 1) * high]
        numer.append(dot3(split(part), split(spread(matrix, mask))))
        weighted.append(part * row)
    inverse = 1.0 / head_sums(jnp.concatenate(weighted, 0), head_ones(mask))
    attended = jnp.concatenate(numer, 0) * inverse
    att_ref[...] = attended
    inv_ref[...] = inverse
    for partner, ref in enumerate(out_refs):
        ref[...] = take_rows(attended, partner, len(out_refs), steps)


def forward_kernel(count, *refs):
    in_refs, (gh_ref, wu_ref, wt_ref) = refs[:count], refs[count : count + 3]
    att_ref, grad_ref, out_refs = refs[count + 3], refs[count + 4], refs[count + 5 :]
    me = lax.axis_index("sensor") % count
    for partner, ref in enumerate(in_refs):
        att_ref[:, columns((me ^ partner) % count)] = ref[...]
    attended = att_ref[...]
    scale = lax.rsqrt(jnp.mean(attended * attended, -1, keepdims=True) + 1e-06)
    normed = attended * scale
    pre = dot(normed.astype(BF16), wu_ref[...])
    c = math.sqrt(2.0 / math.pi)
    square = pre * pre
    t = jnp.tanh(c * pre * (1.0 + 0.044715 * square))
    slope = 0.5 * (1.0 + t) + 0.5 * pre * (1.0 - t * t) * (c * (1.0 + 3 * 0.044715 * square))
    grad_pre = (gh_ref[...] * slope).astype(BF16)
    grad_normed = dot(grad_pre, wt_ref[...])
    grad_ref[...] = (
        grad_normed - normed * jnp.mean(grad_normed * normed, -1, keepdims=True)
    ) * scale
    send_columns([grad_ref], out_refs, me)


def grad_summary_kernel(steps, size, count, *refs):
    in_refs, (att_ref, inv_ref, f_ref) = refs[:count], refs[count : count + 3]
    num_ref, den_ref, g_ref, scratch = refs[count + 3 :]
    place_rows(scratch, in_refs, steps)
    mask = head_mask(size, LANES)
    grad_att = scratch[...]
    inverse = inv_ref[...]
    feat = f_ref[...]
    grad_num = grad_att * inverse
    grad_den = -head_sums(grad_att * att_ref[...], head_ones(mask)) * inverse
    num_ref[...] = grad_num
    den_ref[...] = grad_den
    store_summary(g_ref, *summaries(feat, grad_num, feat * grad_den, steps, size))


def query_back_kernel(steps, factor, s_ref, num_ref, den_ref, f_ref, u_ref, proj_ref, g_ref):
    size = proj_ref.shape[0]
    mask = head_mask(size, LANES)
    high = f_ref.shape[0] // steps
    out = []
    for step, (matrix, row) in enumerate(load_summary([s_ref], steps, size)):
        part = slice(step * high, (step + 1) * high)
        back = dot3(split(num_ref[part, :]), split(spread(matrix, mask)), NT)
        out.append(back + den_ref[part, :] * row)
    weighted = jnp.concatenate(out, 0) * f_ref[...]
    grad = feature_back(
        weighted, u_ref[...], [proj_ref[...]], mask, head_ones(mask)
    )
    g_ref[...] = (grad * factor).astype(BF16)


def key_back_kernel(steps, factor, parts, devices, *refs):
    g_refs, (u_ref, v_ref, f_ref, proj_ref, gq_ref) = refs[:parts], refs[parts : parts + 5]
    x_all, total_ref, keep_ref, send_ref, p_ref = refs[parts + 5 :]
    size = proj_ref.shape[0]
    mask = head_mask(size, LANES)
    high = f_ref.shape[0] // steps
    total = g_refs[0][...]
    for ref in g_refs[1:]:
        total = total + ref[...]
    total_ref[...] = total
    back, grad_v = [], []
    for step, (matrix, row) in enumerate(load_summary([total_ref], steps, size)):
        part = slice(step * high, (step + 1) * high)
        matrix = split(spread(matrix, mask))
        back.append(dot3(split(v_ref[part, :]), matrix, NT) + row)
        grad_v.append(dot3(split(f_ref[part, :]), matrix))
    weighted = jnp.concatenate(back, 0) * f_ref[...]
    grad_k = feature_back(
        weighted, u_ref[...], [proj_ref[...]], mask, head_ones(mask)
    )
    grad = jnp.concatenate([grad_k * factor, jnp.concatenate(grad_v, 0)], -1).astype(BF16)
    total = dot(x_all[...], jnp.concatenate([gq_ref[...], grad], -1))
    block = total.shape[0] // devices
    for place in range(devices):
        p_ref[place % 2, place // 2 % 2, place // 4] = total[place * block : (place + 1) * block]
    low = lax.axis_index("step") % 2
    keep_ref[...] = p_ref[low]
    send_ref[...] = p_ref[1 - low]


def core_kernel(count, own_ref, got_ref, *refs):
    high = lax.axis_index("step") // 2 % 2
    mine = lax.axis_index("sensor") // count
    per = len(refs) // 2
    for place, ref in enumerate(refs):
        part = high ^ (place // per)
        if per == 2:
            block = mine ^ (place % 2)
            ref[...] = own_ref[part, block] + got_ref[part, block]
        else:
            ref[...] = own_ref[part] + got_ref[part]


def collect_columns(target, refs):
    me = lax.axis_index("sensor") % len(refs)
    for partner, ref in enumerate(refs):
        target[:, columns((me ^ partner) % len(refs))] = ref[...]


def query_rows_kernel(steps, factor, count, *refs):
    in_refs, (f_ref, u_ref, att_ref, grad_ref) = refs[:count], refs[count : count + 4]
    proj_ref, wq_ref, out_ref, s_ref = refs[count + 4 :]
    collect_columns(s_ref, in_refs[::-1])
    size = proj_ref.shape[1]
    mask = head_mask(size, WIDE)
    ones = head_ones(mask)
    rows = f_ref.shape[0] // steps
    feat, grad_att = f_ref[...], grad_ref[...]
    normal = [s_ref[steps * size + t : steps * size + t + 1, :] for t in range(steps)]
    normal = jnp.concatenate([jnp.broadcast_to(n, (rows, n.shape[1])) for n in normal], 0)
    denom = jnp.concatenate([head_sums(w, ones) for w in pieces(feat * normal)], -1)
    inverse = 1.0 / denom
    grad_num = grad_att * inverse
    along = pieces(grad_att * att_ref[...])
    grad_den = -jnp.concatenate([head_sums(a, ones) for a in along], -1) * inverse
    back = []
    for step in range(steps):
        nums = pieces(grad_num[step * rows : (step + 1) * rows])
        matrices = pieces(s_ref[step * size : (step + 1) * size, :])
        parts = [dot3(split(n), split(spread(m, mask)), NT) for n, m in zip(nums, matrices)]
        back.append(jnp.concatenate(parts, -1))
    weighted = (jnp.concatenate(back, 0) + grad_den * normal) * feat
    grad = feature_back(weighted, u_ref[...], all_heads(proj_ref), mask, ones) * factor
    out_ref[...] = dot(grad.astype(BF16), wq_ref[...])


def rows_kernel(steps, factor, count, *refs):
    in_refs, (u_ref, v_ref, f_ref, proj_ref) = refs[:count], refs[count : count + 4]
    q_ref, wk_ref, wv_ref, out_ref, g_ref = refs[count + 4 :]
    size = proj_ref.shape[1]
    collect_columns(g_ref, in_refs)
    total = q_ref[...]
    mask = head_mask(size, WIDE)
    rows = f_ref.shape[0] // steps
    back, grad_v = [], []
    for step in range(steps):
        part = slice(step * rows, (step + 1) * rows)
        matrix = g_ref[step * size : (step + 1) * size, :]
        spreads = [split(spread(m, mask)) for m in pieces(matrix)]
        values = [split(v) for v in pieces(v_ref[part, :])]
        feats = [split(f) for f in pieces(f_ref[part, :])]
        row = g_ref[steps * size + step : steps * size + step + 1, :]
        back.append(
            jnp.concatenate([dot3(v, m, NT) for v, m in zip(values, spreads)], -1) + row
        )
        grad_v.append(jnp.concatenate([dot3(f, m) for f, m in zip(feats, spreads)], -1))
    weighted = jnp.concatenate(back, 0) * f_ref[...]
    grad_k = feature_back(weighted, u_ref[...], all_heads(proj_ref), mask, head_ones(mask))
    total = total + dot((grad_k * factor).astype(BF16), wk_ref[...])
    grad_v = jnp.concatenate(grad_v, 0).astype(BF16)
    out_ref[...] = (total + dot(grad_v, wv_ref[...])).astype(BF16)


def final_kernel(scale, parts, *refs):
    in_refs, outs = refs[:parts], refs[parts:]
    total = in_refs[0][...]
    for ref in in_refs[1:]:
        total = total + ref[...]
    cols = outs[0].shape[1]
    for place, ref in enumerate(outs):
        ref[...] = total[:, place * cols : (place + 1) * cols] * scale


def call(kernel, name, outs, args, flops=0, smem=0, hbm=0, scratch=(), limit=20):
    size = lambda a: math.prod(a.shape) * a.dtype.itemsize
    rest = len(args) - smem - hbm
    return pl.pallas_call(
        kernel,
        name=name,
        out_shape=outs,
        in_specs=[SMEM] * smem + [pl.BlockSpec(memory_space=pl.ANY)] * hbm + [VMEM] * rest,
        out_specs=jax.tree.map(lambda _: VMEM, outs),
        scratch_shapes=list(scratch),
        cost_estimate=pl.CostEstimate(
            flops=flops,
            bytes_accessed=sum(size(a) for a in list(args) + list(jax.tree.leaves(outs))),
            transcendentals=0,
        ),
        compiler_params=pltpu.CompilerParams(vmem_limit_bytes=limit * 1024 * 1024),
    )(*args)


def shape(dims, kind=F32):
    return jax.ShapeDtypeStruct(dims, kind)


def swap(a, axis, bit):
    return lax.ppermute(a, axis, [(i, i ^ bit) for i in range(lax.axis_size(axis))])


def trade(parts, axis, together=True):
    order = [len(parts) - 1, *range(1, len(parts) - 1)]
    got = [swap(parts[d], axis, d) for d in order]
    if together:
        got = lax.optimization_barrier(got)
    return [parts[0], *got[1:], got[0]]


def gather(a, axis, count):
    held = {0: a}
    bit = count // 2
    while bit:
        held |= {d | bit: swap(b, axis, bit) for d, b in held.items()}
        bit //= 2
    return [held[d] for d in sorted(held)]


def gather_halves(top, low, axis):
    near_low, next_top = swap(low, axis, 2), swap(top, axis, 1)
    near_top, next_low = swap(top, axis, 2), swap(low, axis, 1)
    across_top, across_low = swap(next_top, axis, 2), swap(near_low, axis, 1)
    return (top, next_top, near_top, across_top), (low, next_low, near_low, across_low)


def far_sum(a, count):
    bit = count
    while bit * 2 < lax.axis_size("sensor"):
        a = a + swap(a, "sensor", bit)
        bit *= 2
    return a, swap(a, "sensor", bit)


def after(a, *others):
    return lax.optimization_barrier((a, others))[0]


def shards(inputs, cotangent, w_query, w_key, w_value, w_up, w_down, feature_proj, live_count):
    steps, sensors, width = inputs.shape
    heads, size, feats = feature_proj.shape
    hidden = w_up.shape[1]
    factor = size ** (-0.25)
    rows = steps * sensors
    devices = lax.axis_size("sensor")
    count = width // LANES
    quads = devices // count
    x = inputs.reshape(rows, width)
    cot = cotangent.reshape(rows, width)
    narrow = shape((rows, LANES))
    tall = shape((rows * count, LANES))
    packed = shape((steps * size + 8, LANES))
    product = 2 * rows * width * width
    kinds = lambda *arrays: [pltpu.VMEM(a.shape, a.dtype) for a in arrays]
    wide = pltpu.VMEM((rows, width), F32)

    top, low = call(
        widen_kernel,
        "widen",
        (shape((rows // 2 + 8, width)),) * 2,
        (live_count, x),
        smem=1,
    )
    tops, lows = gather_halves(top, low, "sensor")
    narrow_w = shape((width, LANES), BF16)
    own_query, own_key, own_value, proj, query_rows, feat_rows, *local_keys = call(
        functools.partial(local_kernel, steps, factor, count),
        "local_keys",
        (narrow_w,) * 3 + (shape((size, LANES)),) + (shape((rows, width)),) * 5,
        (live_count, x, w_query, w_key, w_value, feature_proj),
        flops=3 * product,
        smem=1,
    )
    x_all, key, value, feat_key, summary = call(
        functools.partial(key_kernel, steps, factor, count),
        "keys",
        (shape((rows * count, width), BF16),) + (tall,) * 3 + (packed,),
        (*tops, *lows, own_key, own_value, proj),
        flops=3 * product,
    )
    turned = (x_all, w_query, w_key, w_value, w_up)
    x_turned, wq_turned, wk_turned, wv_turned, wu_turned = call(
        transpose_kernel, "transposes", tuple(shape(a.shape[::-1], BF16) for a in turned), turned
    )
    query, feat_query, grad_hidden = call(
        functools.partial(query_kernel, steps, factor, count),
        "queries",
        (tall, tall, shape((rows, hidden))),
        (live_count, x_all, cot, own_query, w_down, proj),
        flops=2 * product,
        smem=1,
    )
    summary = far_sum(summary, count)
    attended, inverse, summary, *local_att = call(
        functools.partial(attend_kernel, steps, size, len(summary)),
        "attend",
        (tall, tall, packed) + (narrow,) * count,
        (*summary, feat_query),
        flops=product,
    )
    local_att, local_grad_att, *local_grad = call(
        functools.partial(forward_kernel, count),
        "feed_forward",
        (shape((rows, width)),) * 2 + (narrow,) * count,
        (*trade(local_att, "sensor"), grad_hidden, w_up, wu_turned),
        flops=product,
    )
    grad_num, grad_den, grad_summary = call(
        functools.partial(grad_summary_kernel, steps, size, count),
        "grad_summary",
        (tall, tall, packed),
        (*trade(local_grad, "sensor"), attended, inverse, feat_query),
        flops=product,
        scratch=kinds(tall),
    )
    query_part = call(
        functools.partial(query_rows_kernel, steps, factor, count),
        "query_rows",
        shape((rows, width)),
        (
            *gather(summary, "sensor", count)[::-1],
            feat_rows,
            query_rows,
            local_att,
            local_grad_att,
            feature_proj,
            wq_turned,
        ),
        flops=3 * product,
        scratch=[pltpu.VMEM((packed.shape[0], width), F32)],
    )
    grad_summary = far_sum(grad_summary, count)
    grad_q = call(
        functools.partial(query_back_kernel, steps, factor),
        "query_back",
        shape(tall.shape, BF16),
        (summary, grad_num, grad_den, feat_query, query, proj),
        flops=product,
    )
    tile = (width // devices, 3 * LANES)
    half = shape((2, quads, *tile))
    grad_summary, own_half, send_half = call(
        functools.partial(key_back_kernel, steps, factor, len(grad_summary), devices),
        "key_back",
        (packed, half, half),
        (*grad_summary, key, value, feat_key, proj, after(grad_q, query_part), x_turned),
        flops=4 * product,
        scratch=[pltpu.VMEM((2, *half.shape), F32)],
    )
    def turn(a, bit, flip=0):
        pairs = []
        for k in range(quads):
            for q in range(count):
                for j in range(count):
                    target = (k ^ bit) * count + (j ^ flip)
                    pairs.append(((k * count + q) * count + j, target * count + q))
        return lax.ppermute(a, ("sensor", "step"), pairs)

    got_half = swap(send_half, "step", 1)
    if quads == 2:
        kept, away, send_kept, send_away = call(
            functools.partial(core_kernel, count),
            "core_sums",
            (shape(tile),) * 4,
            (own_half, got_half),
        )
        parts = (turn(away, 1), turn(send_away, 1, 2), turn(send_kept, 0, 2), turn(kept, 0))
    else:
        kept, sent = call(
            functools.partial(core_kernel, count),
            "core_sums",
            (shape((quads, *tile)),) * 2,
            (own_half, got_half),
        )
        groups = [[q + count * k for k in range(quads)] for q in range(count)]
        blocks = lax.all_to_all(
            kept + swap(sent, "step", 2), "sensor", 0, 0, tiled=True, axis_index_groups=groups
        )
        parts = (turn(blocks.sum(0), 0),)
    messages = trade([grad_summary] * count, "sensor", False)
    scale = 1.0 / math.sqrt(rows * lax.axis_size("step") * devices)
    out = shape((width // devices, LANES))
    grad_in = call(
        functools.partial(rows_kernel, steps, factor, count),
        "input_rows",
        shape((rows, width), BF16),
        (*messages, *local_keys, feature_proj, query_part, wk_turned, wv_turned),
        flops=30 * product,
        scratch=[pltpu.VMEM((packed.shape[0], width), F32)],
    )
    grads = call(
        functools.partial(final_kernel, scale, len(parts)),
        "weight_sums",
        (out,) * 3,
        (after(parts[0], grad_in), *parts[1:]),
    )
    return (grad_in.reshape(inputs.shape), *grads)


def solution(mesh):
    return jax.shard_map(
        shards,
        mesh=mesh,
        in_specs=(P("step", "sensor", None),) * 2 + (P(),) * 6 + (P("sensor"),),
        out_specs=(P("step", "sensor", None),) + (P("sensor", "step"),) * 3,
        check_vma=False,
    )
```

```python
import functools
import math

import jax
import jax.numpy as jnp
from jax import lax
from jax.experimental import pallas as pl
from jax.experimental.pallas import tpu as pltpu
from jax.sharding import PartitionSpec as P

F32 = jnp.float32
BF16 = jnp.bfloat16
NN = (((1,), (0,)), ((), ()))
NT = (((1,), (1,)), ((), ()))
TN = (((0,), (0,)), ((), ()))
VMEM = pl.BlockSpec(memory_space=pltpu.VMEM)
SMEM = pl.BlockSpec(memory_space=pltpu.SMEM)
LANES = 128
WIDE = 256


def dot(a, b, dims=NN):
    return lax.dot_general(a, b, dims, preferred_element_type=F32)


def split(x):
    high = x.astype(BF16)
    return high, (x - high.astype(F32)).astype(BF16)


def dot3(a, b, dims=NN):
    if a[0].shape[1] == LANES:
        axis = 1 if dims == NN else 0
        parts = [jnp.concatenate([b[0], b[1]], axis), jnp.concatenate([b[0], 0 * b[1]], axis)]
        out = dot(jnp.concatenate(a, 1), jnp.concatenate(parts, 1 - axis), dims)
        return out[:, :LANES] + out[:, LANES:]
    rows = a[0].shape[0]
    out = dot(jnp.concatenate(a, 0), b[0], dims)
    return out[:rows] + (out[rows:] + dot(a[0], b[1], dims))


def dot2(a, b, dims=NN):
    rows = a[0].shape[0]
    out = dot(jnp.concatenate(a, 0), b, dims)
    return out[:rows] + out[rows:]


def head_mask(size, width):
    rows = lax.broadcasted_iota(jnp.int32, (width, width), 0) // size
    cols = lax.broadcasted_iota(jnp.int32, (width, width), 1) // size
    return rows == cols


def head_ones(mask):
    return jnp.where(mask, 1.0, 0.0).astype(BF16)


def spread(x, mask):
    return jnp.where(mask, jnp.concatenate([x] * (x.shape[1] // x.shape[0]), 0), 0.0)


def gather_diagonal(x, size):
    head = lax.broadcasted_iota(jnp.int32, (size, x.shape[1]), 1) // size
    out = x[:size]
    for g in range(1, x.shape[1] // size):
        out = jnp.where(head == g, x[g * size : (g + 1) * size], out)
    return out


def head_sums(x, ones):
    high, low = split(x)
    if x.shape[1] == LANES:
        return dot(jnp.concatenate([high, low], 1), jnp.concatenate([ones, ones], 0))
    return dot2((high, low), ones)


def pieces(x, width=WIDE):
    return [x[:, h : h + width] for h in range(0, x.shape[1], width)]


def projection(proj_ref, heads=None, width=WIDE):
    heads = range(proj_ref.shape[0]) if heads is None else heads
    blocks = [proj_ref[h] for h in heads]
    per = width // proj_ref.shape[2]
    return [jnp.concatenate(blocks[g : g + per], -1) for g in range(0, len(blocks), per)]


def feature_map(scaled, proj, mask, ones, feats):
    out = []
    for u, p in zip(pieces(scaled, mask.shape[0]), proj):
        projected = dot3(split(u), split(spread(p, mask)))
        out.append(jnp.exp(projected - 0.5 * head_sums(u * u, ones)) * feats ** (-0.5))
    return jnp.concatenate(out, -1)


def feature_back(weighted, scaled, proj, mask, ones):
    out = []
    width = mask.shape[0]
    for w, u, p in zip(pieces(weighted, width), pieces(scaled, width), proj):
        back = dot3(split(w), split(spread(p, mask)), NT)
        out.append(back - u * head_sums(w, ones))
    return jnp.concatenate(out, -1)


def store_summary(out_ref, matrices, sums):
    size = matrices[0].shape[0]
    base = size * len(matrices)
    out_ref[base:, :] = jnp.zeros((out_ref.shape[0] - base, LANES), F32)
    for step, (matrix, row) in enumerate(zip(matrices, sums)):
        out_ref[step * size : (step + 1) * size, :] = matrix
        out_ref[base + step : base + step + 1, :] = row


def load_summary(refs, steps, size):
    total = refs[0][...]
    for ref in refs[1:]:
        total = total + ref[...]
    base = steps * size
    return [
        (total[step * size : (step + 1) * size], total[base + step : base + step + 1])
        for step in range(steps)
    ]


def outer_sums(a, b, size):
    out = dot(jnp.concatenate(split(a), 1), jnp.concatenate(split(b), 1), TN)
    whole = out[:LANES, :LANES] + (out[:LANES, LANES:] + out[LANES:, :LANES])
    return gather_diagonal(whole, size)


def summaries(a, b, weighted, steps, size):
    high = a.shape[0] // steps
    parts = [slice(step * high, (step + 1) * high) for step in range(steps)]
    matrices = [outer_sums(a[p], b[p], size) for p in parts]
    return matrices, [jnp.sum(weighted[p], 0, keepdims=True) for p in parts]


def columns(group):
    return pl.ds(pl.multiple_of(group * LANES, LANES), LANES)


def send_columns(sources, refs, me):
    for partner, ref in enumerate(refs):
        own = columns((me ^ partner) % len(refs))
        for place, source in enumerate(sources):
            rows = source.shape[0]
            ref[:rows, place * LANES : (place + 1) * LANES] = source[:, own]


def place_rows(target, refs, steps, column=0):
    rows = target.shape[0] // (steps * len(refs))
    lanes = slice(column * LANES, column * LANES + target.shape[1])
    for partner, ref in enumerate(refs):
        for step in range(steps):
            start = (step * len(refs) + partner) * rows
            target[start : start + rows, :] = ref[step * rows : (step + 1) * rows, lanes].astype(
                target.dtype
            )


def take_rows(values, partner, count, steps):
    rows = values.shape[0] // (steps * count)
    starts = [(step * count + partner) * rows for step in range(steps)]
    return jnp.concatenate([values[s : s + rows] for s in starts], 0)


def widen_kernel(live_ref, x_ref, top_ref, low_ref):
    half = x_ref.shape[0] // 2
    for ref, base in ((top_ref, 0), (low_ref, half)):
        ref[:half, :] = x_ref[base : base + half].astype(F32)
        ref[half:, :] = jnp.full((ref.shape[0] - half, ref.shape[1]), live_ref[0]).astype(F32)


def own_columns(count):
    return columns(lax.axis_index("sensor") % count)


def own_heads(proj_ref, count):
    per = proj_ref.shape[0] // count
    start = (lax.axis_index("sensor") % count) * per
    return jnp.concatenate([proj_ref[start + h] for h in range(per)], -1)


def all_heads(proj_ref):
    per = WIDE // proj_ref.shape[2]
    return [
        jnp.concatenate([proj_ref[g + h] for h in range(per)], -1)
        for g in range(0, proj_ref.shape[0], per)
    ]


def local_kernel(steps, factor, count, live_ref, x_ref, wq_ref, wk_ref, wv_ref, proj_ref, *refs):
    oq_ref, ok_ref, ov_ref, op_ref, uq_ref, fq_ref, u_ref, v_ref, f_ref = refs
    own = own_columns(count)
    oq_ref[...] = wq_ref[:, own]
    ok_ref[...] = wk_ref[:, own]
    ov_ref[...] = wv_ref[:, own]
    op_ref[...] = own_heads(proj_ref, count)
    mask = head_mask(proj_ref.shape[1], WIDE)
    x = x_ref[...]
    proj = all_heads(proj_ref)
    scaled = dot(x, wq_ref[...]) * factor
    uq_ref[...] = scaled
    fq_ref[...] = feature_map(scaled, proj, mask, head_ones(mask), proj_ref.shape[2])
    scaled = dot(x, wk_ref[...]) * factor
    u_ref[...] = scaled
    v_ref[...] = dot(x, wv_ref[...])
    feat = feature_map(scaled, proj, mask, head_ones(mask), proj_ref.shape[2])
    place = lax.broadcasted_iota(jnp.int32, feat.shape, 0) % (feat.shape[0] // steps)
    f_ref[...] = jnp.where(place < live_ref[0], feat, 0.0)


def key_kernel(steps, factor, count, *refs):
    tops, lows = refs[:count], refs[count : 2 * count]
    wk_ref, wv_ref, proj_ref, x_ref, u_ref, v_ref, f_ref, s_ref = refs[2 * count :]
    size = proj_ref.shape[0]
    mask = head_mask(size, LANES)
    rows = x_ref.shape[0] // (steps * count)
    half = steps * rows // 2
    piece = math.gcd(half, rows)
    for partner in range(count):
        for ref, base in ((tops[partner], 0), (lows[partner], half)):
            for row in range(0, half, piece):
                step, inner = divmod(base + row, rows)
                start = (step * count + partner) * rows + inner
                x_ref[start : start + piece, :] = ref[row : row + piece, :].astype(BF16)
    x = x_ref[...]
    scaled = dot(x, wk_ref[...]) * factor
    values = dot(x, wv_ref[...])
    u_ref[...] = scaled
    v_ref[...] = values
    feat = feature_map(scaled, [proj_ref[...]], mask, head_ones(mask), size)
    place = lax.broadcasted_iota(jnp.int32, (rows, LANES), 0).astype(F32)
    keep = jnp.concatenate([place < ref[half : half + 1, :LANES] for ref in tops] * steps, 0)
    feat = jnp.where(keep, feat, 0.0)
    f_ref[...] = feat
    store_summary(s_ref, *summaries(feat, values, feat, steps, size))


def transpose_kernel(*refs):
    half = len(refs) // 2
    for source, target in zip(refs[:half], refs[half:]):
        target[...] = source[...].T


def query_kernel(steps, factor, count, live_ref, x_ref, cot_ref, wq_ref, wd_ref, proj_ref, u_ref, f_ref, gh_ref):
    size = proj_ref.shape[0]
    mask = head_mask(size, LANES)
    scaled = dot(x_ref[...], wq_ref[...]) * factor
    u_ref[...] = scaled
    f_ref[...] = feature_map(
        scaled, [proj_ref[...]], mask, head_ones(mask), size
    )
    hidden = dot(cot_ref[...], wd_ref[...], NT)
    place = lax.broadcasted_iota(jnp.int32, hidden.shape, 0) % (hidden.shape[0] // steps)
    gh_ref[...] = jnp.where(place < live_ref[0], hidden, 0.0)


def attend_kernel(steps, size, parts, *refs):
    s_refs, (f_ref, att_ref, inv_ref, s_ref) = refs[:parts], refs[parts : parts + 4]
    out_refs = refs[parts + 4 :]
    total = s_refs[0][...]
    for ref in s_refs[1:]:
        total = total + ref[...]
    s_ref[...] = total
    mask = head_mask(size, LANES)
    feat = f_ref[...]
    high = feat.shape[0] // steps
    numer, weighted = [], []
    for step, (matrix, row) in enumerate(load_summary([s_ref], steps, size)):
        part = feat[step * high : (step + 1) * high]
        numer.append(dot3(split(part), split(spread(matrix, mask))))
        weighted.append(part * row)
    inverse = 1.0 / head_sums(jnp.concatenate(weighted, 0), head_ones(mask))
    attended = jnp.concatenate(numer, 0) * inverse
    att_ref[...] = attended
    inv_ref[...] = inverse
    for partner, ref in enumerate(out_refs):
        ref[...] = take_rows(attended, partner, len(out_refs), steps)


def forward_kernel(count, *refs):
    in_refs, (gh_ref, wu_ref, wt_ref) = refs[:count], refs[count : count + 3]
    att_ref, grad_ref, out_refs = refs[count + 3], refs[count + 4], refs[count + 5 :]
    me = lax.axis_index("sensor") % count
    for partner, ref in enumerate(in_refs):
        att_ref[:, columns((me ^ partner) % count)] = ref[...]
    attended = att_ref[...]
    scale = lax.rsqrt(jnp.mean(attended * attended, -1, keepdims=True) + 1e-06)
    normed = attended * scale
    pre = dot(normed.astype(BF16), wu_ref[...])
    c = math.sqrt(2.0 / math.pi)
    square = pre * pre
    t = jnp.tanh(c * pre * (1.0 + 0.044715 * square))
    slope = 0.5 * (1.0 + t) + 0.5 * pre * (1.0 - t * t) * (c * (1.0 + 3 * 0.044715 * square))
    grad_pre = (gh_ref[...] * slope).astype(BF16)
    grad_normed = dot(grad_pre, wt_ref[...])
    grad_ref[...] = (
        grad_normed - normed * jnp.mean(grad_normed * normed, -1, keepdims=True)
    ) * scale
    send_columns([grad_ref], out_refs, me)


def grad_summary_kernel(steps, size, count, *refs):
    in_refs, (att_ref, inv_ref, f_ref) = refs[:count], refs[count : count + 3]
    num_ref, den_ref, g_ref, scratch = refs[count + 3 :]
    place_rows(scratch, in_refs, steps)
    mask = head_mask(size, LANES)
    grad_att = scratch[...]
    inverse = inv_ref[...]
    feat = f_ref[...]
    grad_num = grad_att * inverse
    grad_den = -head_sums(grad_att * att_ref[...], head_ones(mask)) * inverse
    num_ref[...] = grad_num
    den_ref[...] = grad_den
    store_summary(g_ref, *summaries(feat, grad_num, feat * grad_den, steps, size))


def query_back_kernel(steps, factor, s_ref, num_ref, den_ref, f_ref, u_ref, proj_ref, g_ref):
    size = proj_ref.shape[0]
    mask = head_mask(size, LANES)
    high = f_ref.shape[0] // steps
    out = []
    for step, (matrix, row) in enumerate(load_summary([s_ref], steps, size)):
        part = slice(step * high, (step + 1) * high)
        back = dot3(split(num_ref[part, :]), split(spread(matrix, mask)), NT)
        out.append(back + den_ref[part, :] * row)
    weighted = jnp.concatenate(out, 0) * f_ref[...]
    grad = feature_back(
        weighted, u_ref[...], [proj_ref[...]], mask, head_ones(mask)
    )
    g_ref[...] = (grad * factor).astype(BF16)


def key_back_kernel(steps, factor, parts, devices, *refs):
    g_refs, (u_ref, v_ref, f_ref, proj_ref, gq_ref) = refs[:parts], refs[parts : parts + 5]
    x_all, total_ref, keep_ref, send_ref, p_ref = refs[parts + 5 :]
    size = proj_ref.shape[0]
    mask = head_mask(size, LANES)
    high = f_ref.shape[0] // steps
    total = g_refs[0][...]
    for ref in g_refs[1:]:
        total = total + ref[...]
    total_ref[...] = total
    back, grad_v = [], []
    for step, (matrix, row) in enumerate(load_summary([total_ref], steps, size)):
        part = slice(step * high, (step + 1) * high)
        matrix = split(spread(matrix, mask))
        back.append(dot3(split(v_ref[part, :]), matrix, NT) + row)
        grad_v.append(dot3(split(f_ref[part, :]), matrix))
    weighted = jnp.concatenate(back, 0) * f_ref[...]
    grad_k = feature_back(
        weighted, u_ref[...], [proj_ref[...]], mask, head_ones(mask)
    )
    grad = jnp.concatenate([grad_k * factor, jnp.concatenate(grad_v, 0)], -1).astype(BF16)
    total = dot(x_all[...], jnp.concatenate([gq_ref[...], grad], -1))
    block = total.shape[0] // devices
    for place in range(devices):
        p_ref[place % 2, place // 2 % 2, place // 4] = total[place * block : (place + 1) * block]
    low = lax.axis_index("step") % 2
    keep_ref[...] = p_ref[low]
    send_ref[...] = p_ref[1 - low]


def core_kernel(count, own_ref, got_ref, *refs):
    high = lax.axis_index("step") // 2 % 2
    mine = lax.axis_index("sensor") // count
    per = len(refs) // 2
    for place, ref in enumerate(refs):
        part = high ^ (place // per)
        if per == 2:
            block = mine ^ (place % 2)
            ref[...] = own_ref[part, block] + got_ref[part, block]
        else:
            ref[...] = own_ref[part] + got_ref[part]


def collect_columns(target, refs):
    me = lax.axis_index("sensor") % len(refs)
    for partner, ref in enumerate(refs):
        target[:, columns((me ^ partner) % len(refs))] = ref[...]


def query_rows_kernel(steps, factor, count, *refs):
    in_refs, (f_ref, u_ref, att_ref, grad_ref) = refs[:count], refs[count : count + 4]
    proj_ref, wq_ref, out_ref, s_ref = refs[count + 4 :]
    collect_columns(s_ref, in_refs[::-1])
    size = proj_ref.shape[1]
    mask = head_mask(size, WIDE)
    ones = head_ones(mask)
    rows = f_ref.shape[0] // steps
    feat, grad_att = f_ref[...], grad_ref[...]
    normal = [s_ref[steps * size + t : steps * size + t + 1, :] for t in range(steps)]
    normal = jnp.concatenate([jnp.broadcast_to(n, (rows, n.shape[1])) for n in normal], 0)
    denom = jnp.concatenate([head_sums(w, ones) for w in pieces(feat * normal)], -1)
    inverse = 1.0 / denom
    grad_num = grad_att * inverse
    along = pieces(grad_att * att_ref[...])
    grad_den = -jnp.concatenate([head_sums(a, ones) for a in along], -1) * inverse
    back = []
    for step in range(steps):
        nums = pieces(grad_num[step * rows : (step + 1) * rows])
        matrices = pieces(s_ref[step * size : (step + 1) * size, :])
        parts = [dot3(split(n), split(spread(m, mask)), NT) for n, m in zip(nums, matrices)]
        back.append(jnp.concatenate(parts, -1))
    weighted = (jnp.concatenate(back, 0) + grad_den * normal) * feat
    grad = feature_back(weighted, u_ref[...], all_heads(proj_ref), mask, ones) * factor
    out_ref[...] = dot(grad.astype(BF16), wq_ref[...])


def rows_kernel(steps, factor, count, *refs):
    in_refs, (u_ref, v_ref, f_ref, proj_ref) = refs[:count], refs[count : count + 4]
    q_ref, wk_ref, wv_ref, out_ref, g_ref = refs[count + 4 :]
    size = proj_ref.shape[1]
    collect_columns(g_ref, in_refs)
    total = q_ref[...]
    mask = head_mask(size, WIDE)
    rows = f_ref.shape[0] // steps
    back, grad_v = [], []
    for step in range(steps):
        part = slice(step * rows, (step + 1) * rows)
        matrix = g_ref[step * size : (step + 1) * size, :]
        spreads = [split(spread(m, mask)) for m in pieces(matrix)]
        values = [split(v) for v in pieces(v_ref[part, :])]
        feats = [split(f) for f in pieces(f_ref[part, :])]
        row = g_ref[steps * size + step : steps * size + step + 1, :]
        back.append(
            jnp.concatenate([dot3(v, m, NT) for v, m in zip(values, spreads)], -1) + row
        )
        grad_v.append(jnp.concatenate([dot3(f, m) for f, m in zip(feats, spreads)], -1))
    weighted = jnp.concatenate(back, 0) * f_ref[...]
    grad_k = feature_back(weighted, u_ref[...], all_heads(proj_ref), mask, head_ones(mask))
    total = total + dot((grad_k * factor).astype(BF16), wk_ref[...])
    grad_v = jnp.concatenate(grad_v, 0).astype(BF16)
    out_ref[...] = (total + dot(grad_v, wv_ref[...])).astype(BF16)


def final_kernel(scale, parts, *refs):
    in_refs, outs = refs[:parts], refs[parts:]
    total = in_refs[0][...]
    for ref in in_refs[1:]:
        total = total + ref[...]
    cols = outs[0].shape[1]
    for place, ref in enumerate(outs):
        ref[...] = total[:, place * cols : (place + 1) * cols] * scale


def call(kernel, name, outs, args, flops=0, smem=0, hbm=0, scratch=(), limit=20):
    size = lambda a: math.prod(a.shape) * a.dtype.itemsize
    rest = len(args) - smem - hbm
    return pl.pallas_call(
        kernel,
        name=name,
        out_shape=outs,
        in_specs=[SMEM] * smem + [pl.BlockSpec(memory_space=pl.ANY)] * hbm + [VMEM] * rest,
        out_specs=jax.tree.map(lambda _: VMEM, outs),
        scratch_shapes=list(scratch),
        cost_estimate=pl.CostEstimate(
            flops=flops,
            bytes_accessed=sum(size(a) for a in list(args) + list(jax.tree.leaves(outs))),
            transcendentals=0,
        ),
        compiler_params=pltpu.CompilerParams(vmem_limit_bytes=limit * 1024 * 1024),
    )(*args)


def shape(dims, kind=F32):
    return jax.ShapeDtypeStruct(dims, kind)


def swap(a, axis, bit):
    return lax.ppermute(a, axis, [(i, i ^ bit) for i in range(lax.axis_size(axis))])


def trade(parts, axis, together=True):
    order = [len(parts) - 1, *reversed(range(1, len(parts) - 1))]
    got = [swap(parts[d], axis, d) for d in order]
    if together:
        got = lax.optimization_barrier(got)
    return [parts[0], *got[:0:-1], got[0]]


def gather(a, axis, count):
    held = {0: a}
    bit = count // 2
    while bit:
        held |= {d | bit: swap(b, axis, bit) for d, b in held.items()}
        bit //= 2
    return [held[d] for d in sorted(held)]


def gather_halves(top, low, axis):
    near_low, next_top = swap(low, axis, 2), swap(top, axis, 1)
    near_top, next_low = swap(top, axis, 2), swap(low, axis, 1)
    across_top, across_low = swap(next_top, axis, 2), swap(near_low, axis, 1)
    return (top, next_top, near_top, across_top), (low, next_low, near_low, across_low)


def far_sum(a, count):
    bit = count
    while bit * 2 < lax.axis_size("sensor"):
        a = a + swap(a, "sensor", bit)
        bit *= 2
    return a, swap(a, "sensor", bit)


def after(a, *others):
    return lax.optimization_barrier((a, others))[0]


def shards(inputs, cotangent, w_query, w_key, w_value, w_up, w_down, feature_proj, live_count):
    steps, sensors, width = inputs.shape
    heads, size, feats = feature_proj.shape
    hidden = w_up.shape[1]
    factor = size ** (-0.25)
    rows = steps * sensors
    devices = lax.axis_size("sensor")
    count = width // LANES
    quads = devices // count
    x = inputs.reshape(rows, width)
    cot = cotangent.reshape(rows, width)
    narrow = shape((rows, LANES))
    tall = shape((rows * count, LANES))
    packed = shape((steps * size + 8, LANES))
    product = 2 * rows * width * width
    kinds = lambda *arrays: [pltpu.VMEM(a.shape, a.dtype) for a in arrays]
    wide = pltpu.VMEM((rows, width), F32)

    top, low = call(
        widen_kernel,
        "widen",
        (shape((rows // 2 + 8, width)),) * 2,
        (live_count, x),
        smem=1,
    )
    tops, lows = gather_halves(top, low, "sensor")
    narrow_w = shape((width, LANES), BF16)
    own_query, own_key, own_value, proj, query_rows, feat_rows, *local_keys = call(
        functools.partial(local_kernel, steps, factor, count),
        "local_keys",
        (narrow_w,) * 3 + (shape((size, LANES)),) + (shape((rows, width)),) * 5,
        (live_count, x, w_query, w_key, w_value, feature_proj),
        flops=3 * product,
        smem=1,
    )
    x_all, key, value, feat_key, summary = call(
        functools.partial(key_kernel, steps, factor, count),
        "keys",
        (shape((rows * count, width), BF16),) + (tall,) * 3 + (packed,),
        (*tops, *lows, own_key, own_value, proj),
        flops=3 * product,
    )
    turned = (x_all, w_query, w_key, w_value, w_up)
    x_turned, wq_turned, wk_turned, wv_turned, wu_turned = call(
        transpose_kernel, "transposes", tuple(shape(a.shape[::-1], BF16) for a in turned), turned
    )
    query, feat_query, grad_hidden = call(
        functools.partial(query_kernel, steps, factor, count),
        "queries",
        (tall, tall, shape((rows, hidden))),
        (live_count, x_all, cot, own_query, w_down, proj),
        flops=2 * product,
        smem=1,
    )
    summary = far_sum(summary, count)
    attended, inverse, summary, *local_att = call(
        functools.partial(attend_kernel, steps, size, len(summary)),
        "attend",
        (tall, tall, packed) + (narrow,) * count,
        (*summary, feat_query),
        flops=product,
    )
    local_att, local_grad_att, *local_grad = call(
        functools.partial(forward_kernel, count),
        "feed_forward",
        (shape((rows, width)),) * 2 + (narrow,) * count,
        (*trade(local_att, "sensor"), grad_hidden, w_up, wu_turned),
        flops=product,
    )
    grad_num, grad_den, grad_summary = call(
        functools.partial(grad_summary_kernel, steps, size, count),
        "grad_summary",
        (tall, tall, packed),
        (*trade(local_grad, "sensor"), attended, inverse, feat_query),
        flops=product,
        scratch=kinds(tall),
    )
    query_part = call(
        functools.partial(query_rows_kernel, steps, factor, count),
        "query_rows",
        shape((rows, width)),
        (
            *gather(summary, "sensor", count)[::-1],
            feat_rows,
            query_rows,
            local_att,
            local_grad_att,
            feature_proj,
            wq_turned,
        ),
        flops=3 * product,
        scratch=[pltpu.VMEM((packed.shape[0], width), F32)],
    )
    grad_summary = far_sum(grad_summary, count)
    grad_q = call(
        functools.partial(query_back_kernel, steps, factor),
        "query_back",
        shape(tall.shape, BF16),
        (summary, grad_num, grad_den, feat_query, query, proj),
        flops=product,
    )
    tile = (width // devices, 3 * LANES)
    half = shape((2, quads, *tile))
    grad_summary, own_half, send_half = call(
        functools.partial(key_back_kernel, steps, factor, len(grad_summary), devices),
        "key_back",
        (packed, half, half),
        (*grad_summary, key, value, feat_key, proj, after(grad_q, query_part), x_turned),
        flops=4 * product,
        scratch=[pltpu.VMEM((2, *half.shape), F32)],
    )
    def turn(a, bit, flip=0):
        pairs = []
        for k in range(quads):
            for q in range(count):
                for j in range(count):
                    target = (k ^ bit) * count + (j ^ flip)
                    pairs.append(((k * count + q) * count + j, target * count + q))
        return lax.ppermute(a, ("sensor", "step"), pairs)

    got_half = swap(send_half, "step", 1)
    if quads == 2:
        kept, away, send_kept, send_away = call(
            functools.partial(core_kernel, count),
            "core_sums",
            (shape(tile),) * 4,
            (own_half, got_half),
        )
        parts = (turn(away, 1), turn(send_away, 1, 2), turn(send_kept, 0, 2), turn(kept, 0))
    else:
        kept, sent = call(
            functools.partial(core_kernel, count),
            "core_sums",
            (shape((quads, *tile)),) * 2,
            (own_half, got_half),
        )
        groups = [[q + count * k for k in range(quads)] for q in range(count)]
        blocks = lax.all_to_all(
            kept + swap(sent, "step", 2), "sensor", 0, 0, tiled=True, axis_index_groups=groups
        )
        parts = (turn(blocks.sum(0), 0),)
    messages = trade([grad_summary] * count, "sensor", False)
    scale = 1.0 / math.sqrt(rows * lax.axis_size("step") * devices)
    out = shape((width // devices, LANES))
    grad_in = call(
        functools.partial(rows_kernel, steps, factor, count),
        "input_rows",
        shape((rows, width), BF16),
        (*messages, *local_keys, feature_proj, query_part, wk_turned, wv_turned),
        flops=30 * product,
        scratch=[pltpu.VMEM((packed.shape[0], width), F32)],
    )
    grads = call(
        functools.partial(final_kernel, scale, len(parts)),
        "weight_sums",
        (out,) * 3,
        (after(parts[0], grad_in), *parts[1:]),
    )
    return (grad_in.reshape(inputs.shape), *grads)


def solution(mesh):
    return jax.shard_map(
        shards,
        mesh=mesh,
        in_specs=(P("step", "sensor", None),) * 2 + (P(),) * 6 + (P("sensor"),),
        out_specs=(P("step", "sensor", None),) + (P("sensor", "step"),) * 3,
        check_vma=False,
    )
```

```python
import functools
import math

import jax
import jax.numpy as jnp
from jax import lax
from jax.experimental import pallas as pl
from jax.experimental.pallas import tpu as pltpu
from jax.sharding import PartitionSpec as P

F32 = jnp.float32
BF16 = jnp.bfloat16
NN = (((1,), (0,)), ((), ()))
NT = (((1,), (1,)), ((), ()))
TN = (((0,), (0,)), ((), ()))
VMEM = pl.BlockSpec(memory_space=pltpu.VMEM)
SMEM = pl.BlockSpec(memory_space=pltpu.SMEM)
LANES = 128
WIDE = 256


def dot(a, b, dims=NN):
    return lax.dot_general(a, b, dims, preferred_element_type=F32)


def split(x):
    high = x.astype(BF16)
    return high, (x - high.astype(F32)).astype(BF16)


def dot3(a, b, dims=NN):
    if a[0].shape[1] == LANES:
        axis = 1 if dims == NN else 0
        parts = [jnp.concatenate([b[0], b[1]], axis), jnp.concatenate([b[0], 0 * b[1]], axis)]
        out = dot(jnp.concatenate(a, 1), jnp.concatenate(parts, 1 - axis), dims)
        return out[:, :LANES] + out[:, LANES:]
    rows = a[0].shape[0]
    out = dot(jnp.concatenate(a, 0), b[0], dims)
    return out[:rows] + (out[rows:] + dot(a[0], b[1], dims))


def dot2(a, b, dims=NN):
    rows = a[0].shape[0]
    out = dot(jnp.concatenate(a, 0), b, dims)
    return out[:rows] + out[rows:]


def head_mask(size, width):
    rows = lax.broadcasted_iota(jnp.int32, (width, width), 0) // size
    cols = lax.broadcasted_iota(jnp.int32, (width, width), 1) // size
    return rows == cols


def head_ones(mask):
    return jnp.where(mask, 1.0, 0.0).astype(BF16)


def spread(x, mask):
    return jnp.where(mask, jnp.concatenate([x] * (x.shape[1] // x.shape[0]), 0), 0.0)


def gather_diagonal(x, size):
    head = lax.broadcasted_iota(jnp.int32, (size, x.shape[1]), 1) // size
    out = x[:size]
    for g in range(1, x.shape[1] // size):
        out = jnp.where(head == g, x[g * size : (g + 1) * size], out)
    return out


def head_sums(x, ones):
    high, low = split(x)
    if x.shape[1] == LANES:
        return dot(jnp.concatenate([high, low], 1), jnp.concatenate([ones, ones], 0))
    return dot2((high, low), ones)


def pieces(x, width=WIDE):
    return [x[:, h : h + width] for h in range(0, x.shape[1], width)]


def projection(proj_ref, heads=None, width=WIDE):
    heads = range(proj_ref.shape[0]) if heads is None else heads
    blocks = [proj_ref[h] for h in heads]
    per = width // proj_ref.shape[2]
    return [jnp.concatenate(blocks[g : g + per], -1) for g in range(0, len(blocks), per)]


def feature_map(scaled, proj, mask, ones, feats):
    out = []
    for u, p in zip(pieces(scaled, mask.shape[0]), proj):
        projected = dot3(split(u), split(spread(p, mask)))
        out.append(jnp.exp(projected - 0.5 * head_sums(u * u, ones)) * feats ** (-0.5))
    return jnp.concatenate(out, -1)


def feature_back(weighted, scaled, proj, mask, ones):
    out = []
    width = mask.shape[0]
    for w, u, p in zip(pieces(weighted, width), pieces(scaled, width), proj):
        back = dot3(split(w), split(spread(p, mask)), NT)
        out.append(back - u * head_sums(w, ones))
    return jnp.concatenate(out, -1)


def store_summary(out_ref, matrices, sums):
    size = matrices[0].shape[0]
    base = size * len(matrices)
    out_ref[base:, :] = jnp.zeros((out_ref.shape[0] - base, LANES), F32)
    for step, (matrix, row) in enumerate(zip(matrices, sums)):
        out_ref[step * size : (step + 1) * size, :] = matrix
        out_ref[base + step : base + step + 1, :] = row


def load_summary(refs, steps, size):
    total = refs[0][...]
    for ref in refs[1:]:
        total = total + ref[...]
    base = steps * size
    return [
        (total[step * size : (step + 1) * size], total[base + step : base + step + 1])
        for step in range(steps)
    ]


def outer_sums(a, b, size):
    out = dot(jnp.concatenate(split(a), 1), jnp.concatenate(split(b), 1), TN)
    whole = out[:LANES, :LANES] + (out[:LANES, LANES:] + out[LANES:, :LANES])
    return gather_diagonal(whole, size)


def summaries(a, b, weighted, steps, size):
    high = a.shape[0] // steps
    parts = [slice(step * high, (step + 1) * high) for step in range(steps)]
    matrices = [outer_sums(a[p], b[p], size) for p in parts]
    return matrices, [jnp.sum(weighted[p], 0, keepdims=True) for p in parts]


def columns(group):
    return pl.ds(pl.multiple_of(group * LANES, LANES), LANES)


def send_columns(sources, refs, me):
    for partner, ref in enumerate(refs):
        own = columns((me ^ partner) % len(refs))
        for place, source in enumerate(sources):
            rows = source.shape[0]
            ref[:rows, place * LANES : (place + 1) * LANES] = source[:, own]


def place_rows(target, refs, steps, column=0):
    rows = target.shape[0] // (steps * len(refs))
    lanes = slice(column * LANES, column * LANES + target.shape[1])
    for partner, ref in enumerate(refs):
        for step in range(steps):
            start = (step * len(refs) + partner) * rows
            target[start : start + rows, :] = ref[step * rows : (step + 1) * rows, lanes].astype(
                target.dtype
            )


def take_rows(values, partner, count, steps):
    rows = values.shape[0] // (steps * count)
    starts = [(step * count + partner) * rows for step in range(steps)]
    return jnp.concatenate([values[s : s + rows] for s in starts], 0)


def widen_kernel(live_ref, x_ref, top_ref, low_ref):
    half = x_ref.shape[0] // 2
    for ref, base in ((top_ref, 0), (low_ref, half)):
        ref[:half, :] = x_ref[base : base + half].astype(F32)
        ref[half:, :] = jnp.full((ref.shape[0] - half, ref.shape[1]), live_ref[0]).astype(F32)


def own_columns(count):
    return columns(lax.axis_index("sensor") % count)


def own_heads(proj_ref, count):
    per = proj_ref.shape[0] // count
    start = (lax.axis_index("sensor") % count) * per
    return jnp.concatenate([proj_ref[start + h] for h in range(per)], -1)


def all_heads(proj_ref):
    per = WIDE // proj_ref.shape[2]
    return [
        jnp.concatenate([proj_ref[g + h] for h in range(per)], -1)
        for g in range(0, proj_ref.shape[0], per)
    ]


def local_kernel(steps, factor, count, live_ref, x_ref, wq_ref, wk_ref, wv_ref, proj_ref, *refs):
    oq_ref, ok_ref, ov_ref, op_ref, uq_ref, fq_ref, u_ref, v_ref, f_ref = refs
    own = own_columns(count)
    oq_ref[...] = wq_ref[:, own]
    ok_ref[...] = wk_ref[:, own]
    ov_ref[...] = wv_ref[:, own]
    op_ref[...] = own_heads(proj_ref, count)
    mask = head_mask(proj_ref.shape[1], WIDE)
    x = x_ref[...]
    proj = all_heads(proj_ref)
    scaled = dot(x, wq_ref[...]) * factor
    uq_ref[...] = scaled
    fq_ref[...] = feature_map(scaled, proj, mask, head_ones(mask), proj_ref.shape[2])
    scaled = dot(x, wk_ref[...]) * factor
    u_ref[...] = scaled
    v_ref[...] = dot(x, wv_ref[...])
    feat = feature_map(scaled, proj, mask, head_ones(mask), proj_ref.shape[2])
    place = lax.broadcasted_iota(jnp.int32, feat.shape, 0) % (feat.shape[0] // steps)
    f_ref[...] = jnp.where(place < live_ref[0], feat, 0.0)


def key_kernel(steps, factor, count, *refs):
    tops, lows = refs[:count], refs[count : 2 * count]
    wk_ref, wv_ref, proj_ref, x_ref, u_ref, v_ref, f_ref, s_ref = refs[2 * count :]
    size = proj_ref.shape[0]
    mask = head_mask(size, LANES)
    rows = x_ref.shape[0] // (steps * count)
    half = steps * rows // 2
    piece = math.gcd(half, rows)
    for partner in range(count):
        for ref, base in ((tops[partner], 0), (lows[partner], half)):
            for row in range(0, half, piece):
                step, inner = divmod(base + row, rows)
                start = (step * count + partner) * rows + inner
                x_ref[start : start + piece, :] = ref[row : row + piece, :].astype(BF16)
    x = x_ref[...]
    scaled = dot(x, wk_ref[...]) * factor
    values = dot(x, wv_ref[...])
    u_ref[...] = scaled
    v_ref[...] = values
    feat = feature_map(scaled, [proj_ref[...]], mask, head_ones(mask), size)
    place = lax.broadcasted_iota(jnp.int32, (rows, LANES), 0).astype(F32)
    keep = jnp.concatenate([place < ref[half : half + 1, :LANES] for ref in tops] * steps, 0)
    feat = jnp.where(keep, feat, 0.0)
    f_ref[...] = feat
    store_summary(s_ref, *summaries(feat, values, feat, steps, size))


def transpose_kernel(*refs):
    half = len(refs) // 2
    for source, target in zip(refs[:half], refs[half:]):
        target[...] = source[...].T


def query_kernel(steps, factor, count, live_ref, x_ref, cot_ref, wq_ref, wd_ref, proj_ref, u_ref, f_ref, gh_ref):
    size = proj_ref.shape[0]
    mask = head_mask(size, LANES)
    scaled = dot(x_ref[...], wq_ref[...]) * factor
    u_ref[...] = scaled
    f_ref[...] = feature_map(
        scaled, [proj_ref[...]], mask, head_ones(mask), size
    )
    hidden = dot(cot_ref[...], wd_ref[...], NT)
    place = lax.broadcasted_iota(jnp.int32, hidden.shape, 0) % (hidden.shape[0] // steps)
    gh_ref[...] = jnp.where(place < live_ref[0], hidden, 0.0)


def attend_kernel(steps, size, parts, *refs):
    s_refs, (f_ref, att_ref, inv_ref, s_ref) = refs[:parts], refs[parts : parts + 4]
    out_refs = refs[parts + 4 :]
    total = s_refs[0][...]
    for ref in s_refs[1:]:
        total = total + ref[...]
    s_ref[...] = total
    mask = head_mask(size, LANES)
    feat = f_ref[...]
    high = feat.shape[0] // steps
    numer, weighted = [], []
    for step, (matrix, row) in enumerate(load_summary([s_ref], steps, size)):
        part = feat[step * high : (step + 1) * high]
        numer.append(dot3(split(part), split(spread(matrix, mask))))
        weighted.append(part * row)
    inverse = 1.0 / head_sums(jnp.concatenate(weighted, 0), head_ones(mask))
    attended = jnp.concatenate(numer, 0) * inverse
    att_ref[...] = attended
    inv_ref[...] = inverse
    for partner, ref in enumerate(out_refs):
        ref[...] = take_rows(attended, partner, len(out_refs), steps)


def forward_kernel(count, *refs):
    in_refs, (gh_ref, wu_ref, wt_ref) = refs[:count], refs[count : count + 3]
    att_ref, grad_ref, out_refs = refs[count + 3], refs[count + 4], refs[count + 5 :]
    me = lax.axis_index("sensor") % count
    for partner, ref in enumerate(in_refs):
        att_ref[:, columns((me ^ partner) % count)] = ref[...]
    attended = att_ref[...]
    scale = lax.rsqrt(jnp.mean(attended * attended, -1, keepdims=True) + 1e-06)
    normed = attended * scale
    pre = dot(normed.astype(BF16), wu_ref[...])
    c = math.sqrt(2.0 / math.pi)
    square = pre * pre
    t = jnp.tanh(c * pre * (1.0 + 0.044715 * square))
    slope = 0.5 * (1.0 + t) + 0.5 * pre * (1.0 - t * t) * (c * (1.0 + 3 * 0.044715 * square))
    grad_pre = (gh_ref[...] * slope).astype(BF16)
    grad_normed = dot(grad_pre, wt_ref[...])
    grad_ref[...] = (
        grad_normed - normed * jnp.mean(grad_normed * normed, -1, keepdims=True)
    ) * scale
    send_columns([grad_ref], out_refs, me)


def grad_summary_kernel(steps, size, count, *refs):
    in_refs, (att_ref, inv_ref, f_ref) = refs[:count], refs[count : count + 3]
    num_ref, den_ref, g_ref, scratch = refs[count + 3 :]
    place_rows(scratch, in_refs, steps)
    mask = head_mask(size, LANES)
    grad_att = scratch[...]
    inverse = inv_ref[...]
    feat = f_ref[...]
    grad_num = grad_att * inverse
    grad_den = -head_sums(grad_att * att_ref[...], head_ones(mask)) * inverse
    num_ref[...] = grad_num
    den_ref[...] = grad_den
    store_summary(g_ref, *summaries(feat, grad_num, feat * grad_den, steps, size))


def query_back_kernel(steps, factor, s_ref, num_ref, den_ref, f_ref, u_ref, proj_ref, g_ref):
    size = proj_ref.shape[0]
    mask = head_mask(size, LANES)
    high = f_ref.shape[0] // steps
    out = []
    for step, (matrix, row) in enumerate(load_summary([s_ref], steps, size)):
        part = slice(step * high, (step + 1) * high)
        back = dot3(split(num_ref[part, :]), split(spread(matrix, mask)), NT)
        out.append(back + den_ref[part, :] * row)
    weighted = jnp.concatenate(out, 0) * f_ref[...]
    grad = feature_back(
        weighted, u_ref[...], [proj_ref[...]], mask, head_ones(mask)
    )
    g_ref[...] = (grad * factor).astype(BF16)


def key_back_kernel(steps, factor, parts, devices, *refs):
    g_refs, (u_ref, v_ref, f_ref, proj_ref, gq_ref) = refs[:parts], refs[parts : parts + 5]
    x_all, total_ref, keep_ref, send_ref, p_ref = refs[parts + 5 :]
    size = proj_ref.shape[0]
    mask = head_mask(size, LANES)
    high = f_ref.shape[0] // steps
    total = g_refs[0][...]
    for ref in g_refs[1:]:
        total = total + ref[...]
    total_ref[...] = total
    back, grad_v = [], []
    for step, (matrix, row) in enumerate(load_summary([total_ref], steps, size)):
        part = slice(step * high, (step + 1) * high)
        matrix = split(spread(matrix, mask))
        back.append(dot3(split(v_ref[part, :]), matrix, NT) + row)
        grad_v.append(dot3(split(f_ref[part, :]), matrix))
    weighted = jnp.concatenate(back, 0) * f_ref[...]
    grad_k = feature_back(
        weighted, u_ref[...], [proj_ref[...]], mask, head_ones(mask)
    )
    grad = jnp.concatenate([grad_k * factor, jnp.concatenate(grad_v, 0)], -1).astype(BF16)
    total = dot(x_all[...], jnp.concatenate([gq_ref[...], grad], -1))
    block = total.shape[0] // devices
    for place in range(devices):
        p_ref[place % 2, place // 2 % 2, place // 4] = total[place * block : (place + 1) * block]
    low = lax.axis_index("step") % 2
    keep_ref[...] = p_ref[low]
    send_ref[...] = p_ref[1 - low]


def core_kernel(count, own_ref, got_ref, *refs):
    high = lax.axis_index("step") // 2 % 2
    mine = lax.axis_index("sensor") // count
    per = len(refs) // 2
    for place, ref in enumerate(refs):
        part = high ^ (place // per)
        if per == 2:
            block = mine ^ (place % 2)
            ref[...] = own_ref[part, block] + got_ref[part, block]
        else:
            ref[...] = own_ref[part] + got_ref[part]


def collect_columns(target, refs):
    me = lax.axis_index("sensor") % len(refs)
    for partner, ref in enumerate(refs):
        target[:, columns((me ^ partner) % len(refs))] = ref[...]


def query_rows_kernel(steps, factor, count, *refs):
    in_refs, (f_ref, u_ref, att_ref, grad_ref) = refs[:count], refs[count : count + 4]
    proj_ref, wq_ref, out_ref, s_ref = refs[count + 4 :]
    collect_columns(s_ref, in_refs[::-1])
    size = proj_ref.shape[1]
    mask = head_mask(size, WIDE)
    ones = head_ones(mask)
    rows = f_ref.shape[0] // steps
    feat, grad_att = f_ref[...], grad_ref[...]
    normal = [s_ref[steps * size + t : steps * size + t + 1, :] for t in range(steps)]
    normal = jnp.concatenate([jnp.broadcast_to(n, (rows, n.shape[1])) for n in normal], 0)
    denom = jnp.concatenate([head_sums(w, ones) for w in pieces(feat * normal)], -1)
    inverse = 1.0 / denom
    grad_num = grad_att * inverse
    along = pieces(grad_att * att_ref[...])
    grad_den = -jnp.concatenate([head_sums(a, ones) for a in along], -1) * inverse
    back = []
    for step in range(steps):
        nums = pieces(grad_num[step * rows : (step + 1) * rows])
        matrices = pieces(s_ref[step * size : (step + 1) * size, :])
        parts = [dot3(split(n), split(spread(m, mask)), NT) for n, m in zip(nums, matrices)]
        back.append(jnp.concatenate(parts, -1))
    weighted = (jnp.concatenate(back, 0) + grad_den * normal) * feat
    grad = feature_back(weighted, u_ref[...], all_heads(proj_ref), mask, ones) * factor
    out_ref[...] = dot(grad.astype(BF16), wq_ref[...])


def rows_kernel(steps, factor, count, *refs):
    in_refs, (u_ref, v_ref, f_ref, proj_ref) = refs[:count], refs[count : count + 4]
    q_ref, wk_ref, wv_ref, out_ref, g_ref = refs[count + 4 :]
    size = proj_ref.shape[1]
    collect_columns(g_ref, in_refs[::-1])
    total = q_ref[...]
    mask = head_mask(size, WIDE)
    rows = f_ref.shape[0] // steps
    back, grad_v = [], []
    for step in range(steps):
        part = slice(step * rows, (step + 1) * rows)
        matrix = g_ref[step * size : (step + 1) * size, :]
        spreads = [split(spread(m, mask)) for m in pieces(matrix)]
        values = [split(v) for v in pieces(v_ref[part, :])]
        feats = [split(f) for f in pieces(f_ref[part, :])]
        row = g_ref[steps * size + step : steps * size + step + 1, :]
        back.append(
            jnp.concatenate([dot3(v, m, NT) for v, m in zip(values, spreads)], -1) + row
        )
        grad_v.append(jnp.concatenate([dot3(f, m) for f, m in zip(feats, spreads)], -1))
    weighted = jnp.concatenate(back, 0) * f_ref[...]
    grad_k = feature_back(weighted, u_ref[...], all_heads(proj_ref), mask, head_ones(mask))
    total = total + dot((grad_k * factor).astype(BF16), wk_ref[...])
    grad_v = jnp.concatenate(grad_v, 0).astype(BF16)
    out_ref[...] = (total + dot(grad_v, wv_ref[...])).astype(BF16)


def final_kernel(scale, parts, *refs):
    in_refs, outs = refs[:parts], refs[parts:]
    total = in_refs[0][...]
    for ref in in_refs[1:]:
        total = total + ref[...]
    cols = outs[0].shape[1]
    for place, ref in enumerate(outs):
        ref[...] = total[:, place * cols : (place + 1) * cols] * scale


def call(kernel, name, outs, args, flops=0, smem=0, hbm=0, scratch=(), limit=20):
    size = lambda a: math.prod(a.shape) * a.dtype.itemsize
    rest = len(args) - smem - hbm
    return pl.pallas_call(
        kernel,
        name=name,
        out_shape=outs,
        in_specs=[SMEM] * smem + [pl.BlockSpec(memory_space=pl.ANY)] * hbm + [VMEM] * rest,
        out_specs=jax.tree.map(lambda _: VMEM, outs),
        scratch_shapes=list(scratch),
        cost_estimate=pl.CostEstimate(
            flops=flops,
            bytes_accessed=sum(size(a) for a in list(args) + list(jax.tree.leaves(outs))),
            transcendentals=0,
        ),
        compiler_params=pltpu.CompilerParams(vmem_limit_bytes=limit * 1024 * 1024),
    )(*args)


def shape(dims, kind=F32):
    return jax.ShapeDtypeStruct(dims, kind)


def swap(a, axis, bit):
    return lax.ppermute(a, axis, [(i, i ^ bit) for i in range(lax.axis_size(axis))])


def trade(parts, axis, together=True):
    order = [len(parts) - 1, *reversed(range(1, len(parts) - 1))]
    got = [swap(parts[d], axis, d) for d in order]
    if together:
        got = lax.optimization_barrier(got)
    return [parts[0], *got[:0:-1], got[0]]


def gather(a, axis, count):
    held = {0: a}
    bit = count // 2
    while bit:
        held |= {d | bit: swap(b, axis, bit) for d, b in held.items()}
        bit //= 2
    return [held[d] for d in sorted(held)]


def gather_halves(top, low, axis):
    near_low, next_top = swap(low, axis, 2), swap(top, axis, 1)
    near_top, next_low = swap(top, axis, 2), swap(low, axis, 1)
    across_top, across_low = swap(next_top, axis, 2), swap(near_low, axis, 1)
    return (top, next_top, near_top, across_top), (low, next_low, near_low, across_low)


def far_sum(a, count):
    bit = count
    while bit * 2 < lax.axis_size("sensor"):
        a = a + swap(a, "sensor", bit)
        bit *= 2
    return a, swap(a, "sensor", bit)


def after(a, *others):
    return lax.optimization_barrier((a, others))[0]


def shards(inputs, cotangent, w_query, w_key, w_value, w_up, w_down, feature_proj, live_count):
    steps, sensors, width = inputs.shape
    heads, size, feats = feature_proj.shape
    hidden = w_up.shape[1]
    factor = size ** (-0.25)
    rows = steps * sensors
    devices = lax.axis_size("sensor")
    count = width // LANES
    quads = devices // count
    x = inputs.reshape(rows, width)
    cot = cotangent.reshape(rows, width)
    narrow = shape((rows, LANES))
    tall = shape((rows * count, LANES))
    packed = shape((steps * size + 8, LANES))
    product = 2 * rows * width * width
    kinds = lambda *arrays: [pltpu.VMEM(a.shape, a.dtype) for a in arrays]
    wide = pltpu.VMEM((rows, width), F32)

    top, low = call(
        widen_kernel,
        "widen",
        (shape((rows // 2 + 8, width)),) * 2,
        (live_count, x),
        smem=1,
    )
    tops, lows = gather_halves(top, low, "sensor")
    narrow_w = shape((width, LANES), BF16)
    own_query, own_key, own_value, proj, query_rows, feat_rows, *local_keys = call(
        functools.partial(local_kernel, steps, factor, count),
        "local_keys",
        (narrow_w,) * 3 + (shape((size, LANES)),) + (shape((rows, width)),) * 5,
        (live_count, x, w_query, w_key, w_value, feature_proj),
        flops=3 * product,
        smem=1,
    )
    x_all, key, value, feat_key, summary = call(
        functools.partial(key_kernel, steps, factor, count),
        "keys",
        (shape((rows * count, width), BF16),) + (tall,) * 3 + (packed,),
        (*tops, *lows, own_key, own_value, proj),
        flops=3 * product,
    )
    turned = (x_all, w_query, w_key, w_value, w_up)
    x_turned, wq_turned, wk_turned, wv_turned, wu_turned = call(
        transpose_kernel, "transposes", tuple(shape(a.shape[::-1], BF16) for a in turned), turned
    )
    query, feat_query, grad_hidden = call(
        functools.partial(query_kernel, steps, factor, count),
        "queries",
        (tall, tall, shape((rows, hidden))),
        (live_count, x_all, cot, own_query, w_down, proj),
        flops=2 * product,
        smem=1,
    )
    summary = far_sum(summary, count)
    attended, inverse, summary, *local_att = call(
        functools.partial(attend_kernel, steps, size, len(summary)),
        "attend",
        (tall, tall, packed) + (narrow,) * count,
        (*summary, feat_query),
        flops=product,
    )
    local_att, local_grad_att, *local_grad = call(
        functools.partial(forward_kernel, count),
        "feed_forward",
        (shape((rows, width)),) * 2 + (narrow,) * count,
        (*trade(local_att, "sensor"), grad_hidden, w_up, wu_turned),
        flops=product,
    )
    grad_num, grad_den, grad_summary = call(
        functools.partial(grad_summary_kernel, steps, size, count),
        "grad_summary",
        (tall, tall, packed),
        (*trade(local_grad, "sensor"), attended, inverse, feat_query),
        flops=product,
        scratch=kinds(tall),
    )
    query_part = call(
        functools.partial(query_rows_kernel, steps, factor, count),
        "query_rows",
        shape((rows, width)),
        (
            *gather(summary, "sensor", count)[::-1],
            feat_rows,
            query_rows,
            local_att,
            local_grad_att,
            feature_proj,
            wq_turned,
        ),
        flops=3 * product,
        scratch=[pltpu.VMEM((packed.shape[0], width), F32)],
    )
    grad_summary = far_sum(grad_summary, count)
    grad_q = call(
        functools.partial(query_back_kernel, steps, factor),
        "query_back",
        shape(tall.shape, BF16),
        (summary, grad_num, grad_den, feat_query, query, proj),
        flops=product,
    )
    tile = (width // devices, 3 * LANES)
    half = shape((2, quads, *tile))
    grad_summary, own_half, send_half = call(
        functools.partial(key_back_kernel, steps, factor, len(grad_summary), devices),
        "key_back",
        (packed, half, half),
        (*grad_summary, key, value, feat_key, proj, after(grad_q, query_part), x_turned),
        flops=4 * product,
        scratch=[pltpu.VMEM((2, *half.shape), F32)],
    )
    def turn(a, bit, flip=0):
        pairs = []
        for k in range(quads):
            for q in range(count):
                for j in range(count):
                    target = (k ^ bit) * count + (j ^ flip)
                    pairs.append(((k * count + q) * count + j, target * count + q))
        return lax.ppermute(a, ("sensor", "step"), pairs)

    got_half = swap(send_half, "step", 1)
    if quads == 2:
        kept, away, send_kept, send_away = call(
            functools.partial(core_kernel, count),
            "core_sums",
            (shape(tile),) * 4,
            (own_half, got_half),
        )
        parts = (turn(away, 1), turn(send_away, 1, 2), turn(send_kept, 0, 2), turn(kept, 0))
    else:
        kept, sent = call(
            functools.partial(core_kernel, count),
            "core_sums",
            (shape((quads, *tile)),) * 2,
            (own_half, got_half),
        )
        groups = [[q + count * k for k in range(quads)] for q in range(count)]
        blocks = lax.all_to_all(
            kept + swap(sent, "step", 2), "sensor", 0, 0, tiled=True, axis_index_groups=groups
        )
        parts = (turn(blocks.sum(0), 0),)
    messages = trade([grad_summary] * count, "sensor", False)
    scale = 1.0 / math.sqrt(rows * lax.axis_size("step") * devices)
    out = shape((width // devices, LANES))
    grad_in = call(
        functools.partial(rows_kernel, steps, factor, count),
        "input_rows",
        shape((rows, width), BF16),
        (*messages[::-1], *local_keys, feature_proj, query_part, wk_turned, wv_turned),
        flops=30 * product,
        scratch=[pltpu.VMEM((packed.shape[0], width), F32)],
    )
    grads = call(
        functools.partial(final_kernel, scale, len(parts)),
        "weight_sums",
        (out,) * 3,
        (after(parts[0], grad_in), *parts[1:]),
    )
    return (grad_in.reshape(inputs.shape), *grads)


def solution(mesh):
    return jax.shard_map(
        shards,
        mesh=mesh,
        in_specs=(P("step", "sensor", None),) * 2 + (P(),) * 6 + (P("sensor"),),
        out_specs=(P("step", "sensor", None),) + (P("sensor", "step"),) * 3,
        check_vma=False,
    )
```

```python
import functools
import math

import jax
import jax.numpy as jnp
from jax import lax
from jax.experimental import pallas as pl
from jax.experimental.pallas import tpu as pltpu
from jax.sharding import PartitionSpec as P

F32 = jnp.float32
BF16 = jnp.bfloat16
NN = (((1,), (0,)), ((), ()))
NT = (((1,), (1,)), ((), ()))
TN = (((0,), (0,)), ((), ()))
VMEM = pl.BlockSpec(memory_space=pltpu.VMEM)
SMEM = pl.BlockSpec(memory_space=pltpu.SMEM)
LANES = 128
WIDE = 256


def dot(a, b, dims=NN):
    return lax.dot_general(a, b, dims, preferred_element_type=F32)


def split(x):
    high = x.astype(BF16)
    return high, (x - high.astype(F32)).astype(BF16)


def dot3(a, b, dims=NN):
    if a[0].shape[1] == LANES:
        axis = 1 if dims == NN else 0
        parts = [jnp.concatenate([b[0], b[1]], axis), jnp.concatenate([b[0], 0 * b[1]], axis)]
        out = dot(jnp.concatenate(a, 1), jnp.concatenate(parts, 1 - axis), dims)
        return out[:, :LANES] + out[:, LANES:]
    rows = a[0].shape[0]
    out = dot(jnp.concatenate(a, 0), b[0], dims)
    return out[:rows] + (out[rows:] + dot(a[0], b[1], dims))


def dot2(a, b, dims=NN):
    rows = a[0].shape[0]
    out = dot(jnp.concatenate(a, 0), b, dims)
    return out[:rows] + out[rows:]


def head_mask(size, width):
    rows = lax.broadcasted_iota(jnp.int32, (width, width), 0) // size
    cols = lax.broadcasted_iota(jnp.int32, (width, width), 1) // size
    return rows == cols


def head_ones(mask):
    return jnp.where(mask, 1.0, 0.0).astype(BF16)


def spread(x, mask):
    return jnp.where(mask, jnp.concatenate([x] * (x.shape[1] // x.shape[0]), 0), 0.0)


def gather_diagonal(x, size):
    head = lax.broadcasted_iota(jnp.int32, (size, x.shape[1]), 1) // size
    out = x[:size]
    for g in range(1, x.shape[1] // size):
        out = jnp.where(head == g, x[g * size : (g + 1) * size], out)
    return out


def head_sums(x, ones):
    high, low = split(x)
    if x.shape[1] == LANES:
        return dot(jnp.concatenate([high, low], 1), jnp.concatenate([ones, ones], 0))
    return dot2((high, low), ones)


def pieces(x, width=WIDE):
    return [x[:, h : h + width] for h in range(0, x.shape[1], width)]


def projection(proj_ref, heads=None, width=WIDE):
    heads = range(proj_ref.shape[0]) if heads is None else heads
    blocks = [proj_ref[h] for h in heads]
    per = width // proj_ref.shape[2]
    return [jnp.concatenate(blocks[g : g + per], -1) for g in range(0, len(blocks), per)]


def feature_map(scaled, proj, mask, ones, feats):
    out = []
    for u, p in zip(pieces(scaled, mask.shape[0]), proj):
        projected = dot3(split(u), split(spread(p, mask)))
        out.append(jnp.exp(projected - 0.5 * head_sums(u * u, ones)) * feats ** (-0.5))
    return jnp.concatenate(out, -1)


def feature_back(weighted, scaled, proj, mask, ones):
    out = []
    width = mask.shape[0]
    for w, u, p in zip(pieces(weighted, width), pieces(scaled, width), proj):
        back = dot3(split(w), split(spread(p, mask)), NT)
        out.append(back - u * head_sums(w, ones))
    return jnp.concatenate(out, -1)


def store_summary(out_ref, matrices, sums):
    size = matrices[0].shape[0]
    base = size * len(matrices)
    out_ref[base:, :] = jnp.zeros((out_ref.shape[0] - base, LANES), F32)
    for step, (matrix, row) in enumerate(zip(matrices, sums)):
        out_ref[step * size : (step + 1) * size, :] = matrix
        out_ref[base + step : base + step + 1, :] = row


def load_summary(refs, steps, size):
    total = refs[0][...]
    for ref in refs[1:]:
        total = total + ref[...]
    base = steps * size
    return [
        (total[step * size : (step + 1) * size], total[base + step : base + step + 1])
        for step in range(steps)
    ]


def outer_sums(a, b, size):
    out = dot(jnp.concatenate(split(a), 1), jnp.concatenate(split(b), 1), TN)
    whole = out[:LANES, :LANES] + (out[:LANES, LANES:] + out[LANES:, :LANES])
    return gather_diagonal(whole, size)


def summaries(a, b, weighted, steps, size):
    high = a.shape[0] // steps
    parts = [slice(step * high, (step + 1) * high) for step in range(steps)]
    matrices = [outer_sums(a[p], b[p], size) for p in parts]
    return matrices, [jnp.sum(weighted[p], 0, keepdims=True) for p in parts]


def columns(group):
    return pl.ds(pl.multiple_of(group * LANES, LANES), LANES)


def send_columns(sources, refs, me):
    for partner, ref in enumerate(refs):
        own = columns((me ^ partner) % len(refs))
        for place, source in enumerate(sources):
            rows = source.shape[0]
            ref[:rows, place * LANES : (place + 1) * LANES] = source[:, own]


def place_rows(target, refs, steps, column=0):
    rows = target.shape[0] // (steps * len(refs))
    lanes = slice(column * LANES, column * LANES + target.shape[1])
    for partner, ref in enumerate(refs):
        for step in range(steps):
            start = (step * len(refs) + partner) * rows
            target[start : start + rows, :] = ref[step * rows : (step + 1) * rows, lanes].astype(
                target.dtype
            )


def take_rows(values, partner, count, steps):
    rows = values.shape[0] // (steps * count)
    starts = [(step * count + partner) * rows for step in range(steps)]
    return jnp.concatenate([values[s : s + rows] for s in starts], 0)


def widen_kernel(live_ref, x_ref, top_ref, low_ref):
    half = x_ref.shape[0] // 2
    for ref, base in ((top_ref, 0), (low_ref, half)):
        ref[:half, :] = x_ref[base : base + half].astype(F32)
        ref[half:, :] = jnp.full((ref.shape[0] - half, ref.shape[1]), live_ref[0]).astype(F32)


def own_columns(count):
    return columns(lax.axis_index("sensor") % count)


def own_heads(proj_ref, count):
    per = proj_ref.shape[0] // count
    start = (lax.axis_index("sensor") % count) * per
    return jnp.concatenate([proj_ref[start + h] for h in range(per)], -1)


def all_heads(proj_ref):
    per = WIDE // proj_ref.shape[2]
    return [
        jnp.concatenate([proj_ref[g + h] for h in range(per)], -1)
        for g in range(0, proj_ref.shape[0], per)
    ]


def local_kernel(steps, factor, count, live_ref, x_ref, wq_ref, wk_ref, wv_ref, proj_ref, *refs):
    oq_ref, ok_ref, ov_ref, op_ref, uq_ref, fq_ref, u_ref, v_ref, f_ref = refs
    own = own_columns(count)
    oq_ref[...] = wq_ref[:, own]
    ok_ref[...] = wk_ref[:, own]
    ov_ref[...] = wv_ref[:, own]
    op_ref[...] = own_heads(proj_ref, count)
    mask = head_mask(proj_ref.shape[1], WIDE)
    x = x_ref[...]
    proj = all_heads(proj_ref)
    scaled = dot(x, wq_ref[...]) * factor
    uq_ref[...] = scaled
    fq_ref[...] = feature_map(scaled, proj, mask, head_ones(mask), proj_ref.shape[2])
    scaled = dot(x, wk_ref[...]) * factor
    u_ref[...] = scaled
    v_ref[...] = dot(x, wv_ref[...])
    feat = feature_map(scaled, proj, mask, head_ones(mask), proj_ref.shape[2])
    place = lax.broadcasted_iota(jnp.int32, feat.shape, 0) % (feat.shape[0] // steps)
    f_ref[...] = jnp.where(place < live_ref[0], feat, 0.0)


def key_kernel(steps, factor, count, *refs):
    tops, lows = refs[:count], refs[count : 2 * count]
    wk_ref, wv_ref, proj_ref, x_ref, u_ref, v_ref, f_ref, s_ref = refs[2 * count :]
    size = proj_ref.shape[0]
    mask = head_mask(size, LANES)
    rows = x_ref.shape[0] // (steps * count)
    half = steps * rows // 2
    piece = math.gcd(half, rows)
    for partner in range(count):
        for ref, base in ((tops[partner], 0), (lows[partner], half)):
            for row in range(0, half, piece):
                step, inner = divmod(base + row, rows)
                start = (step * count + partner) * rows + inner
                x_ref[start : start + piece, :] = ref[row : row + piece, :].astype(BF16)
    x = x_ref[...]
    scaled = dot(x, wk_ref[...]) * factor
    values = dot(x, wv_ref[...])
    u_ref[...] = scaled
    v_ref[...] = values
    feat = feature_map(scaled, [proj_ref[...]], mask, head_ones(mask), size)
    place = lax.broadcasted_iota(jnp.int32, (rows, LANES), 0).astype(F32)
    keep = jnp.concatenate([place < ref[half : half + 1, :LANES] for ref in tops] * steps, 0)
    feat = jnp.where(keep, feat, 0.0)
    f_ref[...] = feat
    store_summary(s_ref, *summaries(feat, values, feat, steps, size))


def transpose_kernel(*refs):
    half = len(refs) // 2
    for source, target in zip(refs[:half], refs[half:]):
        target[...] = source[...].T


def query_kernel(steps, factor, count, live_ref, x_ref, cot_ref, wq_ref, wd_ref, proj_ref, u_ref, f_ref, gh_ref):
    size = proj_ref.shape[0]
    mask = head_mask(size, LANES)
    scaled = dot(x_ref[...], wq_ref[...]) * factor
    u_ref[...] = scaled
    f_ref[...] = feature_map(
        scaled, [proj_ref[...]], mask, head_ones(mask), size
    )
    hidden = dot(cot_ref[...], wd_ref[...], NT)
    place = lax.broadcasted_iota(jnp.int32, hidden.shape, 0) % (hidden.shape[0] // steps)
    gh_ref[...] = jnp.where(place < live_ref[0], hidden, 0.0)


def attend_kernel(steps, size, parts, *refs):
    s_refs, (f_ref, att_ref, inv_ref, s_ref) = refs[:parts], refs[parts : parts + 4]
    out_refs = refs[parts + 4 :]
    total = s_refs[0][...]
    for ref in s_refs[1:]:
        total = total + ref[...]
    s_ref[...] = total
    mask = head_mask(size, LANES)
    feat = f_ref[...]
    high = feat.shape[0] // steps
    numer, weighted = [], []
    for step, (matrix, row) in enumerate(load_summary([s_ref], steps, size)):
        part = feat[step * high : (step + 1) * high]
        numer.append(dot3(split(part), split(spread(matrix, mask))))
        weighted.append(part * row)
    inverse = 1.0 / head_sums(jnp.concatenate(weighted, 0), head_ones(mask))
    attended = jnp.concatenate(numer, 0) * inverse
    att_ref[...] = attended
    inv_ref[...] = inverse
    for partner, ref in enumerate(out_refs):
        ref[...] = take_rows(attended, partner, len(out_refs), steps)


def forward_kernel(count, *refs):
    in_refs, (gh_ref, wu_ref, wt_ref) = refs[:count], refs[count : count + 3]
    att_ref, grad_ref, out_refs = refs[count + 3], refs[count + 4], refs[count + 5 :]
    me = lax.axis_index("sensor") % count
    for partner, ref in enumerate(in_refs):
        att_ref[:, columns((me ^ partner) % count)] = ref[...]
    attended = att_ref[...]
    scale = lax.rsqrt(jnp.mean(attended * attended, -1, keepdims=True) + 1e-06)
    normed = attended * scale
    pre = dot(normed.astype(BF16), wu_ref[...])
    c = math.sqrt(2.0 / math.pi)
    square = pre * pre
    t = jnp.tanh(c * pre * (1.0 + 0.044715 * square))
    slope = 0.5 * (1.0 + t) + 0.5 * pre * (1.0 - t * t) * (c * (1.0 + 3 * 0.044715 * square))
    grad_pre = (gh_ref[...] * slope).astype(BF16)
    grad_normed = dot(grad_pre, wt_ref[...])
    grad_ref[...] = (
        grad_normed - normed * jnp.mean(grad_normed * normed, -1, keepdims=True)
    ) * scale
    send_columns([grad_ref], out_refs, me)


def grad_summary_kernel(steps, size, count, *refs):
    in_refs, (att_ref, inv_ref, f_ref) = refs[:count], refs[count : count + 3]
    num_ref, den_ref, g_ref, scratch = refs[count + 3 :]
    place_rows(scratch, in_refs, steps)
    mask = head_mask(size, LANES)
    grad_att = scratch[...]
    inverse = inv_ref[...]
    feat = f_ref[...]
    grad_num = grad_att * inverse
    grad_den = -head_sums(grad_att * att_ref[...], head_ones(mask)) * inverse
    num_ref[...] = grad_num
    den_ref[...] = grad_den
    store_summary(g_ref, *summaries(feat, grad_num, feat * grad_den, steps, size))


def query_back_kernel(steps, factor, s_ref, num_ref, den_ref, f_ref, u_ref, proj_ref, g_ref):
    size = proj_ref.shape[0]
    mask = head_mask(size, LANES)
    high = f_ref.shape[0] // steps
    out = []
    for step, (matrix, row) in enumerate(load_summary([s_ref], steps, size)):
        part = slice(step * high, (step + 1) * high)
        back = dot3(split(num_ref[part, :]), split(spread(matrix, mask)), NT)
        out.append(back + den_ref[part, :] * row)
    weighted = jnp.concatenate(out, 0) * f_ref[...]
    grad = feature_back(
        weighted, u_ref[...], [proj_ref[...]], mask, head_ones(mask)
    )
    g_ref[...] = (grad * factor).astype(BF16)


def key_back_kernel(steps, factor, parts, devices, *refs):
    g_refs, (u_ref, v_ref, f_ref, proj_ref, gq_ref) = refs[:parts], refs[parts : parts + 5]
    x_all, total_ref, keep_ref, send_ref, p_ref = refs[parts + 5 :]
    size = proj_ref.shape[0]
    mask = head_mask(size, LANES)
    high = f_ref.shape[0] // steps
    total = g_refs[0][...]
    for ref in g_refs[1:]:
        total = total + ref[...]
    total_ref[...] = total
    back, grad_v = [], []
    for step, (matrix, row) in enumerate(load_summary([total_ref], steps, size)):
        part = slice(step * high, (step + 1) * high)
        matrix = split(spread(matrix, mask))
        back.append(dot3(split(v_ref[part, :]), matrix, NT) + row)
        grad_v.append(dot3(split(f_ref[part, :]), matrix))
    weighted = jnp.concatenate(back, 0) * f_ref[...]
    grad_k = feature_back(
        weighted, u_ref[...], [proj_ref[...]], mask, head_ones(mask)
    )
    grad = jnp.concatenate([grad_k * factor, jnp.concatenate(grad_v, 0)], -1).astype(BF16)
    grad = jnp.concatenate([gq_ref[...], grad], -1)
    block = x_all.shape[0] // devices
    low = lax.axis_index("step") % 2
    if block % 16 == 0:
        for ref, part in ((send_ref, 1 - low), (keep_ref, low)):
            places = [(high, quad) for high in range(2) for quad in range(devices // 4)]
            starts = [(4 * quad + 2 * high + part) * block for high, quad in places]
            rows = [x_all[pl.ds(pl.multiple_of(s, block), block), :] for s in starts]
            total = dot(jnp.concatenate(rows, 0), grad)
            for place, (high, quad) in enumerate(places):
                ref[high, quad] = total[place * block : (place + 1) * block]
        return
    total = dot(x_all[...], grad)
    for place in range(devices):
        p_ref[place % 2, place // 2 % 2, place // 4] = total[place * block : (place + 1) * block]
    low = lax.axis_index("step") % 2
    keep_ref[...] = p_ref[low]
    send_ref[...] = p_ref[1 - low]


def core_kernel(count, own_ref, got_ref, *refs):
    high = lax.axis_index("step") // 2 % 2
    mine = lax.axis_index("sensor") // count
    per = len(refs) // 2
    for place, ref in enumerate(refs):
        part = high ^ (place // per)
        if per == 2:
            block = mine ^ (place % 2)
            ref[...] = own_ref[part, block] + got_ref[part, block]
        else:
            ref[...] = own_ref[part] + got_ref[part]


def collect_columns(target, refs):
    me = lax.axis_index("sensor") % len(refs)
    for partner, ref in enumerate(refs):
        target[:, columns((me ^ partner) % len(refs))] = ref[...]


def query_rows_kernel(steps, factor, count, *refs):
    in_refs, (f_ref, u_ref, att_ref, grad_ref) = refs[:count], refs[count : count + 4]
    proj_ref, wq_ref, out_ref, s_ref = refs[count + 4 :]
    collect_columns(s_ref, in_refs[::-1])
    size = proj_ref.shape[1]
    mask = head_mask(size, WIDE)
    ones = head_ones(mask)
    rows = f_ref.shape[0] // steps
    feat, grad_att = f_ref[...], grad_ref[...]
    normal = [s_ref[steps * size + t : steps * size + t + 1, :] for t in range(steps)]
    normal = jnp.concatenate([jnp.broadcast_to(n, (rows, n.shape[1])) for n in normal], 0)
    denom = jnp.concatenate([head_sums(w, ones) for w in pieces(feat * normal)], -1)
    inverse = 1.0 / denom
    grad_num = grad_att * inverse
    along = pieces(grad_att * att_ref[...])
    grad_den = -jnp.concatenate([head_sums(a, ones) for a in along], -1) * inverse
    back = []
    for step in range(steps):
        nums = pieces(grad_num[step * rows : (step + 1) * rows])
        matrices = pieces(s_ref[step * size : (step + 1) * size, :])
        parts = [dot3(split(n), split(spread(m, mask)), NT) for n, m in zip(nums, matrices)]
        back.append(jnp.concatenate(parts, -1))
    weighted = (jnp.concatenate(back, 0) + grad_den * normal) * feat
    grad = feature_back(weighted, u_ref[...], all_heads(proj_ref), mask, ones) * factor
    out_ref[...] = dot(grad.astype(BF16), wq_ref[...])


def rows_kernel(steps, factor, count, *refs):
    in_refs, (u_ref, v_ref, f_ref, proj_ref) = refs[:count], refs[count : count + 4]
    q_ref, wk_ref, wv_ref, out_ref, g_ref = refs[count + 4 :]
    size = proj_ref.shape[1]
    collect_columns(g_ref, in_refs)
    total = q_ref[...]
    mask = head_mask(size, WIDE)
    rows = f_ref.shape[0] // steps
    back, grad_v = [], []
    for step in range(steps):
        part = slice(step * rows, (step + 1) * rows)
        matrix = g_ref[step * size : (step + 1) * size, :]
        spreads = [split(spread(m, mask)) for m in pieces(matrix)]
        values = [split(v) for v in pieces(v_ref[part, :])]
        feats = [split(f) for f in pieces(f_ref[part, :])]
        row = g_ref[steps * size + step : steps * size + step + 1, :]
        back.append(
            jnp.concatenate([dot3(v, m, NT) for v, m in zip(values, spreads)], -1) + row
        )
        grad_v.append(jnp.concatenate([dot3(f, m) for f, m in zip(feats, spreads)], -1))
    weighted = jnp.concatenate(back, 0) * f_ref[...]
    grad_k = feature_back(weighted, u_ref[...], all_heads(proj_ref), mask, head_ones(mask))
    total = total + dot((grad_k * factor).astype(BF16), wk_ref[...])
    grad_v = jnp.concatenate(grad_v, 0).astype(BF16)
    out_ref[...] = (total + dot(grad_v, wv_ref[...])).astype(BF16)


def final_kernel(scale, parts, *refs):
    in_refs, outs = refs[:parts], refs[parts:]
    total = in_refs[0][...]
    for ref in in_refs[1:]:
        total = total + ref[...]
    cols = outs[0].shape[1]
    for place, ref in enumerate(outs):
        ref[...] = total[:, place * cols : (place + 1) * cols] * scale


def call(kernel, name, outs, args, flops=0, smem=0, hbm=0, scratch=(), limit=20):
    size = lambda a: math.prod(a.shape) * a.dtype.itemsize
    rest = len(args) - smem - hbm
    return pl.pallas_call(
        kernel,
        name=name,
        out_shape=outs,
        in_specs=[SMEM] * smem + [pl.BlockSpec(memory_space=pl.ANY)] * hbm + [VMEM] * rest,
        out_specs=jax.tree.map(lambda _: VMEM, outs),
        scratch_shapes=list(scratch),
        cost_estimate=pl.CostEstimate(
            flops=flops,
            bytes_accessed=sum(size(a) for a in list(args) + list(jax.tree.leaves(outs))),
            transcendentals=0,
        ),
        compiler_params=pltpu.CompilerParams(vmem_limit_bytes=limit * 1024 * 1024),
    )(*args)


def shape(dims, kind=F32):
    return jax.ShapeDtypeStruct(dims, kind)


def swap(a, axis, bit):
    return lax.ppermute(a, axis, [(i, i ^ bit) for i in range(lax.axis_size(axis))])


def trade(parts, axis, together=True):
    order = [len(parts) - 1, *reversed(range(1, len(parts) - 1))]
    got = [swap(parts[d], axis, d) for d in order]
    if together:
        got = lax.optimization_barrier(got)
    return [parts[0], *got[:0:-1], got[0]]


def gather(a, axis, count):
    held = {0: a}
    bit = count // 2
    while bit:
        held |= {d | bit: swap(b, axis, bit) for d, b in held.items()}
        bit //= 2
    return [held[d] for d in sorted(held)]


def gather_halves(top, low, axis):
    near_low, next_top = swap(low, axis, 2), swap(top, axis, 1)
    near_top, next_low = swap(top, axis, 2), swap(low, axis, 1)
    across_top, across_low = swap(next_top, axis, 2), swap(near_low, axis, 1)
    return (top, next_top, near_top, across_top), (low, next_low, near_low, across_low)


def far_sum(a, count):
    bit = count
    while bit * 2 < lax.axis_size("sensor"):
        a = a + swap(a, "sensor", bit)
        bit *= 2
    return a, swap(a, "sensor", bit)


def after(a, *others):
    return lax.optimization_barrier((a, others))[0]


def shards(inputs, cotangent, w_query, w_key, w_value, w_up, w_down, feature_proj, live_count):
    steps, sensors, width = inputs.shape
    heads, size, feats = feature_proj.shape
    hidden = w_up.shape[1]
    factor = size ** (-0.25)
    rows = steps * sensors
    devices = lax.axis_size("sensor")
    count = width // LANES
    quads = devices // count
    x = inputs.reshape(rows, width)
    cot = cotangent.reshape(rows, width)
    narrow = shape((rows, LANES))
    tall = shape((rows * count, LANES))
    packed = shape((steps * size + 8, LANES))
    product = 2 * rows * width * width
    kinds = lambda *arrays: [pltpu.VMEM(a.shape, a.dtype) for a in arrays]
    wide = pltpu.VMEM((rows, width), F32)

    top, low = call(
        widen_kernel,
        "widen",
        (shape((rows // 2 + 8, width)),) * 2,
        (live_count, x),
        smem=1,
    )
    tops, lows = gather_halves(top, low, "sensor")
    narrow_w = shape((width, LANES), BF16)
    own_query, own_key, own_value, proj, query_rows, feat_rows, *local_keys = call(
        functools.partial(local_kernel, steps, factor, count),
        "local_keys",
        (narrow_w,) * 3 + (shape((size, LANES)),) + (shape((rows, width)),) * 5,
        (live_count, x, w_query, w_key, w_value, feature_proj),
        flops=3 * product,
        smem=1,
    )
    x_all, key, value, feat_key, summary = call(
        functools.partial(key_kernel, steps, factor, count),
        "keys",
        (shape((rows * count, width), BF16),) + (tall,) * 3 + (packed,),
        (*tops, *lows, own_key, own_value, proj),
        flops=3 * product,
    )
    turned = (x_all, w_query, w_key, w_value, w_up)
    x_turned, wq_turned, wk_turned, wv_turned, wu_turned = call(
        transpose_kernel, "transposes", tuple(shape(a.shape[::-1], BF16) for a in turned), turned
    )
    query, feat_query, grad_hidden = call(
        functools.partial(query_kernel, steps, factor, count),
        "queries",
        (tall, tall, shape((rows, hidden))),
        (live_count, x_all, cot, own_query, w_down, proj),
        flops=2 * product,
        smem=1,
    )
    summary = far_sum(summary, count)
    attended, inverse, summary, *local_att = call(
        functools.partial(attend_kernel, steps, size, len(summary)),
        "attend",
        (tall, tall, packed) + (narrow,) * count,
        (*summary, feat_query),
        flops=product,
    )
    local_att, local_grad_att, *local_grad = call(
        functools.partial(forward_kernel, count),
        "feed_forward",
        (shape((rows, width)),) * 2 + (narrow,) * count,
        (*trade(local_att, "sensor"), grad_hidden, w_up, wu_turned),
        flops=product,
    )
    grad_num, grad_den, grad_summary = call(
        functools.partial(grad_summary_kernel, steps, size, count),
        "grad_summary",
        (tall, tall, packed),
        (*trade(local_grad, "sensor"), attended, inverse, feat_query),
        flops=product,
        scratch=kinds(tall),
    )
    query_part = call(
        functools.partial(query_rows_kernel, steps, factor, count),
        "query_rows",
        shape((rows, width)),
        (
            *gather(summary, "sensor", count)[::-1],
            feat_rows,
            query_rows,
            local_att,
            local_grad_att,
            feature_proj,
            wq_turned,
        ),
        flops=3 * product,
        scratch=[pltpu.VMEM((packed.shape[0], width), F32)],
    )
    grad_summary = far_sum(grad_summary, count)
    grad_q = call(
        functools.partial(query_back_kernel, steps, factor),
        "query_back",
        shape(tall.shape, BF16),
        (summary, grad_num, grad_den, feat_query, query, proj),
        flops=product,
    )
    tile = (width // devices, 3 * LANES)
    half = shape((2, quads, *tile))
    grad_summary, own_half, send_half = call(
        functools.partial(key_back_kernel, steps, factor, len(grad_summary), devices),
        "key_back",
        (packed, half, half),
        (*grad_summary, key, value, feat_key, proj, after(grad_q, query_part), x_turned),
        flops=4 * product,
        scratch=[pltpu.VMEM((2, *half.shape), F32)],
    )
    def turn(a, bit, flip=0):
        pairs = []
        for k in range(quads):
            for q in range(count):
                for j in range(count):
                    target = (k ^ bit) * count + (j ^ flip)
                    pairs.append(((k * count + q) * count + j, target * count + q))
        return lax.ppermute(a, ("sensor", "step"), pairs)

    got_half = swap(send_half, "step", 1)
    if quads == 2:
        kept, away, send_kept, send_away = call(
            functools.partial(core_kernel, count),
            "core_sums",
            (shape(tile),) * 4,
            (own_half, got_half),
        )
        parts = (turn(away, 1), turn(send_away, 1, 2), turn(send_kept, 0, 2), turn(kept, 0))
    else:
        kept, sent = call(
            functools.partial(core_kernel, count),
            "core_sums",
            (shape((quads, *tile)),) * 2,
            (own_half, got_half),
        )
        groups = [[q + count * k for k in range(quads)] for q in range(count)]
        blocks = lax.all_to_all(
            kept + swap(sent, "step", 2), "sensor", 0, 0, tiled=True, axis_index_groups=groups
        )
        parts = (turn(blocks.sum(0), 0),)
    messages = trade([grad_summary] * count, "sensor", False)
    scale = 1.0 / math.sqrt(rows * lax.axis_size("step") * devices)
    out = shape((width // devices, LANES))
    grad_in = call(
        functools.partial(rows_kernel, steps, factor, count),
        "input_rows",
        shape((rows, width), BF16),
        (*messages, *local_keys, feature_proj, query_part, wk_turned, wv_turned),
        flops=30 * product,
        scratch=[pltpu.VMEM((packed.shape[0], width), F32)],
    )
    grads = call(
        functools.partial(final_kernel, scale, len(parts)),
        "weight_sums",
        (out,) * 3,
        (after(parts[0], grad_in), *parts[1:]),
    )
    return (grad_in.reshape(inputs.shape), *grads)


def solution(mesh):
    return jax.shard_map(
        shards,
        mesh=mesh,
        in_specs=(P("step", "sensor", None),) * 2 + (P(),) * 6 + (P("sensor"),),
        out_specs=(P("step", "sensor", None),) + (P("sensor", "step"),) * 3,
        check_vma=False,
    )
```
